32 devices in a mesh: dp: 16 (over z, y, x), mp: 2 (over core).
Axes of the slice: x: 2, y: 2, z: 4, core: 2. Of those that a mesh axis runs over, the one named last changes fastest.
Arguments:
- maps_in: bfloat16 [128, 256, 256], P('dp', None, 'mp'), may hold values from -6 to 6
- timesteps: int32 [128], P('dp'), may hold values from 0 to 999
- temb_table: float32 [1000, 512], replicated, may hold values from -6 to 6
- norm_gain: float32 [3, 256], P(None, 'mp'), may hold values from 0.25 to 1.75
- norm_bias: float32 [3, 256], P(None, 'mp'), may hold values from -2 to 2
- conv1_weight: bfloat16 [3, 3, 256, 256], P(None, None, None, 'mp'), may hold values from -0.125 to 0.125
- conv_bias: float32 [2, 256], P(None, 'mp'), may hold values from -2 to 2
- temb_weight: bfloat16 [512, 256], P(None, 'mp'), may hold values from -0.25 to 0.25
- temb_bias: float32 [256], P('mp'), may hold values from -2 to 2
- conv2_weight: bfloat16 [3, 3, 256, 256], P(None, None, 'mp'), may hold values from -0.125 to 0.125
- qkv_weight: bfloat16 [256, 3, 256], P(None, None, 'mp'), may hold values from -0.5 to 0.5
- qkv_bias: float32 [2, 256], P(None, 'mp'), may hold values from -2 to 2
- out_weight: bfloat16 [256, 256], P('mp'), may hold values from -3 to 3
- out_bias: float32 [256], P('mp'), may hold values from -2 to 2
- out_grad: bfloat16 [128, 256, 256], P('dp', None, 'mp'), may hold values from -6 to 6
Outputs:
- maps_out: bfloat16 [128, 256, 256], P('dp', None, 'mp')
- maps_grad: float32 [128, 256, 256], P('dp', None, 'mp')
- table_grad: float32 [1000, 512], replicated
- norm_gain_grad: float32 [3, 256], P(None, 'mp')
- norm_bias_grad: float32 [3, 256], P(None, 'mp')
- conv1_grad: float32 [3, 3, 256, 256], P(None, None, None, 'mp')
- conv_bias_grad: float32 [2, 256], P(None, 'mp')
- temb_weight_grad: float32 [512, 256], P(None, 'mp')
- temb_bias_grad: float32 [256], P('mp')
- conv2_grad: float32 [3, 3, 256, 256], P(None, None, 'mp')
- qkv_grad: float32 [256, 3, 256], P(None, None, 'mp')
- qkv_bias_grad: float32 [2, 256], P(None, 'mp')
- out_weight_grad: float32 [256, 256], P('mp')
- out_bias_grad: float32 [256], P('mp')
The draws below stay inside these ranges and needn't reach their ends.
All inputs are finite; a program needn't handle non-finite values.
Results may differ from the reference program's by a relative error of at most 0.0185.
Values may be sent and summed in bfloat16 or wider, within the bound.
No kernel may reach another device: no remote copies, remote signals or barrier semaphores. Data moves between devices by JAX's collectives and lax.ppermute only.
A program may use at most 128 MiB of HBM per device.

```python
import math
import jax
import jax.numpy as jnp
from jax import lax

C = 256
TEMB = 512
GROUPS = 32
STEPS = 1000
SIDE = 16
PIX = 256
MAPS = 128


def place_ends(array, rng, smallest, largest):
    dims = array.shape
    index_at = [jax.random.randint(jax.random.fold_in(rng, axis), (), 0, dims[axis]) for axis in range(len(dims))]
    array = array.at[tuple(index_at)].set(smallest)
    longest = dims.index(max(dims))
    index_at[longest] = (index_at[longest] + 1) % dims[longest]
    return array.at[tuple(index_at)].set(largest)


def block_levels(own_key, dims, shards, low, top_value):
    def one(axis_at, shards_of):
        draws = jax.random.uniform(jax.random.fold_in(jax.random.fold_in(own_key, 6), axis_at), (shards_of,), jnp.float32, low / len(shards), top_value / len(shards))
        return jnp.repeat(jnp.exp(draws), dims[axis_at] // shards_of).reshape((-1,) + (1,) * (len(dims) - axis_at - 1))

    level = one(*shards[0])
    for cut in shards[1:]:
        level = level * one(*cut)
    return level


def bell_draw(stream_key, dims, deviation, limit, split=(), held_as=jnp.bfloat16):
    array = deviation * jax.random.normal(stream_key, dims, jnp.float32)
    if split:
        array = array * block_levels(stream_key, dims, split, -0.22, 0.18)
    return jnp.clip(array, -limit, limit).astype(held_as)


def setup_inputs(seed: int = 0) -> dict:
    key_of = jax.random.split(jax.random.key(seed), 16)
    maps_in = bell_draw(key_of[0], (MAPS, PIX, C), 1.0, 6.0, ((0, 16), (2, 2)))
    timesteps = place_ends(jax.random.randint(key_of[1], (MAPS,), 0, STEPS), jax.random.fold_in(key_of[1], 1), 0, STEPS - 1).astype(jnp.int32)
    temb_table = bell_draw(key_of[2], (STEPS, TEMB), 1.0, 6.0, (), jnp.float32)
    norm_gain = jnp.clip(1.0 + 0.15 * jax.random.normal(key_of[3], (3, C), jnp.float32), 0.25, 1.75)
    norm_bias = bell_draw(key_of[4], (3, C), 0.3, 2.0, ((1, 2),), jnp.float32)
    conv1_weight = bell_draw(key_of[5], (3, 3, C, C), (9 * C) ** -0.5, 0.125, ((3, 2),))
    conv_bias = bell_draw(key_of[6], (2, C), 0.3, 2.0, ((1, 2),), jnp.float32)
    temb_weight = bell_draw(key_of[7], (TEMB, C), TEMB ** -0.5, 0.25, ((1, 2),))
    temb_bias = bell_draw(key_of[8], (C,), 0.3, 2.0, ((0, 2),), jnp.float32)
    conv2_weight = bell_draw(key_of[9], (3, 3, C, C), (9 * C) ** -0.5, 0.125, ((2, 2),))
    qkv_weight = bell_draw(key_of[10], (C, 3, C), (C // 2) ** -0.5, 0.5, ((2, 2),))
    qkv_bias = bell_draw(key_of[11], (2, C), 0.3, 2.0, ((1, 2),), jnp.float32)
    out_weight = bell_draw(key_of[12], (C, C), (C // 64) ** -0.5, 3.0, ((0, 2),))
    out_bias = bell_draw(key_of[13], (C,), 0.3, 2.0, ((0, 2),), jnp.float32)
    out_grad = bell_draw(key_of[14], (MAPS, PIX, C), 1.0, 6.0, ((0, 16), (2, 2)))
    return dict(maps_in=maps_in, timesteps=timesteps, temb_table=temb_table, norm_gain=norm_gain, norm_bias=norm_bias, conv1_weight=conv1_weight, conv_bias=conv_bias, temb_weight=temb_weight, temb_bias=temb_bias, conv2_weight=conv2_weight, qkv_weight=qkv_weight, qkv_bias=qkv_bias, out_weight=out_weight, out_bias=out_bias, out_grad=out_grad)


@jax.custom_vjp
def low(v):
    return lax.optimization_barrier(v.astype(jnp.bfloat16)).astype(jnp.float32)

@jax.custom_vjp
def low_back(v):
    return v

def low_keep(v):
    return (low(v), None)

def low_pass(kept, grad):
    return (grad,)

def back_keep(v):
    return (v, None)

def back_low(kept, grad):
    return (low(grad),)
low.defvjp(low_keep, low_pass)
low_back.defvjp(back_keep, back_low)
epsilon = 1e-06

def group_norm(values, gain_row, shift_row):
    count_maps, count_pix, count_ch = values.shape
    group_size = C // GROUPS
    grouped = values.reshape(count_maps, count_pix, count_ch // group_size, group_size)
    center = lax.optimization_barrier(jnp.mean(grouped, axis=(1, 3), keepdims=True))
    spread = lax.optimization_barrier(jnp.mean((grouped - center) ** 2, axis=(1, 3), keepdims=True))
    normed = ((grouped - center) * lax.rsqrt(spread + epsilon)).reshape(count_maps, count_pix, count_ch)
    return normed * gain_row + shift_row

def conv_same(inputs, kernel):
    count_maps = inputs.shape[0]
    grid = inputs.reshape(count_maps, SIDE, SIDE, inputs.shape[2])
    result = lax.conv_general_dilated(grid, kernel, (1, 1), 'SAME', dimension_numbers=('NHWC', 'HWIO', 'NHWC'), precision=lax.Precision.HIGHEST)
    return result.reshape(count_maps, SIDE * SIDE, kernel.shape[3])

def forward(params, block_x, block_t):
    emb_table, gain_rows, shift_rows, conv_one, conv_biases, temb_proj, temb_shift, conv_two, qkv_proj, qkv_shift, out_proj, out_shift = params
    highest = lax.Precision.HIGHEST
    embedded = emb_table[block_t]
    first = low(jax.nn.silu(group_norm(block_x, gain_rows[0], shift_rows[0])))
    time_proj = jnp.dot(jax.nn.silu(embedded), temb_proj, precision=highest) + temb_shift
    hidden = low_back(conv_same(first, conv_one) + conv_biases[0] + time_proj[:, None, :])
    second = low(jax.nn.silu(group_norm(hidden, gain_rows[1], shift_rows[1])))
    middle = block_x + low_back(conv_same(second, conv_two)) + conv_biases[1]
    third = low(group_norm(middle, gain_rows[2], shift_rows[2]))
    projected = jnp.einsum('mpc,cjd->mpjd', third, qkv_proj, precision=highest)
    queries = low(low_back(projected[:, :, 0] + qkv_shift[0]))
    key_rows = low(low_back(projected[:, :, 1]))
    value_rows = low(low_back(projected[:, :, 2] + qkv_shift[1]))
    score_scale = 1.0 / math.sqrt(C)
    scores = low_back(jnp.einsum('mqc,mkc->mqk', queries, key_rows, precision=highest) * score_scale)
    soft_probs = jax.nn.softmax(scores, axis=-1)
    attended = low(low_back(jnp.einsum('mqk,mkc->mqc', low(soft_probs), value_rows, precision=highest)))
    return middle + low_back(jnp.einsum('mqc,cd->mqd', attended, out_proj, precision=highest)) + out_shift

def reference(maps_in, timesteps, temb_table, norm_gain, norm_bias, conv1_weight, conv_bias, temb_weight, temb_bias, conv2_weight, qkv_weight, qkv_bias, out_weight, out_bias, out_grad):
    params = (temb_table, norm_gain, norm_bias, conv1_weight.astype(jnp.float32), conv_bias, temb_weight.astype(jnp.float32), temb_bias, conv2_weight.astype(jnp.float32), qkv_weight.astype(jnp.float32), qkv_bias, out_weight.astype(jnp.float32), out_bias)
    blocks = MAPS // 16
    all_x = maps_in.astype(jnp.float32).reshape(blocks, 16, PIX, C)
    all_t = timesteps.astype(jnp.int32).reshape(blocks, 16)
    all_g = out_grad.astype(jnp.float32).reshape(blocks, 16, PIX, C)

    def scan_step(running, block_in):
        block_x, block_t, block_g = block_in

        def local_forward(param_set, inputs):
            return forward(param_set, inputs, block_t)
        result, pull_back = jax.vjp(local_forward, params, block_x)
        param_grads, input_grad = pull_back(block_g)
        running = jax.tree.map(lambda left, right: left + right, running, param_grads)
        return (running, (result.astype(jnp.bfloat16), input_grad))
    zero_grads = jax.tree.map(jnp.zeros_like, params)
    running, (results, input_grads) = lax.scan(scan_step, zero_grads, (all_x, all_t, all_g))
    return (results.reshape(MAPS, PIX, C), input_grads.reshape(MAPS, PIX, C), running[0], running[1], running[2], running[3], running[4], running[5], running[6], running[7], running[8], running[9], running[10], running[11])
```

```python
import jax
import jax.numpy as jnp
from jax import lax
from jax.experimental import pallas as pl
from jax.experimental.pallas import tpu as pltpu
from jax.sharding import PartitionSpec as P

C = 256
HALF = 128
SIDE = 16
PIX = 256
GROUP = 8
EPS = 1e-06
F32 = jnp.float32
BF16 = jnp.bfloat16
WHOLE = pl.BlockSpec(memory_space=pltpu.VMEM)
SCALAR = pl.BlockSpec(memory_space=pltpu.SMEM)


def call(body, outs, *args, scratch=(), flops=0, limit=24):
    return pl.pallas_call(
        body,
        out_shape=tuple(jax.ShapeDtypeStruct(s, d) for s, d in outs),
        in_specs=[SCALAR] + [WHOLE] * (len(args) - 1),
        out_specs=tuple(WHOLE for _ in outs),
        scratch_shapes=list(scratch),
        compiler_params=pltpu.CompilerParams(vmem_limit_bytes=limit << 20),
        cost_estimate=pl.CostEstimate(flops=flops, bytes_accessed=1 << 20, transcendentals=0),
    )(*args)


def dot(a, b):
    return jnp.dot(a, b, preferred_element_type=F32)


def dot_bt(a, b):
    return lax.dot_general(a, b, (((1,), (1,)), ((), ())), preferred_element_type=F32)


def dot_at(a, b):
    return lax.dot_general(a, b, (((0,), (0,)), ((), ())), preferred_element_type=F32)


def join(first, own, recv, axis):
    low = jnp.where(first, own, recv)
    high = jnp.where(first, recv, own)
    return jnp.concatenate([low, high], axis=axis)


def group_sum(rows):
    lane = lax.broadcasted_iota(jnp.int32, rows.shape, 1)
    width = rows.shape[1]
    for step in (1, 2, 4):
        up = pltpu.roll(rows, width - step, 1)
        down = pltpu.roll(rows, step, 1)
        rows = rows + jnp.where((lane & step) == 0, up, down)
    return rows


def col_sum(values):
    return jnp.sum(values, axis=0, keepdims=True)


def norm_stats(maps):
    count = PIX * GROUP
    mean = group_sum(jnp.concatenate([col_sum(v) for v in maps], axis=0)) / count
    square = [col_sum((v - mean[m : m + 1]) ** 2) for m, v in enumerate(maps)]
    var = group_sum(jnp.concatenate(square, axis=0)) / count
    return mean, lax.rsqrt(var + EPS)


def norm_back(grads, units, gain, rstd):
    count = PIX * GROUP
    plain = jnp.concatenate([col_sum(g) for g in grads], axis=0)
    scaled = jnp.concatenate([col_sum(g * u) for g, u in zip(grads, units)], axis=0)
    both = group_sum(jnp.concatenate([plain * gain, scaled * gain], axis=0)) / count
    n = len(grads)
    result = []
    for m in range(n):
        inner = grads[m] * gain - both[m : m + 1] - units[m] * both[n + m : n + m + 1]
        result.append(inner * rstd[m : m + 1])
    return result, col_sum(scaled), col_sum(plain)


def sigmoid(v):
    return 1.0 / (1.0 + jnp.exp(-v))


def put_windows(win_ref, m, values):
    col = lax.broadcasted_iota(jnp.int32, (PIX, 1), 0) & (SIDE - 1)
    before = jnp.where(col == 0, 0.0, pltpu.roll(values, 1, 0))
    after = jnp.where(col == SIDE - 1, 0.0, pltpu.roll(values, PIX - 1, 0))
    blank = jnp.zeros((SIDE, C), BF16)
    for c, shifted in enumerate((before, values, after)):
        win_ref[m, c, 0:SIDE, :] = blank
        win_ref[m, c, SIDE + PIX : 2 * SIDE + PIX, :] = blank
        win_ref[m, c, SIDE : SIDE + PIX, :] = shifted.astype(BF16)


def window(win_ref, m, r, c):
    return win_ref[m, c, SIDE * r : SIDE * r + PIX, :]


def all_windows(win_ref, r, c):
    n = win_ref.shape[0]
    return win_ref[:, c, SIDE * r : SIDE * r + PIX, :].reshape(n * PIX, C)


def conv_forward(win_ref, w_ref):
    total = None
    for r in range(3):
        for c in range(3):
            part = dot(all_windows(win_ref, r, c), w_ref[3 * r + c])
            total = part if total is None else total + part
    return total


def conv_transposed(win_ref, w_ref):
    total = None
    for r in range(3):
        for c in range(3):
            part = dot_bt(all_windows(win_ref, 2 - r, 2 - c), w_ref[3 * r + c])
            total = part if total is None else total + part
    return total


def window_scratch(n):
    return pltpu.VMEM((n, 3, PIX + 2 * SIDE, C), BF16)


def first_kernel(mp, x_own, x_recv, w_own, w_recv, prm, emb, tw_own, tw_recv, act, hid, stat, win, wfull):
    first = mp[0] == 0
    n = x_own.shape[0]
    for t in range(9):
        wfull[t] = join(first, w_own[t], w_recv[t], 1)
    xs = [join(first, x_own[m], x_recv[m], 1).astype(F32) for m in range(n)]
    mean, rstd = norm_stats(xs)
    stat[0:n] = mean
    stat[n : 2 * n] = rstd
    for m in range(n):
        u = (xs[m] - mean[m : m + 1]) * (rstd[m : m + 1] * prm[0:1]) + prm[3:4]
        a = u * sigmoid(u)
        act[m] = a.astype(BF16)
        put_windows(win, m, a)
    rows = jnp.where(first, emb[0:n], emb[n : 2 * n])
    e = rows * sigmoid(rows)
    e_high = e.astype(BF16)
    e_low = (e - e_high.astype(F32)).astype(BF16)
    tw = join(first, tw_own[...], tw_recv[...], 1)
    time_row = dot(e_high, tw) + dot(e_low, tw) + prm[11:12] + prm[6:7]
    out = conv_forward(win, wfull)
    for m in range(n):
        hid[m] = out[m * PIX : (m + 1) * PIX] + time_row[m : m + 1]


def second_kernel(mp, x_own, x_recv, hid, w_own, w_recv, prm, act, mid, stat, win, wfull):
    first = mp[0] == 0
    n = x_own.shape[0]
    for t in range(9):
        wfull[t] = join(first, w_own[t], w_recv[t], 0)
    hs = [hid[m] for m in range(n)]
    mean, rstd = norm_stats(hs)
    stat[0:n] = mean
    stat[n : 2 * n] = rstd
    for m in range(n):
        u = (hs[m] - mean[m : m + 1]) * (rstd[m : m + 1] * prm[1:2]) + prm[4:5]
        a = u * sigmoid(u)
        act[m] = a.astype(BF16)
        put_windows(win, m, a)
    out = conv_forward(win, wfull)
    for m in range(n):
        x = join(first, x_own[m], x_recv[m], 1).astype(F32)
        mid[m] = x + out[m * PIX : (m + 1) * PIX] + prm[7:8]


def attention_kernel(
    mp, mid, g_own, g_recv, qw_own, qw_recv, ow_own, ow_recv, prm,
    out_keep, out_send, dmid, wg_keep, wg_send, sums, unit, qkv, att, third, dall,
):
    first = mp[0] == 0
    n = mid.shape[0]
    scale = 1.0 / 16.0
    qw = [join(first, qw_own[j], qw_recv[j], 1) for j in range(3)]
    ow = join(first, ow_own[...], ow_recv[...], 0)
    ms = [mid[m] for m in range(n)]
    mean, rstd = norm_stats(ms)
    for m in range(n):
        un = (ms[m] - mean[m : m + 1]) * rstd[m : m + 1]
        unit[m] = un
        third[m * PIX : (m + 1) * PIX] = (un * prm[2:3] + prm[5:6]).astype(BF16)
    for j in range(3):
        part = dot(third[...], qw[j])
        if j == 0:
            part = part + prm[8:9]
        if j == 2:
            part = part + prm[9:10]
        qkv[j] = part.astype(BF16)
    for m in range(n):
        rows = slice(m * PIX, (m + 1) * PIX)
        q, k, v = qkv[0, rows], qkv[1, rows], qkv[2, rows]
        s = dot_bt(q, k) * scale
        e = jnp.exp(s - jnp.max(s, axis=1, keepdims=True))
        p = e * (1.0 / jnp.sum(e, axis=1, keepdims=True))
        p_low = p.astype(BF16)
        a = dot(p_low, v).astype(BF16)
        att[rows] = a
        result = mid[m] + dot(a, ow) + prm[10:11]
        left, right = result[:, :HALF].astype(BF16), result[:, HALF:].astype(BF16)
        out_keep[m] = jnp.where(first, left, right)
        out_send[m] = jnp.where(first, right, left)
        gb = join(first, g_own[m], g_recv[m], 1)
        da = dot_bt(gb, ow).astype(BF16)
        dp = dot_bt(da, v)
        ds = (p * (dp - jnp.sum(p * dp, axis=1, keepdims=True))).astype(BF16)
        dall[0, rows] = (dot(ds, k) * scale).astype(BF16)
        dall[1, rows] = (dot_at(ds, q) * scale).astype(BF16)
        dall[2, rows] = dot_at(p_low, da).astype(BF16)
    g_all = jnp.concatenate([join(first, g_own[m], g_recv[m], 1) for m in range(n)], axis=0)
    og = dot_at(att[...], g_all).astype(BF16)
    for h in range(2):
        lanes = slice(h * HALF, (h + 1) * HALF)
        top, low = og[:HALF, lanes], og[HALF:, lanes]
        wg_keep[3 * C + h * HALF : 3 * C + (h + 1) * HALF] = jnp.where(first, top, low)
        wg_send[3 * C + h * HALF : 3 * C + (h + 1) * HALF] = jnp.where(first, low, top)
    third_grad = None
    for j in range(3):
        d = dall[j]
        qg = dot_at(third[...], d).astype(BF16)
        left, right = qg[:, :HALF], qg[:, HALF:]
        wg_keep[j * C : (j + 1) * C] = jnp.where(first, left, right)
        wg_send[j * C : (j + 1) * C] = jnp.where(first, right, left)
        part = dot_bt(d, qw[j])
        third_grad = part if third_grad is None else third_grad + part
    grads = [third_grad[m * PIX : (m + 1) * PIX] for m in range(n)]
    units = [unit[m] for m in range(n)]
    back, gain_grad, bias_grad = norm_back(grads, units, prm[2:3], rstd)
    mid_bias = jnp.zeros((1, C), F32)
    for m in range(n):
        d = back[m] + join(first, g_own[m], g_recv[m], 1).astype(F32)
        dmid[m] = d
        mid_bias = mid_bias + col_sum(d)
    sums[0:1] = gain_grad
    sums[1:2] = bias_grad
    sums[2:3] = mid_bias
    sums[3:4] = col_sum(dall[0].astype(F32))
    sums[4:5] = col_sum(dall[2].astype(F32))
    sums[5:6] = col_sum(g_all.astype(F32))
    sums[6:8] = jnp.zeros((2, C), F32)


def turned(values):
    return jnp.concatenate([values[m].T for m in range(values.shape[0])], axis=1)


def conv2_grad_kernel(mp, dmid, act, keep, send, win):
    first = mp[0] == 0
    for m in range(dmid.shape[0]):
        put_windows(win, m, dmid[m])
    act_t = turned(act)
    for r in range(3):
        for c in range(3):
            t = 3 * r + c
            g = dot(act_t, all_windows(win, 2 - r, 2 - c)).astype(BF16)
            for h in range(2):
                lanes = slice(h * HALF, (h + 1) * HALF)
                rows = slice((2 * t + h) * HALF, (2 * t + h + 1) * HALF)
                keep[rows] = jnp.where(first, g[:HALF, lanes], g[HALF:, lanes])
                send[rows] = jnp.where(first, g[HALF:, lanes], g[:HALF, lanes])


def hidden_back_kernel(mp, win, hid, stat, w_own, w_recv, prm, dhid, sums, dtime, wfull):
    first = mp[0] == 0
    n = hid.shape[0]
    for t in range(9):
        wfull[t] = join(first, w_own[t], w_recv[t], 0)
    second_grad = conv_transposed(win, wfull)
    units, grads = [], []
    for m in range(n):
        un = (hid[m] - stat[m : m + 1]) * stat[n + m : n + m + 1]
        u = un * prm[1:2] + prm[4:5]
        sig = sigmoid(u)
        units.append(un)
        grads.append(second_grad[m * PIX : (m + 1) * PIX] * (sig * (1.0 + u * (1.0 - sig))))
    back, gain_grad, bias_grad = norm_back(grads, units, prm[1:2], stat[n : 2 * n])
    rows = []
    for m in range(n):
        low = back[m].astype(BF16)
        dhid[m] = low
        rows.append(col_sum(low.astype(F32)))
    dt = jnp.concatenate(rows, axis=0)
    dtime[...] = dt
    sums[0:1] = gain_grad
    sums[1:2] = bias_grad
    sums[2:3] = col_sum(dt)
    sums[3:8] = jnp.zeros((5, C), F32)


def conv1_grad_kernel(mp, dhid, act, keep, send, win):
    first = mp[0] == 0
    for m in range(dhid.shape[0]):
        put_windows(win, m, dhid[m].astype(F32))
    act_t = turned(act)
    for r in range(3):
        for c in range(3):
            t = 3 * r + c
            g = dot(act_t, all_windows(win, 2 - r, 2 - c)).astype(BF16)
            left, right = g[:, :HALF], g[:, HALF:]
            keep[t * C : (t + 1) * C] = jnp.where(first, left, right)
            send[t * C : (t + 1) * C] = jnp.where(first, right, left)


def input_back_kernel(mp, win, x_own, x_recv, stat, w_own, w_recv, prm, dmid, keep, send, sums, wfull):
    first = mp[0] == 0
    n = x_own.shape[0]
    for t in range(9):
        wfull[t] = join(first, w_own[t], w_recv[t], 1)
    first_grad = conv_transposed(win, wfull)
    units, grads = [], []
    for m in range(n):
        x = join(first, x_own[m], x_recv[m], 1).astype(F32)
        un = (x - stat[m : m + 1]) * stat[n + m : n + m + 1]
        u = un * prm[0:1] + prm[3:4]
        sig = sigmoid(u)
        units.append(un)
        grads.append(first_grad[m * PIX : (m + 1) * PIX] * (sig * (1.0 + u * (1.0 - sig))))
    back, gain_grad, bias_grad = norm_back(grads, units, prm[0:1], stat[n : 2 * n])
    for m in range(n):
        d = back[m] + dmid[m]
        left, right = d[:, :HALF], d[:, HALF:]
        keep[m] = jnp.where(first, left, right)
        send[m] = jnp.where(first, right, left).astype(BF16)
    sums[0:1] = gain_grad
    sums[1:2] = bias_grad
    sums[2:8] = jnp.zeros((6, C), F32)


def table_kernel(mp, dtime, emb, tw_own, tw_recv, times, table, tw_grad):
    first = mp[0] == 0
    tw = join(first, tw_own[...], tw_recv[...], 1)
    e = emb[...]
    sig = sigmoid(e)
    demb = dot_bt(dtime[...], tw) * (sig * (1.0 + e * (1.0 - sig)))
    act = e * sig
    act_high = act.astype(BF16)
    act_low = (act - act_high.astype(F32)).astype(BF16)
    mine = jnp.where(first, dtime[:, :HALF], dtime[:, HALF:])
    tw_grad[...] = dot_at(act_high, mine) + dot_at(act_low, mine)
    steps = table.shape[0]
    row = lax.broadcasted_iota(jnp.int32, (steps, e.shape[0]), 0)
    pick = jnp.where(row == times[...], 1.0, 0.0).astype(BF16)
    d_high = demb.astype(BF16)
    rest = demb - d_high.astype(F32)
    d_low = rest.astype(BF16)
    table[...] = dot(pick, d_high) + dot(pick, d_low)


def stages_of(count):
    stages, bit = [], 0
    while (1 << bit) < count:
        width = 2 if (1 << (bit + 2)) <= count else 1
        stages.append((bit, 1 << width))
        bit += width
    return stages


def swap_dp(values, flip):
    count = lax.axis_size("dp")
    return lax.ppermute(values, "dp", [(i, i ^ flip) for i in range(count)])


def swap_mp(values):
    return lax.ppermute(values, "mp", [(0, 1), (1, 0)])


ORDER = {2: (1,), 4: (1, 3, 2)}


def take(values, index):
    return lax.dynamic_index_in_dim(values, index, 0, keepdims=False)


def scatter_stage(values, stage):
    bit, size = stage
    me = (lax.axis_index("dp") >> bit) & (size - 1)
    total = take(values, me).astype(F32)
    for k in ORDER[size]:
        total = total + swap_dp(take(values, me ^ k), k << bit).astype(F32)
    return total.astype(BF16)


def gather_stage(values, stage):
    bit, size = stage
    me = (lax.axis_index("dp") >> bit) & (size - 1)
    result = jnp.zeros((size,) + values.shape, values.dtype)
    result = lax.dynamic_update_index_in_dim(result, values, me, 0)
    for k in ORDER[size]:
        result = lax.dynamic_update_index_in_dim(result, swap_dp(values, k << bit), me ^ k, 0)
    return result


def reduce_scatter(values, stages):
    count = lax.axis_size("dp")
    values = values.reshape(tuple(s for _, s in stages) + (values.shape[0] // count, HALF))
    for stage in stages:
        values = scatter_stage(values, stage)
    return values


def gather(values, stages):
    rows = values.shape[0]
    for stage in reversed(stages):
        values = gather_stage(values, stage)
    return values.reshape(-1, rows, HALF)


def on_device(
    maps_in, timesteps, temb_table, norm_gain, norm_bias, conv1_weight, conv_bias, temb_weight,
    temb_bias, conv2_weight, qkv_weight, qkv_bias, out_weight, out_bias, out_grad,
):
    me = lax.axis_index("mp")
    count = lax.axis_size("dp")
    stages = stages_of(count)
    n = maps_in.shape[0] // 2
    mp = jnp.reshape(me, (1,)).astype(jnp.int32)
    first = me == 0

    def mine(values):
        return lax.dynamic_slice_in_dim(values, me * n, n, 0)

    def theirs(values):
        return lax.dynamic_slice_in_dim(values, (1 - me) * n, n, 0)

    prm_own = jnp.concatenate(
        [norm_gain, norm_bias, conv_bias, qkv_bias, out_bias[None], temb_bias[None], jnp.zeros((4, HALF), F32)]
    )
    prm_recv = swap_mp(prm_own)
    prm = jnp.where(
        first,
        jnp.concatenate([prm_own, prm_recv], axis=1),
        jnp.concatenate([prm_recv, prm_own], axis=1),
    )
    x_own, x_recv = mine(maps_in), swap_mp(theirs(maps_in))
    w1_own = conv1_weight.reshape(9, C, HALF)
    w1_recv = swap_mp(w1_own)
    tw_recv = swap_mp(temb_weight)
    w2_own = conv2_weight.reshape(9, HALF, C)
    w2_recv = swap_mp(w2_own)
    qw_own = jnp.transpose(qkv_weight, (1, 0, 2))
    qw_recv = swap_mp(qw_own)
    ow_recv = swap_mp(out_weight)
    g_own, g_recv = mine(out_grad), swap_mp(theirs(out_grad))
    emb = jnp.take(temb_table, timesteps, axis=0)

    maps_shape = (n, PIX, C)
    unit = 2 * n * PIX * C * C
    act1, hid, stat1 = call(
        first_kernel,
        [(maps_shape, BF16), (maps_shape, F32), ((2 * n, C), F32)],
        mp, x_own, x_recv, w1_own, w1_recv, prm, emb, temb_weight, tw_recv,
        scratch=[window_scratch(n), pltpu.VMEM((9, C, C), BF16)],
        flops=9 * unit,
    )
    act2, mid, stat2 = call(
        second_kernel,
        [(maps_shape, BF16), (maps_shape, F32), ((2 * n, C), F32)],
        mp, x_own, x_recv, hid, w2_own, w2_recv, prm,
        scratch=[window_scratch(n), pltpu.VMEM((9, C, C), BF16)],
        flops=9 * unit,
    )
    half_shape = (n, PIX, HALF)
    out_keep, out_send, dmid, wg_keep, wg_send, sums3 = call(
        attention_kernel,
        [
            (half_shape, BF16), (half_shape, BF16), (maps_shape, F32),
            ((4 * C, HALF), BF16), ((4 * C, HALF), BF16), ((8, C), F32),
        ],
        mp, mid, g_own, g_recv, qw_own, qw_recv, out_weight, ow_recv, prm,
        scratch=[
            pltpu.VMEM(maps_shape, F32),
            pltpu.VMEM((3, n * PIX, C), BF16),
            pltpu.VMEM((n * PIX, C), BF16),
            pltpu.VMEM((n * PIX, C), BF16),
            pltpu.VMEM((3, n * PIX, C), BF16),
        ],
        flops=18 * unit,
    )
    win_shape = (n, 3, PIX + 2 * SIDE, C)
    grad_shape = (9 * C, HALF)
    c2_keep, c2_send, win2 = call(
        conv2_grad_kernel,
        [(grad_shape, BF16), (grad_shape, BF16), (win_shape, BF16)],
        mp, dmid, act2,
        flops=9 * unit,
    )
    dhid, sums2, dtime = call(
        hidden_back_kernel,
        [(maps_shape, BF16), ((8, C), F32), ((n, C), F32)],
        mp, win2, hid, stat2, w2_own, w2_recv, prm,
        scratch=[pltpu.VMEM((9, C, C), BF16)],
        flops=9 * unit,
    )
    c1_keep, c1_send, win1 = call(
        conv1_grad_kernel,
        [(grad_shape, BF16), (grad_shape, BF16), (win_shape, BF16)],
        mp, dhid, act1,
        flops=9 * unit,
    )
    mg_keep, mg_send, sums1 = call(
        input_back_kernel,
        [(half_shape, F32), (half_shape, BF16), ((8, C), F32)],
        mp, win1, x_own, x_recv, stat1, w1_own, w1_recv, prm, dmid,
        scratch=[pltpu.VMEM((9, C, C), BF16)],
        flops=9 * unit,
    )

    def paired(keep, send):
        return (keep.astype(F32) + swap_mp(send).astype(F32)).astype(BF16)

    early = jnp.concatenate([paired(c2_keep, c2_send), paired(wg_keep, wg_send)])
    late = paired(c1_keep, c1_send)
    early = reduce_scatter(early, stages)
    late = reduce_scatter(late, stages)

    small = jnp.concatenate(
        [
            sums1[0:1], sums2[0:1], sums3[0:1], sums1[1:2], sums2[1:2], sums3[1:2],
            sums2[2:3], sums3[2:3], sums3[3:6], jnp.zeros((5, C), F32),
        ]
    )
    small_keep = jnp.where(first, small[:, :HALF], small[:, HALF:])
    small_send = jnp.where(first, small[:, HALF:], small[:, :HALF])
    rows_send = jnp.concatenate([small_send, dtime.reshape(2 * n, HALF)])
    rows_recv = swap_mp(rows_send)
    small = small_keep + rows_recv[:16]
    time_own, time_recv = dtime.reshape(2 * n, HALF), rows_recv[16:]
    time_rows = jnp.where(
        first,
        jnp.concatenate([time_own, time_recv]),
        jnp.concatenate([time_recv, time_own]),
    )
    step_row = jnp.concatenate(
        [timesteps >> 5, timesteps & 31, jnp.zeros((HALF - 4 * n,), jnp.int32)]
    ).astype(F32)[None]
    extra = jnp.concatenate([small[:11], step_row, small[12:], time_rows]).astype(BF16)
    early_rows = early.shape[0]
    early = gather(jnp.concatenate([early, extra]), stages)
    late = gather(late, stages)

    extra = early[:, early_rows:]
    early = early[:, :early_rows].reshape(-1, HALF)
    small = jnp.sum(extra[:, :16].astype(F32), axis=0)
    steps = extra[:, 11, : 4 * n].astype(jnp.int32)
    steps = (steps[:, : 2 * n] * 32 + steps[:, 2 * n :]).reshape(-1)
    time_all = extra[:, 16:].reshape(count * 2 * n, C)
    emb_all = jnp.take(temb_table, steps, axis=0)
    table_grad, temb_weight_grad = call(
        table_kernel,
        [(temb_table.shape, F32), (temb_weight.shape, F32)],
        mp, time_all, emb_all, temb_weight, tw_recv, steps[None],
        flops=unit,
    )
    temb_bias_sum = jnp.sum(time_all.astype(F32), axis=0)
    temb_bias_grad = jnp.where(first, temb_bias_sum[:HALF], temb_bias_sum[HALF:])

    def both_maps(keep, recv):
        return jnp.where(first, jnp.concatenate([keep, recv]), jnp.concatenate([recv, keep]))

    maps_out = both_maps(out_keep, swap_mp(out_send))
    maps_grad = both_maps(mg_keep, swap_mp(mg_send).astype(F32))

    early = early.astype(F32)
    conv2_grad = early[: 9 * C].reshape(9, 2, HALF, HALF)
    conv2_grad = jnp.transpose(conv2_grad, (0, 2, 1, 3)).reshape(3, 3, HALF, C)
    qkv_grad = jnp.transpose(early[9 * C : 12 * C].reshape(3, C, HALF), (1, 0, 2))
    out_weight_grad = jnp.transpose(early[12 * C :].reshape(2, HALF, HALF), (1, 0, 2)).reshape(HALF, C)
    conv1_grad = late.astype(F32).reshape(3, 3, C, HALF)
    return (
        maps_out, maps_grad, table_grad, small[0:3], small[3:6], conv1_grad, small[6:8],
        temb_weight_grad, temb_bias_grad, conv2_grad, qkv_grad, small[8:10], out_weight_grad, small[10],
    )


def solution(mesh):
    args = (
        P("dp", None, "mp"), P("dp"), P(), P(None, "mp"), P(None, "mp"), P(None, None, None, "mp"),
        P(None, "mp"), P(None, "mp"), P("mp"), P(None, None, "mp", None), P(None, None, "mp"),
        P(None, "mp"), P("mp", None), P("mp"), P("dp", None, "mp"),
    )
    outs = (
        P("dp", None, "mp"), P("dp", None, "mp"), P(), P(None, "mp"), P(None, "mp"),
        P(None, None, None, "mp"), P(None, "mp"), P(None, "mp"), P("mp"), P(None, None, "mp", None),
        P(None, None, "mp"), P(None, "mp"), P("mp", None), P("mp"),
    )
    return jax.shard_map(on_device, mesh=mesh, in_specs=args, out_specs=outs, check_vma=False)
```

```python
import jax
import jax.numpy as jnp
from jax import lax
from jax.experimental import pallas as pl
from jax.experimental.pallas import tpu as pltpu
from jax.sharding import PartitionSpec as P

C = 256
HALF = 128
SIDE = 16
PIX = 256
GROUP = 8
EPS = 1e-06
F32 = jnp.float32
BF16 = jnp.bfloat16
WHOLE = pl.BlockSpec(memory_space=pltpu.VMEM)
SCALAR = pl.BlockSpec(memory_space=pltpu.SMEM)
ANYWHERE = pl.BlockSpec(memory_space=pl.ANY)
IN_HBM = pl.BlockSpec(memory_space=pltpu.HBM)


def call(body, outs, *args, scratch=(), specs=None, limit=16, flops=1):
    specs = specs or {}
    return pl.pallas_call(
        body,
        out_shape=tuple(jax.ShapeDtypeStruct(s, d) for s, d in outs),
        in_specs=[specs.get(i, WHOLE) for i in range(len(args))],
        out_specs=tuple(WHOLE for _ in outs),
        scratch_shapes=list(scratch),
        compiler_params=pltpu.CompilerParams(vmem_limit_bytes=limit << 20),
        cost_estimate=pl.CostEstimate(flops=flops, bytes_accessed=0, transcendentals=0),
    )(*args)


def dot(a, b):
    return jnp.dot(a, b, preferred_element_type=F32)


def dot_bt(a, b):
    return lax.dot_general(a, b, (((1,), (1,)), ((), ())), preferred_element_type=F32)


def dot_at(a, b):
    return lax.dot_general(a, b, (((0,), (0,)), ((), ())), preferred_element_type=F32)


def join(first, own, recv, axis):
    low = jnp.where(first, own, recv)
    high = jnp.where(first, recv, own)
    return jnp.concatenate([low, high], axis=axis)


def split(first, values, axis=1):
    low, high = jnp.split(values, 2, axis)
    return jnp.where(first, low, high), jnp.where(first, high, low)


def group_merge(mean, square, count):
    lane = lax.broadcasted_iota(jnp.int32, mean.shape, 1)
    width = mean.shape[1]

    def partner(rows, step):
        up = pltpu.roll(rows, width - step, 1)
        down = pltpu.roll(rows, step, 1)
        return jnp.where((lane & step) == 0, up, down)

    for step in (1, 2, 4):
        other = partner(mean, step)
        gap = mean - other
        square = square + partner(square, step) + gap * gap * (0.5 * count * step)
        mean = 0.5 * (mean + other)
    return mean, square


def group_sum(rows):
    lane = lax.broadcasted_iota(jnp.int32, rows.shape, 1)
    width = rows.shape[1]
    for step in (1, 2, 4):
        up = pltpu.roll(rows, width - step, 1)
        down = pltpu.roll(rows, step, 1)
        rows = rows + jnp.where((lane & step) == 0, up, down)
    return rows


def col_sum(values):
    return jnp.sum(values, axis=0, keepdims=True)


def norm_stats(values):
    mean = col_sum(values) * (1.0 / PIX)
    square = col_sum((values - mean) ** 2)
    mean, square = group_merge(mean, square, PIX)
    return mean, lax.rsqrt(square * (1.0 / (PIX * GROUP)) + EPS)


def all_stats(maps):
    means = [col_sum(v) * (1.0 / PIX) for v in maps]
    squares = [col_sum((v - mean) ** 2) for v, mean in zip(maps, means)]
    mean, square = group_merge(jnp.concatenate(means, axis=0), jnp.concatenate(squares, axis=0), PIX)
    return mean, lax.rsqrt(square * (1.0 / (PIX * GROUP)) + EPS)


def norm_back(grad, unit, gain, rstd):
    plain = col_sum(grad)
    scaled = col_sum(grad * unit)
    both = group_sum(jnp.concatenate([plain * gain, scaled * gain], axis=0)) * (1.0 / (PIX * GROUP))
    inner = grad * gain - both[0:1] - unit * both[1:2]
    return inner * rstd, scaled, plain


def sigmoid(v):
    return 1.0 / (1.0 + jnp.exp(-v))


def put_windows(win, values):
    col = lax.broadcasted_iota(jnp.int32, (PIX, 1), 0) & (SIDE - 1)
    before = jnp.where(col == 0, 0.0, pltpu.roll(values, 1, 0))
    after = jnp.where(col == SIDE - 1, 0.0, pltpu.roll(values, PIX - 1, 0))
    blank = jnp.zeros((SIDE, C), BF16)
    for c, shifted in enumerate((before, values, after)):
        win[c, 0:SIDE, :] = blank
        win[c, SIDE + PIX : 2 * SIDE + PIX, :] = blank
        win[c, SIDE : SIDE + PIX, :] = shifted.astype(BF16)


def window(win, r, c):
    return win[c, SIDE * r : SIDE * r + PIX, :]


def conv_forward(win, w_ref):
    total = None
    for r in range(3):
        for c in range(3):
            part = dot(window(win, r, c), w_ref[3 * r + c])
            total = part if total is None else total + part
    return total


def conv_transposed(win, w_ref):
    total = None
    for r in range(3):
        for c in range(3):
            part = dot_bt(window(win, 2 - r, 2 - c), w_ref[3 * r + c])
            total = part if total is None else total + part
    return total


WIN = ((3, PIX + 2 * SIDE, C), BF16)

GAIN, BIAS, CONV_B, QKV_B, OUT_B, TIME_B, PACK = 0, 3, 6, 8, 10, 11, 16


def blank_kernel(result):
    result[...] = jnp.zeros_like(result)


def time_kernel(steps, pk, table, tw, result):
    total = result.shape[0] - PACK
    result[0:PACK] = pk[...]
    rows = jnp.concatenate([table[pl.ds(steps[i], 1)] for i in range(total)], axis=0)
    e = rows * sigmoid(rows)
    e_high = e.astype(BF16)
    e_low = (e - e_high.astype(F32)).astype(BF16)
    shift = pk[TIME_B : TIME_B + 1] + pk[CONV_B : CONV_B + 1]
    result[PACK : PACK + total] = dot(e_high, tw[...]) + dot(e_low, tw[...]) + shift


def first_kernel(x_own, x_recv, w_own, w_recv, pk_own, pk_recv, *rest):
    n = x_own.shape[0] // 2
    hid, act_t, act2_t, stat0, stat1, prm_out, wfull = rest[:7]
    win2, wins = rest[7 : 7 + n], rest[7 + n :]
    me = lax.axis_index("mp")
    first = me == 0
    pk = join(first, pk_own[0:PACK], pk_recv[0:PACK], 1)
    prm_out[...] = pk
    xs = [join(first, x_own[me * n + m], x_recv[me * n + m], 1).astype(F32) for m in range(n)]
    mean, rstd = all_stats(xs)
    stat0[0:n] = mean
    stat0[n : 2 * n] = rstd
    scale = rstd * pk[GAIN : GAIN + 1]
    shift = pk[BIAS : BIAS + 1] - mean * scale
    for m in range(n):
        u = xs[m] * scale[m : m + 1] + shift[m : m + 1]
        a = u * sigmoid(u)
        act_t[:, m * PIX : (m + 1) * PIX] = a.astype(BF16).T
        put_windows(wins[m], a)
    for t in range(9):
        wfull[t] = join(first, w_own[t], w_recv[t], 1)
    both = join(first, pk_own[PACK:], pk_recv[PACK:], 1)
    time_row = jnp.where(first, both[0:n], both[n : 2 * n])
    for m in range(n):
        h = conv_forward(wins[m], wfull) + time_row[m : m + 1]
        hid[m] = h
        mean, rstd = norm_stats(h)
        stat1[m : m + 1] = mean
        stat1[n + m : n + m + 1] = rstd
        u = (h - mean) * (rstd * pk[GAIN + 1 : GAIN + 2]) + pk[BIAS + 1 : BIAS + 2]
        a = u * sigmoid(u)
        act2_t[:, m * PIX : (m + 1) * PIX] = a.astype(BF16).T
        put_windows(win2[m], a)


def middle_kernel(x_own, x_recv, w_own, w_recv, prm, g_own, g_recv, qw_own, qw_recv, ow_own, ow_recv, *rest):
    n = g_own.shape[0] // 2
    win2, rest = rest[:n], rest[n:]
    out_keep, out_send, dmid, wg_keep, wg_send, sums, wfull = rest[:7]
    win3, rest = rest[7 : 7 + n], rest[7 + n :]
    qw, ow, rest = rest[0], rest[1], rest[2:]
    mids, units, probs = rest[:n], rest[n : 2 * n], rest[2 * n : 3 * n]
    thirds, qkvs, lows, douts, atts, grads = [rest[(3 + i) * n : (4 + i) * n] for i in range(6)]
    me = lax.axis_index("mp")
    first = me == 0
    scale = 1.0 / 16.0
    for t in range(9):
        wfull[t] = join(first, w_own[t], w_recv[t], 0)
    for j in range(3):
        qw[j] = join(first, qw_own[j], qw_recv[j], 1)
    ow[...] = join(first, ow_own[...], ow_recv[...], 0)
    rstds = []
    for m in range(n):
        at = me * n + m
        x = join(first, x_own[at], x_recv[at], 1).astype(F32)
        mid = x + conv_forward(win2[m], wfull) + prm[CONV_B + 1 : CONV_B + 2]
        mids[m][...] = mid
        mean, rstd = norm_stats(mid)
        rstds.append(rstd)
        unit = (mid - mean) * rstd
        units[m][...] = unit
        thirds[m][...] = (unit * prm[GAIN + 2 : GAIN + 3] + prm[BIAS + 2 : BIAS + 3]).astype(BF16)
    for m in range(n):
        a3 = thirds[m][...]
        qkvs[m][0] = (dot(a3, qw[0]) + prm[QKV_B : QKV_B + 1]).astype(BF16)
        qkvs[m][1] = dot(a3, qw[1]).astype(BF16)
        qkvs[m][2] = (dot(a3, qw[2]) + prm[QKV_B + 1 : QKV_B + 2]).astype(BF16)
    for m in range(n):
        s = dot_bt(qkvs[m][0], qkvs[m][1]) * scale
        e = jnp.exp(s - jnp.max(s, axis=1, keepdims=True))
        p = e * (1.0 / jnp.sum(e, axis=1, keepdims=True))
        probs[m][...] = p
        lows[m][...] = p.astype(BF16)
    for m in range(n):
        gb = join(first, g_own[me * n + m], g_recv[me * n + m], 1)
        douts[m][...] = dot_bt(gb, ow[...]).astype(BF16)
    for m in range(n):
        a = dot(lows[m][...], qkvs[m][2]).astype(BF16)
        atts[m][...] = a
        result = mids[m][...] + dot(a, ow[...]) + prm[OUT_B : OUT_B + 1]
        keep, send = split(first, result.astype(BF16))
        out_keep[m] = keep
        out_send[m] = send
    for m in range(n):
        p = probs[m][...]
        dp = dot_bt(douts[m][...], qkvs[m][2])
        ds = (p * (dp - jnp.sum(p * dp, axis=1, keepdims=True))).astype(BF16)
        grads[m][2] = dot_at(lows[m][...], douts[m][...]).astype(BF16)
        lows[m][...] = ds
    for m in range(n):
        ds = lows[m][...]
        grads[m][0] = (dot(ds, qkvs[m][1]) * scale).astype(BF16)
        grads[m][1] = (dot_at(ds, qkvs[m][0]) * scale).astype(BF16)
    gains, biases, mid_bias, out_bias = [], [], [], []
    for m in range(n):
        grad = dot_bt(grads[m][0], qw[0]) + dot_bt(grads[m][1], qw[1]) + dot_bt(grads[m][2], qw[2])
        back, gain_grad, bias_grad = norm_back(grad, units[m][...], prm[GAIN + 2 : GAIN + 3], rstds[m])
        gains.append(gain_grad)
        biases.append(bias_grad)
        g = join(first, g_own[me * n + m], g_recv[me * n + m], 1).astype(F32)
        out_bias.append(col_sum(g))
        d = back + g
        dmid[m] = d
        mid_bias.append(col_sum(d))
        put_windows(win3[m], d)
    third_t = jnp.concatenate([thirds[m][...].T for m in range(n)], axis=1)
    for j in range(3):
        d = jnp.concatenate([grads[m][j] for m in range(n)], axis=0)
        keep, send = split(first, dot(third_t, d).astype(BF16))
        wg_keep[j * C : (j + 1) * C] = keep
        wg_send[j * C : (j + 1) * C] = send
    att_t = jnp.concatenate([atts[m][...].T for m in range(n)], axis=1)
    g_all = jnp.concatenate([join(first, g_own[me * n + m], g_recv[me * n + m], 1) for m in range(n)], axis=0)
    keep, send = split(first, dot(att_t, g_all).astype(BF16), 0)
    for h in range(2):
        lanes, rows = slice(h * HALF, (h + 1) * HALF), slice(3 * C + h * HALF, 3 * C + (h + 1) * HALF)
        wg_keep[rows] = keep[:, lanes]
        wg_send[rows] = send[:, lanes]
    sums[0:1] = sum(gains)
    sums[1:2] = sum(biases)
    sums[2:3] = sum(mid_bias)
    sums[3:4] = sum(col_sum(grads[m][0].astype(F32)) for m in range(n))
    sums[4:5] = sum(col_sum(grads[m][2].astype(F32)) for m in range(n))
    sums[5:6] = sum(out_bias)
    sums[6:8] = jnp.zeros((2, C), F32)


TAPS = (range(0, 5), range(5, 9))


def conv2_grad_kernel(taps):
    def body(act_t, *rest):
        win, (keep, send) = rest[:-2], rest[-2:]
        first = lax.axis_index("mp") == 0
        for i, t in enumerate(taps):
            shifted = jnp.concatenate([window(w, 2 - t // 3, 2 - t % 3) for w in win], axis=0)
            g_keep, g_send = split(first, dot(act_t[...], shifted).astype(BF16), 0)
            for h in range(2):
                lanes = slice(h * HALF, (h + 1) * HALF)
                rows = slice((2 * i + h) * HALF, (2 * i + h + 1) * HALF)
                keep[rows] = g_keep[:, lanes]
                send[rows] = g_send[:, lanes]

    return body


def hidden_back_kernel(steps, after, hid, stat, wfull, prm, sums3, *rest):
    n = hid.shape[0]
    win3, (rows_keep, rows_send), win4 = rest[:n], rest[n : n + 2], rest[n + 2 :]
    first = lax.axis_index("mp") == 0
    gain, bias = prm[GAIN + 1 : GAIN + 2], prm[BIAS + 1 : BIAS + 2]
    gains, biases, times = [], [], []
    for m in range(n):
        rstd = stat[n + m : n + m + 1]
        unit = (hid[m] - stat[m : m + 1]) * rstd
        u = unit * gain + bias
        sig = sigmoid(u)
        slope = sig * (1.0 + u * (1.0 - sig))
        grad = conv_transposed(win3[m], wfull) * slope
        back, gain_grad, bias_grad = norm_back(grad, unit, gain, rstd)
        gains.append(gain_grad)
        biases.append(bias_grad)
        low = back.astype(BF16).astype(F32)
        times.append(col_sum(low))
        put_windows(win4[m], low)
    small = [
        sum(gains), sums3[0:1], sum(biases), sums3[1:2], sum(times), sums3[2:6], jnp.zeros((7, C), F32),
    ]
    small_keep, small_send = split(first, jnp.concatenate(small, axis=0))
    rows_keep[0:16] = small_keep
    rows_send[0:16] = small_send
    time_rows = jnp.concatenate(times, axis=0)
    blank = jnp.zeros((n, HALF), F32)
    for ref in (rows_keep, rows_send):
        ref[16:32] = jnp.concatenate([time_rows[:, :HALF], blank, time_rows[:, HALF:], blank], axis=0)
    for i in range(2 * n):
        rows_keep[32 + i : 33 + i] = jnp.full((1, HALF), steps[i] >> 5, jnp.int32).astype(F32)
        rows_keep[40 + i : 41 + i] = jnp.full((1, HALF), steps[i] & 31, jnp.int32).astype(F32)


def conv1_grad_kernel(taps):
    def body(act_t, *rest):
        win, (keep, send) = rest[:-2], rest[-2:]
        first = lax.axis_index("mp") == 0
        for i, t in enumerate(taps):
            shifted = jnp.concatenate([window(w, 2 - t // 3, 2 - t % 3) for w in win], axis=0)
            g_keep, g_send = split(first, dot(act_t[...], shifted).astype(BF16))
            keep[i * C : (i + 1) * C] = g_keep
            send[i * C : (i + 1) * C] = g_send

    return body


def input_back_kernel(after, x_own, x_recv, stat, wfull, prm, dmid, *rest):
    n = dmid.shape[0]
    win4, (keep, send, rows_keep, rows_send) = rest[:n], rest[n:]
    me = lax.axis_index("mp")
    first = me == 0
    gain, bias = prm[GAIN : GAIN + 1], prm[BIAS : BIAS + 1]
    gains, biases = [], []
    for m in range(n):
        at = me * n + m
        rstd = stat[n + m : n + m + 1]
        x = join(first, x_own[at], x_recv[at], 1).astype(F32)
        unit = (x - stat[m : m + 1]) * rstd
        u = unit * gain + bias
        sig = sigmoid(u)
        slope = sig * (1.0 + u * (1.0 - sig))
        grad = conv_transposed(win4[m], wfull) * slope
        back, gain_grad, bias_grad = norm_back(grad, unit, gain, rstd)
        gains.append(gain_grad)
        biases.append(bias_grad)
        d_keep, d_send = split(first, back + dmid[m])
        keep[m] = d_keep
        send[m] = d_send.astype(BF16)
    small = jnp.concatenate([sum(gains), sum(biases), jnp.zeros((14, C), F32)], axis=0)
    rows_keep[...], rows_send[...] = split(first, small)


def maps_kernel(after, out_keep, out_recv, grad_keep, grad_recv, out, grad, turn):
    n = out_keep.shape[0]
    me = lax.axis_index("mp")
    for m in range(n):
        out[me * n + m] = out_keep[m]
        out[(1 - me) * n + m] = out_recv[m]
        grad[me * n + m] = grad_keep[m]
        grad[(1 - me) * n + m] = grad_recv[m].astype(F32)
    turn[...] = jnp.zeros_like(turn)


EXTRA = 48


def bits_of(count):
    bits = list(range(count.bit_length() - 1))
    cut = len(bits) // 2
    return [(bits[:cut], bits[cut:]), (bits[:cut][::-1], bits[cut:][::-1])]


def piece_of(rows, pieces):
    return -(-rows // (16 * pieces)) * 16


def digit(bits):
    first = lax.axis_index("mp") == 0
    return (lax.axis_index("dp") >> jnp.where(first, bits[0], bits[1])) & 1


def swap_dp(values, bits):
    pairs = []
    for i in range(lax.axis_size("dp")):
        for core in range(2):
            pairs.append((2 * i + core, 2 * (i ^ (1 << bits[core])) + core))
    return lax.ppermute(values, ("dp", "mp"), pairs)


def swap_mp(values):
    return lax.ppermute(values, "mp", [(0, 1), (1, 0)])


def part(index, rows):
    return pl.ds(pl.multiple_of(index * rows, 16), rows)


def start_scatter(pairs, rows, bits, after=()):
    def body(*refs):
        sources, (own, send, values) = refs[: 2 * len(pairs)], refs[-3:]
        at = 0
        for i in range(len(pairs)):
            keep, recv = sources[2 * i], sources[2 * i + 1]
            size = keep.shape[0]
            values[at : at + size] = (keep[...].astype(F32) + recv[...].astype(F32)).astype(BF16)
            at += size
        if at < rows:
            values[at:rows] = jnp.zeros((rows - at, HALF), BF16)
        me = digit(bits)
        own[...] = values[part(me, rows // 2)]
        send[...] = values[part(1 - me, rows // 2)]

    shape = ((rows // 2, HALF), BF16)
    args = [v for pair in pairs for v in pair]
    specs = {len(args) + i: ANYWHERE for i in range(len(after))}
    return call(body, [shape] * 2, *args, *after, scratch=[pltpu.VMEM((rows, HALF), BF16)], specs=specs)


def next_scatter(own, recv, bits, after):
    rows = own.shape[0]

    def body(own_ref, recv_ref, after_ref, out, send, values):
        values[...] = (own_ref[...].astype(F32) + recv_ref[...].astype(F32)).astype(BF16)
        me = digit(bits)
        out[...] = values[part(me, rows // 2)]
        send[...] = values[part(1 - me, rows // 2)]

    shape = ((rows // 2, HALF), BF16)
    scratch = [pltpu.VMEM((rows, HALF), BF16)]
    return call(body, [shape] * 2, own, recv, after, scratch=scratch, specs={2: ANYWHERE})


def end_scatter(own, recv, keep, other, after):
    rows, extra = own.shape[0], keep.shape[0]

    def body(own_ref, recv_ref, keep_ref, other_ref, after_ref, out):
        out[0:rows] = (own_ref[...].astype(F32) + recv_ref[...].astype(F32)).astype(BF16)
        out[rows : rows + 16] = (keep_ref[0:16] + other_ref[0:16]).astype(BF16)
        if extra > 16:
            first = lax.axis_index("mp") == 0
            sides = [join(first, keep_ref[at : at + 4], other_ref[at : at + 4], 0) for at in (16, 24)]
            out[rows + 16 : rows + 32] = jnp.concatenate(sides, axis=0).astype(BF16)
            out[rows + 32 : rows + 48] = keep_ref[32:48].astype(BF16)

    return call(body, [((rows + extra, HALF), BF16)], own, recv, keep, other, after, specs={4: ANYWHERE})[0]


def sum_blocks(own, recv, rows, bits, after):
    rest = own.shape[0] - rows

    def body(own_ref, recv_ref, after_ref, out):
        out[0:rows] = (own_ref[0:rows].astype(F32) + recv_ref[0:rows].astype(F32)).astype(BF16)
        if rest:
            low = digit(bits) == 0
            mine, theirs = own_ref[rows:], recv_ref[rows:]
            out[rows : rows + rest] = jnp.where(low, mine, theirs)
            out[rows + rest :] = jnp.where(low, theirs, mine)

    return call(body, [((rows + 2 * rest, HALF), BF16)], own, recv, after, specs={2: ANYWHERE})[0]


def next_gather(own, recv, bits, after):
    rows = own.shape[0]

    def body(own_ref, recv_ref, after_ref, out):
        me = digit(bits)
        out[part(me, rows)] = own_ref[...]
        out[part(1 - me, rows)] = recv_ref[...]

    return call(body, [((2 * rows, HALF), BF16)], own, recv, after, specs={2: ANYWHERE})[0]


def owner(halving, whole, order, p, q):
    cut, total = len(halving[order]), 0
    for i, bit in enumerate(halving[order]):
        total |= (p >> (cut - 1 - i) & 1) << bit
    for i, bit in enumerate(whole[order]):
        total |= (q >> i & 1) << bit
    return total


def late_result(gains, biases, own, recv, bits, halving, whole, piece):
    pieces, blocks, extra_rows = 1 << len(halving[0]), 1 << len(whole[0]), 16
    full = piece + extra_rows * blocks

    def body(gains_ref, biases_ref, own_ref, recv_ref, out, gains, biases, values, extra):
        me = digit(bits)
        values[part(me, own.shape[0])] = own_ref[...]
        values[part(1 - me, own.shape[0])] = recv_ref[...]
        first = lax.axis_index("mp") == 0
        for p in range(pieces):
            rows = min(piece, 9 * C - p * piece)
            if rows > 0:
                out[p * piece : p * piece + rows] = values[p * full : p * full + rows].astype(F32)
            for q in range(blocks):
                base = p * full + piece + q * extra_rows
                at = jnp.where(first, owner(halving, whole, 0, p, q), owner(halving, whole, 1, p, q))
                extra[at] = values[base : base + extra_rows].astype(F32)
        small = extra[0]
        for i in range(1, pieces * blocks):
            small = small + extra[i]
        gains[0:1] = small[0:1]
        gains[1:3] = gains_ref[...]
        biases[0:1] = small[1:2]
        biases[1:3] = biases_ref[...]

    scratch = [pltpu.VMEM((2 * own.shape[0], HALF), BF16), pltpu.VMEM((pieces * blocks, extra_rows, HALF), F32)]
    outs = [((9 * C, HALF), F32), ((3, HALF), F32), ((3, HALF), F32)]
    return call(body, outs, gains, biases, own, recv, scratch=scratch)


def early_result(own, recv, bits, halving, whole, piece, table, tw_own, tw_recv, after):
    steps, width = table.shape
    padded = -(-steps // HALF) * HALF
    pieces, blocks = 1 << len(halving[0]), 1 << len(whole[0])
    full = piece + EXTRA * blocks

    def body(own_ref, recv_ref, table_ref, tw_own_ref, tw_recv_ref, after_ref, *refs):
        conv2, qkv, out_w, table_grad, tw_grad, gains, biases, conv_b, qkv_b, out_b, time_b = refs[:11]
        values, extra, act_high, act_low = refs[11:]
        me = digit(bits)
        values[part(me, own.shape[0])] = own_ref[...]
        values[part(1 - me, own.shape[0])] = recv_ref[...]
        first = lax.axis_index("mp") == 0

        def rows_of(start, size):
            found = []
            while size:
                at, left = start % piece, piece - start % piece
                now = min(size, left)
                base = start // piece * full + at
                found.append(values[base : base + now].astype(F32))
                start, size = start + now, size - now
            return jnp.concatenate(found, axis=0)

        for t in range(9):
            for h in range(2):
                conv2[t, :, h * HALF : (h + 1) * HALF] = rows_of((2 * t + h) * HALF, HALF)
        for j in range(3):
            qkv[j] = rows_of((9 + j) * C, C)
        for h in range(2):
            out_w[:, h * HALF : (h + 1) * HALF] = rows_of(12 * C + h * HALF, HALF)
        for p in range(pieces):
            for q in range(blocks):
                base = p * full + piece + q * EXTRA
                at = jnp.where(first, owner(halving, whole, 0, p, q), owner(halving, whole, 1, p, q))
                extra[at] = values[base : base + EXTRA].astype(F32)
        small = extra[0, 0:16]
        for i in range(1, pieces * blocks):
            small = small + extra[i, 0:16]
        gains[...] = small[0:2]
        biases[...] = small[2:4]
        conv_b[...] = small[4:6]
        qkv_b[...] = small[6:8]
        out_b[...] = small[8:9]
        maps = 8 * pieces * blocks
        left, right = extra[:, 16:24].reshape(maps, HALF), extra[:, 24:32].reshape(maps, HALF)
        step = (extra[:, 32:40] * 32.0 + extra[:, 40:48]).reshape(maps, HALF)[:, 0:1].astype(jnp.int32)
        mine = jnp.where(first, left, right)
        time_b[...] = col_sum(mine)
        lane = lax.broadcasted_iota(jnp.int32, (maps, padded), 1)
        pick = jnp.where(lane == step, 1.0, 0.0).astype(BF16)
        tw = join(first, tw_own_ref[...], tw_recv_ref[...], 1)
        back = dot_bt(jnp.concatenate([left, right], axis=1).astype(BF16), tw)
        back_high = back.astype(BF16)
        back_low = (back - back_high.astype(F32)).astype(BF16)
        e = table_ref[...]
        sig = sigmoid(e)
        spread = (dot_at(pick, back_high) + dot_at(pick, back_low))[0:steps]
        table_grad[...] = spread * (sig * (1.0 + e * (1.0 - sig)))
        act = e * sig
        high = act.astype(BF16).astype(F32)
        act_high[steps:padded] = jnp.zeros((padded - steps, width), F32)
        act_low[steps:padded] = jnp.zeros((padded - steps, width), F32)
        act_high[0:steps] = high
        act_low[0:steps] = act - high
        by_step = dot_at(mine.astype(BF16), pick)
        step_high = by_step.astype(BF16)
        step_low = (by_step - step_high.astype(F32)).astype(BF16)
        high, low = act_high[...].astype(BF16), act_low[...].astype(BF16)
        tw_grad[...] = (dot(step_high, high) + dot(step_high, low) + dot(step_low, high)).T

    outs = [
        ((9, HALF, C), F32), ((3, C, HALF), F32), ((HALF, C), F32), (table.shape, F32), (tw_own.shape, F32),
        ((2, HALF), F32), ((2, HALF), F32), ((2, HALF), F32), ((2, HALF), F32), ((1, HALF), F32), ((1, HALF), F32),
    ]
    scratch = [
        pltpu.VMEM((2 * own.shape[0], HALF), BF16),
        pltpu.VMEM((pieces * blocks, EXTRA, HALF), F32),
        pltpu.VMEM((padded, width), F32),
        pltpu.VMEM((padded, width), F32),
    ]
    args = (own, recv, table, tw_own, tw_recv, after)
    return call(body, outs, *args, scratch=scratch, specs={5: ANYWHERE}, limit=24)


def on_device(
    maps_in, timesteps, temb_table, norm_gain, norm_bias, conv1_weight, conv_bias, temb_weight,
    temb_bias, conv2_weight, qkv_weight, qkv_bias, out_weight, out_bias, out_grad,
):
    count = lax.axis_size("dp")
    orders = bits_of(count)
    halving, whole = [[order[i] for order in orders] for i in range(2)]
    halving_steps, whole_steps = list(zip(*halving)), list(zip(*whole))
    pieces = 1 << len(halving_steps)
    total = maps_in.shape[0]
    n = total // 2
    maps_shape, half_shape = (n, PIX, C), (n, PIX, HALF)
    weight_shape = ((9, C, C), BF16)

    x_recv = swap_mp(maps_in)
    w1_own = conv1_weight.reshape(9, C, HALF)
    w1_recv = swap_mp(w1_own)
    blank = call(blank_kernel, [((4, HALF), F32)], flops=10**11)[0]
    pk_own = jnp.concatenate(
        [norm_gain, norm_bias, conv_bias, qkv_bias, out_bias[None], temb_bias[None], blank]
    )
    pk_own = call(
        time_kernel, [((PACK + total, HALF), F32)], timesteps, pk_own, temb_table, temb_weight, specs={0: SCALAR},
    )[0]
    pk_recv = swap_mp(pk_own)
    tw_recv = swap_mp(temb_weight)
    w2_own = conv2_weight.reshape(9, HALF, C)
    w2_recv = swap_mp(w2_own)
    qw_own = jnp.transpose(qkv_weight, (1, 0, 2))
    qw_recv = swap_mp(qw_own)
    ow_recv = swap_mp(out_weight)
    g_recv = swap_mp(out_grad)

    hid, act1_t, act2_t, stat0, stat1, prm, w1_full, *win2 = call(
        first_kernel,
        [
            (maps_shape, F32), ((C, n * PIX), BF16), ((C, n * PIX), BF16),
            ((2 * n, C), F32), ((2 * n, C), F32), ((PACK, C), F32), weight_shape,
        ] + [WIN] * n,
        maps_in, x_recv, w1_own, w1_recv, pk_own, pk_recv,
        scratch=[pltpu.VMEM(*WIN)] * n,
        flops=10**11,
    )
    tile_f32, tile_low = pltpu.VMEM((PIX, C), F32), pltpu.VMEM((PIX, C), BF16)
    three_low = pltpu.VMEM((3, PIX, C), BF16)
    out_keep, out_send, dmid, wg_keep, wg_send, sums3, w2_full, *win3 = call(
        middle_kernel,
        [
            (half_shape, BF16), (half_shape, BF16), (maps_shape, F32),
            ((4 * C, HALF), BF16), ((4 * C, HALF), BF16), ((8, C), F32), weight_shape,
        ] + [WIN] * n,
        maps_in, x_recv, w2_own, w2_recv, prm, out_grad, g_recv, qw_own, qw_recv, out_weight, ow_recv, *win2,
        scratch=[pltpu.VMEM((3, C, C), BF16), tile_low]
        + [tile_f32] * (3 * n) + [tile_low] * n + [three_low] * n + [tile_low] * (3 * n) + [three_low] * n,
    )
    wg_recv = swap_mp(wg_send)
    early_pairs = []
    for taps in TAPS:
        shape = ((len(taps) * C, HALF), BF16)
        keep, send = call(conv2_grad_kernel(taps), [shape, shape], act2_t, *win3)
        early_pairs.append((keep, swap_mp(send)))
    early_pairs.append((wg_keep, wg_recv))
    early_piece, late_piece = piece_of(13 * C, pieces), piece_of(9 * C, pieces)
    early, early_send = start_scatter(early_pairs, early_piece * pieces, halving_steps[0])
    early_recv = swap_dp(early_send, halving_steps[0])
    rows_keep, rows_send, *win4 = call(
        hidden_back_kernel,
        [((EXTRA, HALF), F32), ((32, HALF), F32)] + [WIN] * n,
        timesteps, early, hid, stat1, w2_full, prm, sums3, *win3,
        specs={0: SCALAR, 1: ANYWHERE},
    )
    rows_recv = swap_mp(rows_send)
    late_pairs = []
    for taps in TAPS:
        shape = ((len(taps) * C, HALF), BF16)
        keep, send = call(conv1_grad_kernel(taps), [shape, shape], act1_t, *win4)
        late_pairs.append((keep, swap_mp(send)))
    late, late_send = start_scatter(late_pairs, late_piece * pieces, halving_steps[0])
    late_recv = swap_dp(late_send, halving_steps[0])

    turn = late
    for i, bits in enumerate(halving_steps[1:]):
        early, early_send = next_scatter(early, early_recv, bits, turn)
        early_recv = swap_dp(early_send, bits)
        turn = early
        if i == 0:
            mg_keep, mg_send, last_keep, last_send = call(
                input_back_kernel,
                [(half_shape, F32), (half_shape, BF16), ((16, HALF), F32), ((16, HALF), F32)],
                turn, maps_in, x_recv, stat0, w1_full, prm, dmid, *win4,
                specs={0: ANYWHERE},
            )
            last_recv = swap_mp(last_send)
            out_recv, mg_recv = swap_mp(out_send), swap_mp(mg_send)
            turn = last_keep
        late, late_send = next_scatter(late, late_recv, bits, turn)
        late_recv = swap_dp(late_send, bits)
        turn = late
    early = end_scatter(early, early_recv, rows_keep, rows_recv, turn)
    early_recv = swap_dp(early, whole_steps[0])
    maps_out, maps_grad, turn = call(
        maps_kernel, [(maps_in.shape, BF16), (maps_in.shape, F32), ((8, HALF), F32)],
        early, out_keep, out_recv, mg_keep, mg_recv,
        specs={0: ANYWHERE},
    )
    late = end_scatter(late, late_recv, last_keep, last_recv, turn)
    late_recv = swap_dp(late, whole_steps[0])
    gathers = halving_steps[::-1]
    following = whole_steps[1:] + gathers[:1]
    for bits, next_bits in zip(whole_steps, following):
        early = sum_blocks(early, early_recv, early_piece, bits, late)
        early_recv = swap_dp(early, next_bits)
        late = sum_blocks(late, late_recv, late_piece, bits, early)
        late_recv = swap_dp(late, next_bits)
    for bits, next_bits in zip(gathers[:-1], gathers[1:]):
        early = next_gather(early, early_recv, bits, late)
        early_recv = swap_dp(early, next_bits)
        late = next_gather(late, late_recv, bits, early)
        late_recv = swap_dp(late, next_bits)
    bits = gathers[-1]
    conv2, qkv, out_w, table_grad, tw_grad, gains, biases, conv_b, qkv_b, out_b, time_b = early_result(
        early, early_recv, bits, halving, whole, early_piece, temb_table, temb_weight, tw_recv, late,
    )
    conv1, gains, biases = late_result(
        gains, biases, late, late_recv, bits, halving, whole, late_piece,
    )
    return (
        maps_out, maps_grad, table_grad, gains, biases, conv1.reshape(3, 3, C, HALF), conv_b, tw_grad,
        time_b.reshape(HALF), conv2.reshape(3, 3, HALF, C), jnp.transpose(qkv, (1, 0, 2)), qkv_b, out_w,
        out_b.reshape(HALF),
    )


def solution(mesh):
    args = (
        P("dp", None, "mp"), P("dp"), P(), P(None, "mp"), P(None, "mp"), P(None, None, None, "mp"),
        P(None, "mp"), P(None, "mp"), P("mp"), P(None, None, "mp", None), P(None, None, "mp"),
        P(None, "mp"), P("mp", None), P("mp"), P("dp", None, "mp"),
    )
    outs = (
        P("dp", None, "mp"), P("dp", None, "mp"), P(), P(None, "mp"), P(None, "mp"),
        P(None, None, None, "mp"), P(None, "mp"), P(None, "mp"), P("mp"), P(None, None, "mp", None),
        P(None, None, "mp"), P(None, "mp"), P("mp", None), P("mp"),
    )
    return jax.shard_map(on_device, mesh=mesh, in_specs=args, out_specs=outs, check_vma=False)
```

```python
import jax
import jax.numpy as jnp
from jax import lax
from jax.experimental import pallas as pl
from jax.experimental.pallas import tpu as pltpu
from jax.sharding import PartitionSpec as P

C = 256
HALF = 128
SIDE = 16
PIX = 256
GROUP = 8
EPS = 1e-06
F32 = jnp.float32
BF16 = jnp.bfloat16
WHOLE = pl.BlockSpec(memory_space=pltpu.VMEM)
SCALAR = pl.BlockSpec(memory_space=pltpu.SMEM)
ANYWHERE = pl.BlockSpec(memory_space=pl.ANY)
IN_HBM = pl.BlockSpec(memory_space=pltpu.HBM)


def call(body, outs, *args, scratch=(), specs=None, limit=16, flops=1):
    specs = specs or {}
    return pl.pallas_call(
        body,
        out_shape=tuple(jax.ShapeDtypeStruct(s, d) for s, d in outs),
        in_specs=[specs.get(i, WHOLE) for i in range(len(args))],
        out_specs=tuple(WHOLE for _ in outs),
        scratch_shapes=list(scratch),
        compiler_params=pltpu.CompilerParams(vmem_limit_bytes=limit << 20),
        cost_estimate=pl.CostEstimate(flops=flops, bytes_accessed=0, transcendentals=0),
    )(*args)


def dot(a, b):
    return jnp.dot(a, b, preferred_element_type=F32)


def dot_bt(a, b):
    return lax.dot_general(a, b, (((1,), (1,)), ((), ())), preferred_element_type=F32)


def dot_at(a, b):
    return lax.dot_general(a, b, (((0,), (0,)), ((), ())), preferred_element_type=F32)


def join(first, own, recv, axis):
    low = jnp.where(first, own, recv)
    high = jnp.where(first, recv, own)
    return jnp.concatenate([low, high], axis=axis)


def split(first, values, axis=1):
    low, high = jnp.split(values, 2, axis)
    return jnp.where(first, low, high), jnp.where(first, high, low)


def group_merge(mean, square, count):
    lane = lax.broadcasted_iota(jnp.int32, mean.shape, 1)
    width = mean.shape[1]

    def partner(rows, step):
        up = pltpu.roll(rows, width - step, 1)
        down = pltpu.roll(rows, step, 1)
        return jnp.where((lane & step) == 0, up, down)

    for step in (1, 2, 4):
        other = partner(mean, step)
        gap = mean - other
        square = square + partner(square, step) + gap * gap * (0.5 * count * step)
        mean = 0.5 * (mean + other)
    return mean, square


def group_sum(rows):
    lane = lax.broadcasted_iota(jnp.int32, rows.shape, 1)
    width = rows.shape[1]
    for step in (1, 2, 4):
        up = pltpu.roll(rows, width - step, 1)
        down = pltpu.roll(rows, step, 1)
        rows = rows + jnp.where((lane & step) == 0, up, down)
    return rows


def col_sum(values):
    return jnp.sum(values, axis=0, keepdims=True)


def norm_stats(values):
    mean = col_sum(values) * (1.0 / PIX)
    square = col_sum((values - mean) ** 2)
    mean, square = group_merge(mean, square, PIX)
    return mean, lax.rsqrt(square * (1.0 / (PIX * GROUP)) + EPS)


def all_stats(maps):
    means = [col_sum(v) * (1.0 / PIX) for v in maps]
    squares = [col_sum((v - mean) ** 2) for v, mean in zip(maps, means)]
    mean, square = group_merge(jnp.concatenate(means, axis=0), jnp.concatenate(squares, axis=0), PIX)
    return mean, lax.rsqrt(square * (1.0 / (PIX * GROUP)) + EPS)


def norm_back(grad, unit, gain, rstd):
    plain = col_sum(grad)
    scaled = col_sum(grad * unit)
    both = group_sum(jnp.concatenate([plain * gain, scaled * gain], axis=0)) * (1.0 / (PIX * GROUP))
    inner = grad * gain - both[0:1] - unit * both[1:2]
    return inner * rstd, scaled, plain


def sigmoid(v):
    return 1.0 / (1.0 + jnp.exp(-v))


def put_windows(win, values):
    col = lax.broadcasted_iota(jnp.int32, (PIX, 1), 0) & (SIDE - 1)
    before = jnp.where(col == 0, 0.0, pltpu.roll(values, 1, 0))
    after = jnp.where(col == SIDE - 1, 0.0, pltpu.roll(values, PIX - 1, 0))
    blank = jnp.zeros((SIDE, C), BF16)
    for c, shifted in enumerate((before, values, after)):
        win[c, 0:SIDE, :] = blank
        win[c, SIDE + PIX : 2 * SIDE + PIX, :] = blank
        win[c, SIDE : SIDE + PIX, :] = shifted.astype(BF16)


def window(win, r, c):
    return win[c, SIDE * r : SIDE * r + PIX, :]


def conv_forward(win, w_ref):
    total = None
    for r in range(3):
        for c in range(3):
            part = dot(window(win, r, c), w_ref[3 * r + c])
            total = part if total is None else total + part
    return total


def conv_transposed(win, w_ref):
    total = None
    for r in range(3):
        for c in range(3):
            part = dot_bt(window(win, 2 - r, 2 - c), w_ref[3 * r + c])
            total = part if total is None else total + part
    return total


WIN = ((3, PIX + 2 * SIDE, C), BF16)

GAIN, BIAS, CONV_B, QKV_B, OUT_B, TIME_B, PACK = 0, 3, 6, 8, 10, 11, 16


def blank_kernel(result):
    result[...] = jnp.zeros_like(result)


def time_kernel(steps, pk, table, tw, w1, result):
    total = result.shape[0] - PACK
    result[0:PACK] = pk[...]
    rows = jnp.concatenate([table[pl.ds(steps[i], 1)] for i in range(total)], axis=0)
    e = rows * sigmoid(rows)
    e_high = e.astype(BF16)
    e_low = (e - e_high.astype(F32)).astype(BF16)
    shift = pk[TIME_B : TIME_B + 1] + pk[CONV_B : CONV_B + 1]
    result[PACK : PACK + total] = dot(e_high, tw[...]) + dot(e_low, tw[...]) + shift


def first_kernel(x_own, x_recv, w_own, w_recv, pk_own, pk_recv, *rest):
    n = x_own.shape[0] // 2
    hid, act_t, act2_t, stat0, stat1, prm_out, wfull = rest[:7]
    win2, (*wins, w_here, w_sem) = rest[7 : 7 + n], rest[7 + n :]
    me = lax.axis_index("mp")
    first = me == 0
    w_copy = pltpu.make_async_copy(w_recv, w_here, w_sem)
    w_copy.start()
    pk = join(first, pk_own[0:PACK], pk_recv[0:PACK], 1)
    prm_out[...] = pk
    xs = [join(first, x_own[me * n + m], x_recv[me * n + m], 1).astype(F32) for m in range(n)]
    mean, rstd = all_stats(xs)
    stat0[0:n] = mean
    stat0[n : 2 * n] = rstd
    scale = rstd * pk[GAIN : GAIN + 1]
    shift = pk[BIAS : BIAS + 1] - mean * scale
    for m in range(n):
        u = xs[m] * scale[m : m + 1] + shift[m : m + 1]
        a = u * sigmoid(u)
        act_t[:, m * PIX : (m + 1) * PIX] = a.astype(BF16).T
        put_windows(wins[m], a)
    w_copy.wait()
    for t in range(9):
        wfull[t] = join(first, w_own[t], w_here[t], 1)
    both = join(first, pk_own[PACK:], pk_recv[PACK:], 1)
    time_row = jnp.where(first, both[0:n], both[n : 2 * n])
    for m in range(n):
        h = conv_forward(wins[m], wfull) + time_row[m : m + 1]
        hid[m] = h
        mean, rstd = norm_stats(h)
        stat1[m : m + 1] = mean
        stat1[n + m : n + m + 1] = rstd
        u = (h - mean) * (rstd * pk[GAIN + 1 : GAIN + 2]) + pk[BIAS + 1 : BIAS + 2]
        a = u * sigmoid(u)
        act2_t[:, m * PIX : (m + 1) * PIX] = a.astype(BF16).T
        put_windows(win2[m], a)


def middle_kernel(x_own, x_recv, w_own, w_recv, prm, g_own, g_recv, qw_own, qw_recv, ow_own, ow_recv, *rest):
    n = g_own.shape[0] // 2
    win2, rest = rest[:n], rest[n:]
    out_keep, out_send, dmid, wg_keep, wg_send, sums, wfull = rest[:7]
    win3, rest = rest[7 : 7 + n], rest[7 + n :]
    qw, ow, rest = rest[0], rest[1], rest[2:]
    mids, units, probs = rest[:n], rest[n : 2 * n], rest[2 * n : 3 * n]
    thirds, qkvs, lows, douts, atts, grads = [rest[(3 + i) * n : (4 + i) * n] for i in range(6)]
    me = lax.axis_index("mp")
    first = me == 0
    scale = 1.0 / 16.0
    for t in range(9):
        wfull[t] = join(first, w_own[t], w_recv[t], 0)
    for j in range(3):
        qw[j] = join(first, qw_own[j], qw_recv[j], 1)
    ow[...] = join(first, ow_own[...], ow_recv[...], 0)
    rstds = []
    for m in range(n):
        at = me * n + m
        x = join(first, x_own[at], x_recv[at], 1).astype(F32)
        mid = x + conv_forward(win2[m], wfull) + prm[CONV_B + 1 : CONV_B + 2]
        mids[m][...] = mid
        mean, rstd = norm_stats(mid)
        rstds.append(rstd)
        unit = (mid - mean) * rstd
        units[m][...] = unit
        thirds[m][...] = (unit * prm[GAIN + 2 : GAIN + 3] + prm[BIAS + 2 : BIAS + 3]).astype(BF16)
    for m in range(n):
        a3 = thirds[m][...]
        qkvs[m][0] = (dot(a3, qw[0]) + prm[QKV_B : QKV_B + 1]).astype(BF16)
        qkvs[m][1] = dot(a3, qw[1]).astype(BF16)
        qkvs[m][2] = (dot(a3, qw[2]) + prm[QKV_B + 1 : QKV_B + 2]).astype(BF16)
    for m in range(n):
        s = dot_bt(qkvs[m][0], qkvs[m][1]) * scale
        e = jnp.exp(s - jnp.max(s, axis=1, keepdims=True))
        p = e * (1.0 / jnp.sum(e, axis=1, keepdims=True))
        probs[m][...] = p
        lows[m][...] = p.astype(BF16)
    for m in range(n):
        gb = join(first, g_own[me * n + m], g_recv[me * n + m], 1)
        douts[m][...] = dot_bt(gb, ow[...]).astype(BF16)
    for m in range(n):
        a = dot(lows[m][...], qkvs[m][2]).astype(BF16)
        atts[m][...] = a
        result = mids[m][...] + dot(a, ow[...]) + prm[OUT_B : OUT_B + 1]
        keep, send = split(first, result.astype(BF16))
        out_keep[m] = keep
        out_send[m] = send
    for m in range(n):
        p = probs[m][...]
        dp = dot_bt(douts[m][...], qkvs[m][2])
        ds = (p * (dp - jnp.sum(p * dp, axis=1, keepdims=True))).astype(BF16)
        grads[m][2] = dot_at(lows[m][...], douts[m][...]).astype(BF16)
        lows[m][...] = ds
    for m in range(n):
        ds = lows[m][...]
        grads[m][0] = (dot(ds, qkvs[m][1]) * scale).astype(BF16)
        grads[m][1] = (dot_at(ds, qkvs[m][0]) * scale).astype(BF16)
    gains, biases, mid_bias, out_bias = [], [], [], []
    for m in range(n):
        grad = dot_bt(grads[m][0], qw[0]) + dot_bt(grads[m][1], qw[1]) + dot_bt(grads[m][2], qw[2])
        back, gain_grad, bias_grad = norm_back(grad, units[m][...], prm[GAIN + 2 : GAIN + 3], rstds[m])
        gains.append(gain_grad)
        biases.append(bias_grad)
        g = join(first, g_own[me * n + m], g_recv[me * n + m], 1).astype(F32)
        out_bias.append(col_sum(g))
        d = back + g
        dmid[m] = d
        mid_bias.append(col_sum(d))
        put_windows(win3[m], d)
    third_t = jnp.concatenate([thirds[m][...].T for m in range(n)], axis=1)
    for j in range(3):
        d = jnp.concatenate([grads[m][j] for m in range(n)], axis=0)
        keep, send = split(first, dot(third_t, d).astype(BF16))
        wg_keep[j * C : (j + 1) * C] = keep
        wg_send[j * C : (j + 1) * C] = send
    att_t = jnp.concatenate([atts[m][...].T for m in range(n)], axis=1)
    g_all = jnp.concatenate([join(first, g_own[me * n + m], g_recv[me * n + m], 1) for m in range(n)], axis=0)
    keep, send = split(first, dot(att_t, g_all).astype(BF16), 0)
    for h in range(2):
        lanes, rows = slice(h * HALF, (h + 1) * HALF), slice(3 * C + h * HALF, 3 * C + (h + 1) * HALF)
        wg_keep[rows] = keep[:, lanes]
        wg_send[rows] = send[:, lanes]
    sums[0:1] = sum(gains)
    sums[1:2] = sum(biases)
    sums[2:3] = sum(mid_bias)
    sums[3:4] = sum(col_sum(grads[m][0].astype(F32)) for m in range(n))
    sums[4:5] = sum(col_sum(grads[m][2].astype(F32)) for m in range(n))
    sums[5:6] = sum(out_bias)
    sums[6:8] = jnp.zeros((2, C), F32)


CONV1_TAPS = (range(0, 6), range(6, 9))
CONV2_TAPS = (range(0, 5), range(5, 9))


def conv2_grad_kernel(taps):
    def body(act_t, *rest):
        win, (keep, send) = rest[: act_t.shape[1] // PIX], rest[-2:]
        first = lax.axis_index("mp") == 0
        for i, t in enumerate(taps):
            shifted = jnp.concatenate([window(w, 2 - t // 3, 2 - t % 3) for w in win], axis=0)
            g_keep, g_send = split(first, dot(act_t[...], shifted).astype(BF16), 0)
            for h in range(2):
                lanes = slice(h * HALF, (h + 1) * HALF)
                rows = slice((2 * i + h) * HALF, (2 * i + h + 1) * HALF)
                keep[rows] = g_keep[:, lanes]
                send[rows] = g_send[:, lanes]

    return body


def hidden_back_kernel(steps, hid, stat, wfull, prm, *rest):
    n = hid.shape[0]
    win3, (sums, time_rows), win4 = rest[:n], rest[n : n + 2], rest[n + 2 :]
    gain, bias = prm[GAIN + 1 : GAIN + 2], prm[BIAS + 1 : BIAS + 2]
    gains, biases, times = [], [], []
    for m in range(n):
        rstd = stat[n + m : n + m + 1]
        unit = (hid[m] - stat[m : m + 1]) * rstd
        u = unit * gain + bias
        sig = sigmoid(u)
        slope = sig * (1.0 + u * (1.0 - sig))
        grad = conv_transposed(win3[m], wfull) * slope
        back, gain_grad, bias_grad = norm_back(grad, unit, gain, rstd)
        gains.append(gain_grad)
        biases.append(bias_grad)
        low = back.astype(BF16).astype(F32)
        times.append(col_sum(low))
        put_windows(win4[m], low)
    rows, blank = jnp.concatenate(times, axis=0), jnp.zeros((n, HALF), F32)
    time_rows[0:16] = jnp.concatenate([rows[:, :HALF], blank, rows[:, HALF:], blank], axis=0).astype(BF16)
    lane = lax.broadcasted_iota(jnp.int32, (16, HALF), 1)
    step_row = jnp.zeros((16, HALF), jnp.int32)
    for i in range(2 * n):
        step_row = jnp.where(lane == i, steps[i] >> 5, jnp.where(lane == 2 * n + i, steps[i] & 31, step_row))
    time_rows[16:32] = step_row.astype(F32).astype(BF16)
    sums[0:1] = sum(gains)
    sums[1:2] = sum(biases)
    sums[2:3] = sum(times)
    sums[3:8] = jnp.zeros((5, C), F32)


def conv1_grad_kernel(taps):
    def body(act_t, *rest):
        win, others, (keep, send) = rest[: act_t.shape[1] // PIX], rest[act_t.shape[1] // PIX : -2], rest[-2:]
        first = lax.axis_index("mp") == 0
        for i, t in enumerate(taps):
            shifted = jnp.concatenate([window(w, 2 - t // 3, 2 - t % 3) for w in win], axis=0)
            g_keep, g_send = split(first, dot(act_t[...], shifted).astype(BF16))
            keep[i * C : (i + 1) * C] = g_keep
            send[i * C : (i + 1) * C] = g_send
        if others:
            rows = len(taps) * C
            keep[rows:] = others[0][...]
            send[rows:] = others[0][...]

    return body


def input_back_kernel(after, x_own, x_recv, stat, wfull, prm, dmid, sums2, sums3, *rest):
    n = dmid.shape[0]
    win4, (keep, send, rows_keep, rows_send) = rest[:n], rest[n:]
    me = lax.axis_index("mp")
    first = me == 0
    gain, bias = prm[GAIN : GAIN + 1], prm[BIAS : BIAS + 1]
    gains, biases = [], []
    for m in range(n):
        at = me * n + m
        rstd = stat[n + m : n + m + 1]
        x = join(first, x_own[at], x_recv[at], 1).astype(F32)
        unit = (x - stat[m : m + 1]) * rstd
        u = unit * gain + bias
        sig = sigmoid(u)
        slope = sig * (1.0 + u * (1.0 - sig))
        grad = conv_transposed(win4[m], wfull) * slope
        back, gain_grad, bias_grad = norm_back(grad, unit, gain, rstd)
        gains.append(gain_grad)
        biases.append(bias_grad)
        d_keep, d_send = split(first, back + dmid[m])
        keep[m] = d_keep
        send[m] = d_send.astype(BF16)
    small = [
        sum(gains), sums2[0:1], sums3[0:1], sum(biases), sums2[1:2], sums3[1:2], sums2[2:3], sums3[2:6],
        jnp.zeros((5, C), F32),
    ]
    rows_keep[...], rows_send[...] = split(first, jnp.concatenate(small, axis=0))


def maps_kernel(after, out_keep, out_recv, grad_keep, grad_recv, out, grad, turn):
    n = out_keep.shape[0]
    me = lax.axis_index("mp")
    for m in range(n):
        out[me * n + m] = out_keep[m]
        out[(1 - me) * n + m] = out_recv[m]
        grad[me * n + m] = grad_keep[m]
        grad[(1 - me) * n + m] = grad_recv[m].astype(F32)
    turn[...] = jnp.zeros_like(turn)


EXTRA, SUMS = 32, 16


def bits_of(count):
    bits = list(range(count.bit_length() - 1))
    cut = len(bits) // 2
    low, high = bits[:cut], bits[cut:]
    return [[(high, low), (high[::-1], low)], [(low, high), (low[::-1], high[::-1])]]


def digit(bits):
    first = lax.axis_index("mp") == 0
    return (lax.axis_index("dp") >> jnp.where(first, bits[0], bits[1])) & 1


def swap_dp(values, bits):
    pairs = []
    for i in range(lax.axis_size("dp")):
        for core in range(2):
            pairs.append((2 * i + core, 2 * (i ^ (1 << bits[core])) + core))
    return lax.ppermute(values, ("dp", "mp"), pairs)


def swap_mp(values):
    return lax.ppermute(values, "mp", [(0, 1), (1, 0)])


def part(index, rows):
    return pl.ds(pl.multiple_of(index * rows, 16), rows)


def added(a, b):
    return (a.astype(F32) + b.astype(F32)).astype(BF16)


def start_exchanges(chains, groups):
    rows = [chain.rows for chain in chains]

    def body(*refs):
        refs = list(refs)
        sources = [[(refs.pop(0), refs.pop(0)) for _ in pairs] for pairs in groups]
        outs, buffers = refs[:4], refs[4:]
        first = lax.axis_index("mp") == 0
        time_own, time_other = [ref[ref.shape[0] - EXTRA :].astype(F32) for ref in sources[0][0]]
        sides = [join(first, time_own[at : at + 4], time_other[at : at + 4], 0) for at in (0, 8)]
        extra = jnp.concatenate(sides + [time_own[16:32]], axis=0).astype(BF16)
        for g, values in enumerate(buffers):
            end = 0
            for i, (keep, recv) in enumerate(sources[g]):
                size = keep.shape[0] - (EXTRA if g == 0 and i == 0 else 0)
                values[end : end + size] = added(keep[0:size], recv[0:size])
                end += size
            if end < rows[g]:
                values[end : rows[g]] = jnp.zeros((rows[g] - end, HALF), BF16)
            me, half = digit(chains[g].steps[0]), rows[g] // 2
            for index, ref in zip((me, 1 - me), outs[2 * g : 2 * g + 2]):
                ref[0:half] = values[part(index, half)]
                if g == 0:
                    ref[half:] = extra

    outs = [((r // 2 + (EXTRA if g == 0 else 0), HALF), BF16) for g, r in enumerate(rows) for _ in range(2)]
    args = [v for pairs in groups for pair in pairs for v in pair]
    results = call(body, outs, *args, scratch=[pltpu.VMEM((r, HALF), BF16) for r in rows])
    for g, chain in enumerate(chains):
        chain.own = results[2 * g]
        chain.recv = swap_dp(results[2 * g + 1], chain.steps[0])
        chain.rows //= 2


class Exchange:
    def __init__(self, order, pairs, extra):
        halving, whole = [list(zip(*[core[i] for core in order])) for i in range(2)]
        self.cut, self.whole = len(halving), len(halving) + len(whole)
        self.steps = halving + whole + halving[::-1]
        self.bits = [[core[0] + core[1] for core in order][c] for c in range(2)]
        self.at = 0
        pieces = 1 << self.cut
        self.piece = -(-(sum(keep.shape[0] for keep, _ in pairs) - extra) // (16 * pieces)) * 16
        self.rows = self.piece * pieces

    def step(self, after, small=()):
        bits, following = self.steps[self.at : self.at + 2]
        self.at += 1
        head, rest = self.rows, self.own.shape[0] - self.rows
        halve, ends, last = self.at < self.cut, self.at == self.cut, self.at == self.whole
        gather = self.at > self.whole
        with_small = SUMS if small and ends else 0

        def body(own, recv, after_ref, *refs):
            small_refs, outs = refs[: len(small) if ends else 0], refs[len(small) if ends else 0 :]
            me = digit(bits)
            out = outs[0]
            if gather:
                out[part(me, head)] = own[...]
                out[part(1 - me, head)] = recv[...]
                return
            tails = []
            if halve:
                values, send = outs[-1], outs[1]
                values[...] = added(own[0:head], recv[0:head])
                index = digit(following)
                out[0 : head // 2] = values[part(index, head // 2)]
                send[0 : head // 2] = values[part(1 - index, head // 2)]
                tails = [(out, head // 2), (send, head // 2)]
            else:
                out[0:head] = added(own[0:head], recv[0:head])
                if with_small:
                    out[head : head + SUMS] = (small_refs[0][...] + small_refs[1][...]).astype(BF16)
                tails = [(outs[-1], 0 if last else head + with_small)]
            if rest:
                low = me == 0
                mine, theirs = own[head:], recv[head:]
                for ref, at in tails:
                    ref[at : at + rest] = jnp.where(low, mine, theirs)
                    ref[at + rest : at + 2 * rest] = jnp.where(low, theirs, mine)

        def shape(rows):
            return ((rows, HALF), BF16)

        if gather:
            outs, self.rows = [shape(2 * head)], 2 * head
        elif halve:
            outs, self.rows = [shape(head // 2 + 2 * rest)] * 2, head // 2
        else:
            self.rows = head + with_small
            outs = [shape(self.rows), shape(2 * rest)] if last and rest else [shape(self.rows + 2 * rest)]
        args = (self.own, self.recv, after) + (tuple(small) if ends else ())
        scratch = [pltpu.VMEM((head, HALF), BF16)] if halve else []
        results = call(body, outs, *args, scratch=scratch, specs={2: ANYWHERE})
        self.own = results[0]
        if last and rest:
            self.gathered = results[1]
        self.recv = swap_dp(results[1] if halve else self.own, following)


def time_results(gathered, order, table, tw_own, tw_recv, after):
    steps, width = table.shape
    padded = -(-steps // HALF) * HALF
    blocks = gathered.shape[0] // EXTRA
    maps = 8 * blocks

    def owner(core, block):
        return sum((block >> i & 1) << bit for i, bit in enumerate(order[core]))

    def body(rows_ref, table_ref, tw_own_ref, tw_recv_ref, after_ref, *refs):
        table_grad, tw_grad, time_b, turn, extra, act_high, act_low = refs
        first = lax.axis_index("mp") == 0
        for block in range(blocks):
            at = jnp.where(first, owner(0, block), owner(1, block))
            extra[at] = rows_ref[block * EXTRA : (block + 1) * EXTRA].astype(F32)
        left, right = extra[:, 0:8].reshape(maps, HALF), extra[:, 8:16].reshape(maps, HALF)
        step_rows = extra[:, 16:24].reshape(maps, HALF)
        lane = lax.broadcasted_iota(jnp.int32, (maps, HALF), 1)
        row = lax.broadcasted_iota(jnp.int32, (maps, HALF), 0) & 7
        weight = jnp.where(lane == row, 32.0, jnp.where(lane == row + 8, 1.0, 0.0))
        step = jnp.sum(step_rows * weight, axis=1, keepdims=True).astype(jnp.int32)
        mine = jnp.where(first, left, right)
        time_b[...] = col_sum(mine)
        lane = lax.broadcasted_iota(jnp.int32, (maps, padded), 1)
        pick = jnp.where(lane == step, 1.0, 0.0).astype(BF16)
        tw = join(first, tw_own_ref[...], tw_recv_ref[...], 1)
        back = dot_bt(jnp.concatenate([left, right], axis=1).astype(BF16), tw)
        back_high = back.astype(BF16)
        back_low = (back - back_high.astype(F32)).astype(BF16)
        e = table_ref[...]
        sig = sigmoid(e)
        spread = (dot_at(pick, back_high) + dot_at(pick, back_low))[0:steps]
        table_grad[...] = spread * (sig * (1.0 + e * (1.0 - sig)))
        act = e * sig
        high = act.astype(BF16).astype(F32)
        act_high[steps:padded] = jnp.zeros((padded - steps, width), F32)
        act_low[steps:padded] = jnp.zeros((padded - steps, width), F32)
        act_high[0:steps] = high
        act_low[0:steps] = act - high
        by_step = dot_at(mine.astype(BF16), pick)
        step_high = by_step.astype(BF16)
        step_low = (by_step - step_high.astype(F32)).astype(BF16)
        high, low = act_high[...].astype(BF16), act_low[...].astype(BF16)
        tw_grad[...] = (dot(step_high, high) + dot(step_high, low) + dot(step_low, high)).T
        turn[...] = jnp.zeros_like(turn)

    outs = [(table.shape, F32), (tw_own.shape, F32), ((1, HALF), F32), ((8, HALF), F32)]
    scratch = [
        pltpu.VMEM((blocks, EXTRA, HALF), F32),
        pltpu.VMEM((padded, width), F32),
        pltpu.VMEM((padded, width), F32),
    ]
    args = (gathered, table, tw_own, tw_recv, after)
    return call(body, outs, *args, scratch=scratch, specs={4: ANYWHERE}, limit=24)


def weight_results(chains, split_at):
    def body(own1, recv1, own2, recv2, *refs):
        conv1, conv2, qkv, out_w, gains, biases, conv_b, qkv_b, out_b = refs[:9]
        reads = []
        for chain, own, recv, values in zip(chains, (own1, own2), (recv1, recv2), refs[9:]):
            me, rows = digit(chain.steps[-1]), own.shape[0]
            values[part(me, rows)] = own[...]
            values[part(1 - me, rows)] = recv[...]
            reads.append(row_reader(values, chain.piece, values.shape[0] >> chain.cut))
        conv1[0:split_at] = reads[0](0, split_at)
        conv1[split_at : 9 * C] = reads[1](0, 9 * C - split_at)
        at = 9 * C - split_at
        for t in range(9):
            for h in range(2):
                conv2[t, :, h * HALF : (h + 1) * HALF] = reads[1](at + (2 * t + h) * HALF, HALF)
        at += 9 * C
        for j in range(3):
            qkv[j] = reads[1](at + j * C, C)
        for h in range(2):
            out_w[:, h * HALF : (h + 1) * HALF] = reads[1](at + 3 * C + h * HALF, HALF)
        values, chain = refs[9], chains[0]
        full = values.shape[0] >> chain.cut
        small = None
        for p in range(1 << chain.cut):
            base = p * full + chain.piece
            block = values[base : base + SUMS].astype(F32)
            small = block if small is None else small + block
        gains[...] = small[0:3]
        biases[...] = small[3:6]
        conv_b[...] = small[6:8]
        qkv_b[...] = small[8:10]
        out_b[...] = small[10:11]

    outs = [
        ((9 * C, HALF), F32), ((9, HALF, C), F32), ((3, C, HALF), F32), ((HALF, C), F32),
        ((3, HALF), F32), ((3, HALF), F32), ((2, HALF), F32), ((2, HALF), F32), ((1, HALF), F32),
    ]
    scratch = [pltpu.VMEM((2 * chain.own.shape[0], HALF), BF16) for chain in chains]
    args = [v for chain in chains for v in (chain.own, chain.recv)]
    return call(body, outs, *args, scratch=scratch)


def row_reader(values, piece, full):
    def read(start, size):
        found = []
        while size:
            at, left = start % piece, piece - start % piece
            now = min(size, left)
            base = start // piece * full + at
            found.append(values[base : base + now].astype(F32))
            start, size = start + now, size - now
        return jnp.concatenate(found, axis=0)

    return read


def on_device(
    maps_in, timesteps, temb_table, norm_gain, norm_bias, conv1_weight, conv_bias, temb_weight,
    temb_bias, conv2_weight, qkv_weight, qkv_bias, out_weight, out_bias, out_grad,
):
    count = lax.axis_size("dp")
    orders = bits_of(count)
    total = maps_in.shape[0]
    n = total // 2
    maps_shape, half_shape = (n, PIX, C), (n, PIX, HALF)
    weight_shape = ((9, C, C), BF16)

    x_recv = swap_mp(maps_in)
    w1_own = conv1_weight.reshape(9, C, HALF)
    w1_recv = swap_mp(w1_own)
    blank = call(blank_kernel, [((4, HALF), F32)], flops=10**11)[0]
    pk_own = jnp.concatenate(
        [norm_gain, norm_bias, conv_bias, qkv_bias, out_bias[None], temb_bias[None], blank]
    )
    pk_own = call(
        time_kernel, [((PACK + total, HALF), F32)], timesteps, pk_own, temb_table, temb_weight, w1_own,
        specs={0: SCALAR},
    )[0]
    pk_recv = swap_mp(pk_own)
    tw_recv = swap_mp(temb_weight)
    w2_own = conv2_weight.reshape(9, HALF, C)
    w2_recv = swap_mp(w2_own)
    qw_own = jnp.transpose(qkv_weight, (1, 0, 2))
    qw_recv = swap_mp(qw_own)
    ow_recv = swap_mp(out_weight)
    g_recv = swap_mp(out_grad)

    hid, act1_t, act2_t, stat0, stat1, prm, w1_full, *win2 = call(
        first_kernel,
        [
            (maps_shape, F32), ((C, n * PIX), BF16), ((C, n * PIX), BF16),
            ((2 * n, C), F32), ((2 * n, C), F32), ((PACK, C), F32), weight_shape,
        ] + [WIN] * n,
        maps_in, x_recv, w1_own, w1_recv, pk_own, pk_recv,
        scratch=[pltpu.VMEM(*WIN)] * n + [pltpu.VMEM(w1_own.shape, BF16), pltpu.SemaphoreType.DMA],
        specs={3: ANYWHERE},
        flops=10**11,
    )
    tile_f32, tile_low = pltpu.VMEM((PIX, C), F32), pltpu.VMEM((PIX, C), BF16)
    three_low = pltpu.VMEM((3, PIX, C), BF16)
    out_keep, out_send, dmid, wg_keep, wg_send, sums3, w2_full, *win3 = call(
        middle_kernel,
        [
            (half_shape, BF16), (half_shape, BF16), (maps_shape, F32),
            ((4 * C, HALF), BF16), ((4 * C, HALF), BF16), ((8, C), F32), weight_shape,
        ] + [WIN] * n,
        maps_in, x_recv, w2_own, w2_recv, prm, out_grad, g_recv, qw_own, qw_recv, out_weight, ow_recv, *win2,
        scratch=[pltpu.VMEM((3, C, C), BF16), tile_low]
        + [tile_f32] * (3 * n) + [tile_low] * n + [three_low] * n + [tile_low] * (3 * n) + [three_low] * n,
    )
    wg_recv = swap_mp(wg_send)
    sums2, time_rows, *win4 = call(
        hidden_back_kernel,
        [((8, C), F32), ((EXTRA, HALF), BF16)] + [WIN] * n,
        timesteps, hid, stat1, w2_full, prm, *win3,
        specs={0: SCALAR},
    )

    def conv_grad(kernel, taps, act_t, windows, others=(), after=()):
        shape = ((len(taps) * C + sum(v.shape[0] for v in others), HALF), BF16)
        specs = {1 + n + len(others) + i: ANYWHERE for i in range(len(after))}
        keep, send = call(kernel(taps), [shape, shape], act_t, *windows, *others, *after, specs=specs)
        return keep, swap_mp(send)

    conv1_pairs = [
        conv_grad(conv1_grad_kernel, CONV1_TAPS[0], act1_t, win4, others=(time_rows,)),
        conv_grad(conv1_grad_kernel, CONV1_TAPS[1], act1_t, win4),
    ]
    arrived = (wg_recv,) + tuple(recv for _, recv in conv1_pairs)
    conv2_pairs = [
        conv_grad(conv2_grad_kernel, CONV2_TAPS[0], act2_t, win3, after=(conv1_pairs[1][0],)),
        conv_grad(conv2_grad_kernel, CONV2_TAPS[1], act2_t, win3, after=arrived),
    ]
    groups = [conv1_pairs[:1], conv1_pairs[1:] + conv2_pairs + [(wg_keep, wg_recv)]]
    chains = [Exchange(order, pairs, extra) for order, pairs, extra in zip(orders, groups, (EXTRA, 0))]
    early, late = chains
    start_exchanges(chains, groups)
    mg_keep, mg_send, rows_keep, rows_send = call(
        input_back_kernel,
        [(half_shape, F32), (half_shape, BF16), ((SUMS, HALF), F32), ((SUMS, HALF), F32)],
        late.own, maps_in, x_recv, stat0, w1_full, prm, dmid, sums2, sums3, *win4,
        specs={0: ANYWHERE},
    )
    rows_recv = swap_mp(rows_send)
    out_recv, mg_recv = swap_mp(out_send), swap_mp(mg_send)
    turn = rows_keep
    for i in range(len(early.steps) - 1):
        early.step(turn, (rows_keep, rows_recv))
        late.step(early.own)
        turn = late.own
        if i == 0:
            maps_out, maps_grad, turn = call(
                maps_kernel, [(maps_in.shape, BF16), (maps_in.shape, F32), ((8, HALF), F32)],
                turn, out_keep, out_recv, mg_keep, mg_recv,
                specs={0: ANYWHERE},
            )
        if i == early.whole - 1:
            table_grad, tw_grad, time_b, turn = time_results(
                early.gathered, early.bits, temb_table, temb_weight, tw_recv, turn,
            )
    conv1, conv2, qkv, out_w, gains, biases, conv_b, qkv_b, out_b = weight_results(chains, len(CONV1_TAPS[0]) * C)
    return (
        maps_out, maps_grad, table_grad, gains, biases, conv1.reshape(3, 3, C, HALF), conv_b, tw_grad,
        time_b.reshape(HALF), conv2.reshape(3, 3, HALF, C), jnp.transpose(qkv, (1, 0, 2)), qkv_b, out_w,
        out_b.reshape(HALF),
    )


def solution(mesh):
    args = (
        P("dp", None, "mp"), P("dp"), P(), P(None, "mp"), P(None, "mp"), P(None, None, None, "mp"),
        P(None, "mp"), P(None, "mp"), P("mp"), P(None, None, "mp", None), P(None, None, "mp"),
        P(None, "mp"), P("mp", None), P("mp"), P("dp", None, "mp"),
    )
    outs = (
        P("dp", None, "mp"), P("dp", None, "mp"), P(), P(None, "mp"), P(None, "mp"),
        P(None, None, None, "mp"), P(None, "mp"), P(None, "mp"), P("mp"), P(None, None, "mp", None),
        P(None, None, "mp"), P(None, "mp"), P("mp", None), P("mp"),
    )
    return jax.shard_map(on_device, mesh=mesh, in_specs=args, out_specs=outs, check_vma=False)
```

```python
import jax
import jax.numpy as jnp
from jax import lax
from jax.experimental import pallas as pl
from jax.experimental.pallas import tpu as pltpu
from jax.sharding import PartitionSpec as P

C = 256
HALF = 128
SIDE = 16
PIX = 256
GROUP = 8
EPS = 1e-06
F32 = jnp.float32
BF16 = jnp.bfloat16
WHOLE = pl.BlockSpec(memory_space=pltpu.VMEM)
SCALAR = pl.BlockSpec(memory_space=pltpu.SMEM)
ANYWHERE = pl.BlockSpec(memory_space=pl.ANY)
IN_HBM = pl.BlockSpec(memory_space=pltpu.HBM)


def call(body, outs, *args, scratch=(), specs=None, limit=16, flops=1):
    specs = specs or {}
    return pl.pallas_call(
        body,
        out_shape=tuple(jax.ShapeDtypeStruct(s, d) for s, d in outs),
        in_specs=[specs.get(i, WHOLE) for i in range(len(args))],
        out_specs=tuple(WHOLE for _ in outs),
        scratch_shapes=list(scratch),
        compiler_params=pltpu.CompilerParams(vmem_limit_bytes=limit << 20),
        cost_estimate=pl.CostEstimate(flops=flops, bytes_accessed=0, transcendentals=0),
    )(*args)


def dot(a, b):
    return jnp.dot(a, b, preferred_element_type=F32)


def dot_bt(a, b):
    return lax.dot_general(a, b, (((1,), (1,)), ((), ())), preferred_element_type=F32)


def dot_at(a, b):
    return lax.dot_general(a, b, (((0,), (0,)), ((), ())), preferred_element_type=F32)


def join(first, own, recv, axis):
    low = jnp.where(first, own, recv)
    high = jnp.where(first, recv, own)
    return jnp.concatenate([low, high], axis=axis)


def split(first, values, axis=1):
    low, high = jnp.split(values, 2, axis)
    return jnp.where(first, low, high), jnp.where(first, high, low)


def group_merge(mean, square, count):
    lane = lax.broadcasted_iota(jnp.int32, mean.shape, 1)
    width = mean.shape[1]

    def partner(rows, step):
        up = pltpu.roll(rows, width - step, 1)
        down = pltpu.roll(rows, step, 1)
        return jnp.where((lane & step) == 0, up, down)

    for step in (1, 2, 4):
        other = partner(mean, step)
        gap = mean - other
        square = square + partner(square, step) + gap * gap * (0.5 * count * step)
        mean = 0.5 * (mean + other)
    return mean, square


def group_sum(rows):
    lane = lax.broadcasted_iota(jnp.int32, rows.shape, 1)
    width = rows.shape[1]
    for step in (1, 2, 4):
        up = pltpu.roll(rows, width - step, 1)
        down = pltpu.roll(rows, step, 1)
        rows = rows + jnp.where((lane & step) == 0, up, down)
    return rows


def col_sum(values):
    return jnp.sum(values, axis=0, keepdims=True)


def norm_stats(values):
    mean = col_sum(values) * (1.0 / PIX)
    square = col_sum((values - mean) ** 2)
    mean, square = group_merge(mean, square, PIX)
    return mean, lax.rsqrt(square * (1.0 / (PIX * GROUP)) + EPS)


def all_stats(maps):
    means = [col_sum(v) * (1.0 / PIX) for v in maps]
    squares = [col_sum((v - mean) ** 2) for v, mean in zip(maps, means)]
    mean, square = group_merge(jnp.concatenate(means, axis=0), jnp.concatenate(squares, axis=0), PIX)
    return mean, lax.rsqrt(square * (1.0 / (PIX * GROUP)) + EPS)


def norm_back(grad, unit, gain, rstd):
    plain = col_sum(grad)
    scaled = col_sum(grad * unit)
    both = group_sum(jnp.concatenate([plain * gain, scaled * gain], axis=0)) * (1.0 / (PIX * GROUP))
    inner = grad * gain - both[0:1] - unit * both[1:2]
    return inner * rstd, scaled, plain


def sigmoid(v):
    return 1.0 / (1.0 + jnp.exp(-v))


def put_windows(win, values):
    col = lax.broadcasted_iota(jnp.int32, (PIX, 1), 0) & (SIDE - 1)
    before = jnp.where(col == 0, 0.0, pltpu.roll(values, 1, 0))
    after = jnp.where(col == SIDE - 1, 0.0, pltpu.roll(values, PIX - 1, 0))
    blank = jnp.zeros((SIDE, C), BF16)
    for c, shifted in enumerate((before, values, after)):
        win[c, 0:SIDE, :] = blank
        win[c, SIDE + PIX : 2 * SIDE + PIX, :] = blank
        win[c, SIDE : SIDE + PIX, :] = shifted.astype(BF16)


def window(win, r, c):
    return win[c, SIDE * r : SIDE * r + PIX, :]


def conv_forward(win, w_ref):
    total = None
    for r in range(3):
        for c in range(3):
            part = dot(window(win, r, c), w_ref[3 * r + c])
            total = part if total is None else total + part
    return total


def conv_transposed(win, w_ref):
    total = None
    for r in range(3):
        for c in range(3):
            part = dot_bt(window(win, 2 - r, 2 - c), w_ref[3 * r + c])
            total = part if total is None else total + part
    return total


WIN = ((3, PIX + 2 * SIDE, C), BF16)

GAIN, BIAS, CONV_B, QKV_B, OUT_B, TIME_B, PACK = 0, 3, 6, 8, 10, 11, 16


def blank_kernel(result):
    result[...] = jnp.zeros_like(result)


def time_kernel(steps, pk, table, tw, w1, result):
    total = result.shape[0] - PACK
    result[0:PACK] = pk[...]
    rows = jnp.concatenate([table[pl.ds(steps[i], 1)] for i in range(total)], axis=0)
    e = rows * sigmoid(rows)
    e_high = e.astype(BF16)
    e_low = (e - e_high.astype(F32)).astype(BF16)
    shift = pk[TIME_B : TIME_B + 1] + pk[CONV_B : CONV_B + 1]
    result[PACK : PACK + total] = dot(e_high, tw[...]) + dot(e_low, tw[...]) + shift


def first_kernel(x_own, x_recv, w_own, w_recv, pk_own, pk_recv, *rest):
    n = x_own.shape[0] // 2
    hid, act_t, act2_t, stat0, stat1, prm_out, wfull = rest[:7]
    win2, (*wins, w_here, w_sem) = rest[7 : 7 + n], rest[7 + n :]
    me = lax.axis_index("mp")
    first = me == 0
    w_copy = pltpu.make_async_copy(w_recv, w_here, w_sem)
    w_copy.start()
    pk = join(first, pk_own[0:PACK], pk_recv[0:PACK], 1)
    prm_out[...] = pk
    xs = [join(first, x_own[me * n + m], x_recv[me * n + m], 1).astype(F32) for m in range(n)]
    mean, rstd = all_stats(xs)
    stat0[0:n] = mean
    stat0[n : 2 * n] = rstd
    scale = rstd * pk[GAIN : GAIN + 1]
    shift = pk[BIAS : BIAS + 1] - mean * scale
    for m in range(n):
        u = xs[m] * scale[m : m + 1] + shift[m : m + 1]
        a = u * sigmoid(u)
        act_t[:, m * PIX : (m + 1) * PIX] = a.astype(BF16).T
        put_windows(wins[m], a)
    w_copy.wait()
    for t in range(9):
        wfull[t] = join(first, w_own[t], w_here[t], 1)
    both = join(first, pk_own[PACK:], pk_recv[PACK:], 1)
    time_row = jnp.where(first, both[0:n], both[n : 2 * n])
    for m in range(n):
        h = conv_forward(wins[m], wfull) + time_row[m : m + 1]
        hid[m] = h
        mean, rstd = norm_stats(h)
        stat1[m : m + 1] = mean
        stat1[n + m : n + m + 1] = rstd
        u = (h - mean) * (rstd * pk[GAIN + 1 : GAIN + 2]) + pk[BIAS + 1 : BIAS + 2]
        a = u * sigmoid(u)
        act2_t[:, m * PIX : (m + 1) * PIX] = a.astype(BF16).T
        put_windows(win2[m], a)


def middle_kernel(x_own, x_recv, w_own, w_recv, prm, g_own, g_recv, qw_own, qw_recv, ow_own, ow_recv, *rest):
    n = g_own.shape[0] // 2
    win2, rest = rest[:n], rest[n:]
    out_keep, out_send, dmid, wg_keep, wg_send, sums, wfull = rest[:7]
    win3, rest = rest[7 : 7 + n], rest[7 + n :]
    qw, ow, rest = rest[0], rest[1], rest[2:]
    mids, units, probs = rest[:n], rest[n : 2 * n], rest[2 * n : 3 * n]
    thirds, qkvs, lows, douts, atts, grads = [rest[(3 + i) * n : (4 + i) * n] for i in range(6)]
    me = lax.axis_index("mp")
    first = me == 0
    scale = 1.0 / 16.0
    for t in range(9):
        wfull[t] = join(first, w_own[t], w_recv[t], 0)
    for j in range(3):
        qw[j] = join(first, qw_own[j], qw_recv[j], 1)
    ow[...] = join(first, ow_own[...], ow_recv[...], 0)
    rstds = []
    for m in range(n):
        at = me * n + m
        x = join(first, x_own[at], x_recv[at], 1).astype(F32)
        mid = x + conv_forward(win2[m], wfull) + prm[CONV_B + 1 : CONV_B + 2]
        mids[m][...] = mid
        mean, rstd = norm_stats(mid)
        rstds.append(rstd)
        unit = (mid - mean) * rstd
        units[m][...] = unit
        thirds[m][...] = (unit * prm[GAIN + 2 : GAIN + 3] + prm[BIAS + 2 : BIAS + 3]).astype(BF16)
    for m in range(n):
        a3 = thirds[m][...]
        qkvs[m][0] = (dot(a3, qw[0]) + prm[QKV_B : QKV_B + 1]).astype(BF16)
        qkvs[m][1] = dot(a3, qw[1]).astype(BF16)
        qkvs[m][2] = (dot(a3, qw[2]) + prm[QKV_B + 1 : QKV_B + 2]).astype(BF16)
    for m in range(n):
        s = dot_bt(qkvs[m][0], qkvs[m][1]) * scale
        e = jnp.exp(s - jnp.max(s, axis=1, keepdims=True))
        p = e * (1.0 / jnp.sum(e, axis=1, keepdims=True))
        probs[m][...] = p
        lows[m][...] = p.astype(BF16)
    for m in range(n):
        gb = join(first, g_own[me * n + m], g_recv[me * n + m], 1)
        douts[m][...] = dot_bt(gb, ow[...]).astype(BF16)
    for m in range(n):
        a = dot(lows[m][...], qkvs[m][2]).astype(BF16)
        atts[m][...] = a
        result = mids[m][...] + dot(a, ow[...]) + prm[OUT_B : OUT_B + 1]
        keep, send = split(first, result.astype(BF16))
        out_keep[m] = keep
        out_send[m] = send
    for m in range(n):
        p = probs[m][...]
        dp = dot_bt(douts[m][...], qkvs[m][2])
        ds = (p * (dp - jnp.sum(p * dp, axis=1, keepdims=True))).astype(BF16)
        grads[m][2] = dot_at(lows[m][...], douts[m][...]).astype(BF16)
        lows[m][...] = ds
    for m in range(n):
        ds = lows[m][...]
        grads[m][0] = (dot(ds, qkvs[m][1]) * scale).astype(BF16)
        grads[m][1] = (dot_at(ds, qkvs[m][0]) * scale).astype(BF16)
    gains, biases, mid_bias, out_bias = [], [], [], []
    for m in range(n):
        grad = dot_bt(grads[m][0], qw[0]) + dot_bt(grads[m][1], qw[1]) + dot_bt(grads[m][2], qw[2])
        back, gain_grad, bias_grad = norm_back(grad, units[m][...], prm[GAIN + 2 : GAIN + 3], rstds[m])
        gains.append(gain_grad)
        biases.append(bias_grad)
        g = join(first, g_own[me * n + m], g_recv[me * n + m], 1).astype(F32)
        out_bias.append(col_sum(g))
        d = back + g
        dmid[m] = d
        mid_bias.append(col_sum(d))
        put_windows(win3[m], d)
    third_t = jnp.concatenate([thirds[m][...].T for m in range(n)], axis=1)
    for j in range(3):
        d = jnp.concatenate([grads[m][j] for m in range(n)], axis=0)
        keep, send = split(first, dot(third_t, d).astype(BF16))
        wg_keep[j * C : (j + 1) * C] = keep
        wg_send[j * C : (j + 1) * C] = send
    att_t = jnp.concatenate([atts[m][...].T for m in range(n)], axis=1)
    g_all = jnp.concatenate([join(first, g_own[me * n + m], g_recv[me * n + m], 1) for m in range(n)], axis=0)
    keep, send = split(first, dot(att_t, g_all).astype(BF16), 0)
    for h in range(2):
        lanes, rows = slice(h * HALF, (h + 1) * HALF), slice(3 * C + h * HALF, 3 * C + (h + 1) * HALF)
        wg_keep[rows] = keep[:, lanes]
        wg_send[rows] = send[:, lanes]
    sums[0:1] = sum(gains)
    sums[1:2] = sum(biases)
    sums[2:3] = sum(mid_bias)
    sums[3:4] = sum(col_sum(grads[m][0].astype(F32)) for m in range(n))
    sums[4:5] = sum(col_sum(grads[m][2].astype(F32)) for m in range(n))
    sums[5:6] = sum(out_bias)
    sums[6:8] = jnp.zeros((2, C), F32)


CONV2_TAPS = (range(0, 7), range(7, 9))
CONV1_TAPS = (range(0, 4), range(4, 8), range(8, 9))


def conv2_rows(taps, first, act_t, win, keep, send):
    for i, t in enumerate(taps):
        shifted = jnp.concatenate([window(w, 2 - t // 3, 2 - t % 3) for w in win], axis=0)
        g_keep, g_send = split(first, dot(act_t[...], shifted).astype(BF16), 0)
        for h in range(2):
            lanes = slice(h * HALF, (h + 1) * HALF)
            rows = slice((2 * i + h) * HALF, (2 * i + h + 1) * HALF)
            keep[rows] = g_keep[:, lanes]
            send[rows] = g_send[:, lanes]


def conv2_grad_kernel(act_t, wg_keep, wg_send, *rest):
    win, (keep, send) = rest[:-2], rest[-2:]
    at = len(CONV2_TAPS[0]) * C
    keep[at:] = wg_keep[...]
    send[at:] = wg_send[...]
    conv2_rows(CONV2_TAPS[0], lax.axis_index("mp") == 0, act_t, win, keep, send)


def last_conv2_kernel(after, act_t, *rest):
    win, (keep, send) = rest[:-2], rest[-2:]
    conv2_rows(CONV2_TAPS[1], lax.axis_index("mp") == 0, act_t, win, keep, send)


def hidden_back_kernel(steps, after, hid, stat, wfull, prm, *rest):
    n = hid.shape[0]
    win3, (sums, time_rows), win4 = rest[:n], rest[n : n + 2], rest[n + 2 :]
    gain, bias = prm[GAIN + 1 : GAIN + 2], prm[BIAS + 1 : BIAS + 2]
    gains, biases, times = [], [], []
    for m in range(n):
        rstd = stat[n + m : n + m + 1]
        unit = (hid[m] - stat[m : m + 1]) * rstd
        u = unit * gain + bias
        sig = sigmoid(u)
        slope = sig * (1.0 + u * (1.0 - sig))
        grad = conv_transposed(win3[m], wfull) * slope
        back, gain_grad, bias_grad = norm_back(grad, unit, gain, rstd)
        gains.append(gain_grad)
        biases.append(bias_grad)
        low = back.astype(BF16).astype(F32)
        times.append(col_sum(low))
        put_windows(win4[m], low)
    me = lax.axis_index("mp")
    lane = lax.broadcasted_iota(jnp.int32, (1, HALF), 1)
    step_row = jnp.zeros((1, HALF), jnp.int32)
    for i in range(n):
        step = steps[me * n + i]
        step_row = jnp.where(lane == i, step >> 5, jnp.where(lane == n + i, step & 31, step_row))
    rows = jnp.concatenate(times, axis=0)
    blank = jnp.zeros((8 - n, HALF), F32)
    left = [rows[:, :HALF], step_row.astype(F32), blank[1:]]
    time_rows[...] = jnp.concatenate(left + [rows[:, HALF:], blank], axis=0).astype(BF16)
    sums[0:1] = sum(gains)
    sums[1:2] = sum(biases)
    sums[2:3] = sum(times)
    sums[3:8] = jnp.zeros((5, C), F32)


def conv1_grad_kernel(taps, count):
    def body(act_t, *rest):
        n = act_t.shape[1] // PIX
        win, others, (keep, send) = rest[:n], rest[n : n + count], rest[-2:]
        first = lax.axis_index("mp") == 0
        at = 0
        for ref, other in zip((keep, send), others):
            at = other.shape[0]
            ref[0:at] = other[...]
        for i, t in enumerate(taps):
            shifted = jnp.concatenate([window(w, 2 - t // 3, 2 - t % 3) for w in win], axis=0)
            g_keep, g_send = split(first, dot(act_t[...], shifted).astype(BF16))
            keep[at + i * C : at + (i + 1) * C] = g_keep
            send[at + i * C : at + (i + 1) * C] = g_send

    return body


def input_back_kernel(after, x_own, x_recv, stat, wfull, prm, dmid, sums2, sums3, out_send, *rest):
    n = dmid.shape[0]
    win4, (keep, send, out_pass, rows_keep, rows_send) = rest[:n], rest[n:]
    me = lax.axis_index("mp")
    first = me == 0
    gain, bias = prm[GAIN : GAIN + 1], prm[BIAS : BIAS + 1]
    gains, biases = [], []
    for m in range(n):
        at = me * n + m
        rstd = stat[n + m : n + m + 1]
        x = join(first, x_own[at], x_recv[at], 1).astype(F32)
        unit = (x - stat[m : m + 1]) * rstd
        u = unit * gain + bias
        sig = sigmoid(u)
        slope = sig * (1.0 + u * (1.0 - sig))
        grad = conv_transposed(win4[m], wfull) * slope
        back, gain_grad, bias_grad = norm_back(grad, unit, gain, rstd)
        gains.append(gain_grad)
        biases.append(bias_grad)
        d_keep, d_send = split(first, back + dmid[m])
        keep[m] = d_keep
        send[m] = d_send.astype(BF16)
        out_pass[m] = out_send[m]
    small = [
        sum(gains), sums2[0:1], sums3[0:1], sum(biases), sums2[1:2], sums3[1:2], sums2[2:3], sums3[2:6],
        jnp.zeros((5, C), F32),
    ]
    rows_keep[...], rows_send[...] = split(first, jnp.concatenate(small, axis=0))


def maps_kernel(after, tw_recv, out_keep, out_recv, grad_keep, grad_recv, out, grad, turn):
    n = out_keep.shape[0]
    me = lax.axis_index("mp")
    for m in range(n):
        out[me * n + m] = out_keep[m]
        out[(1 - me) * n + m] = out_recv[m]
        grad[me * n + m] = grad_keep[m]
        grad[(1 - me) * n + m] = grad_recv[m].astype(F32)
    turn[...] = jnp.zeros_like(turn)


EXTRA, SUMS = 16, 16


def bits_of(count):
    bits = list(range(count.bit_length() - 1))
    cut = len(bits) // 2
    orders = [[(1, 3, 0, 2), (2, 1, 0, 3)], [(0, 2, 1, 3), (2, 0, 3, 1)]]
    if len(bits) != 4:
        orders = [[bits, bits[::-1]], [bits[cut:] + bits[:cut], bits[:cut][::-1] + bits[cut:]]]
    return [[(list(order[:cut]), list(order[cut:])) for order in group] for group in orders]


def digit(bits):
    first = lax.axis_index("mp") == 0
    return (lax.axis_index("dp") >> jnp.where(first, bits[0], bits[1])) & 1


def swap_dp(values, bits):
    pairs = []
    for i in range(lax.axis_size("dp")):
        for core in range(2):
            pairs.append((2 * i + core, 2 * (i ^ (1 << bits[core])) + core))
    return lax.ppermute(values, ("dp", "mp"), pairs)


def swap_mp(values):
    return lax.ppermute(values, "mp", [(0, 1), (1, 0)])


def part(index, rows):
    return pl.ds(pl.multiple_of(index * rows, 16), rows)


def added(a, b):
    return (a.astype(F32) + b.astype(F32)).astype(BF16)


def start_exchange(chain, pairs, time_rows, after):
    rows = chain.rows
    half, extra = rows // 2, EXTRA if time_rows else 0

    def body(*refs):
        refs = list(refs)
        sources = [(refs.pop(0), refs.pop(0)) for _ in pairs]
        outs, values = refs[-3:-1], refs[-1]
        end = 0
        for keep, recv in sources:
            size = keep.shape[0]
            values[end : end + size] = added(keep[...], recv[...])
            end += size
        if end < rows:
            values[end:rows] = jnp.zeros((rows - end, HALF), BF16)
        me = digit(chain.steps[0])
        for index, ref in zip((me, 1 - me), outs):
            ref[0:half] = values[part(index, half)]
            if extra:
                ref[half:] = refs[0][...]

    args = [v for pair in pairs for v in pair] + list(time_rows)
    specs = {len(args) + i: ANYWHERE for i in range(len(after))}
    shape = ((half + extra, HALF), BF16)
    scratch = [pltpu.VMEM((rows, HALF), BF16)]
    chain.own, send = call(body, [shape, shape], *args, *after, scratch=scratch, specs=specs)
    chain.recv = swap_dp(send, chain.steps[0])
    chain.rows = half


class Exchange:
    def __init__(self, order, rows):
        halving, whole = [list(zip(*[core[i] for core in order])) for i in range(2)]
        self.cut, self.whole = len(halving), len(halving) + len(whole)
        self.steps = halving + whole + halving[::-1]
        self.bits = [[core[0] + core[1] for core in order][c] for c in range(2)]
        self.at = 0
        pieces = 1 << self.cut
        self.piece = -(-rows // (16 * pieces)) * 16
        self.rows = self.piece * pieces

    def step(self, after, small=()):
        bits, following = self.steps[self.at : self.at + 2]
        self.at += 1
        head, rest = self.rows, self.own.shape[0] - self.rows
        halve, ends, last = self.at < self.cut, self.at == self.cut, self.at == self.whole
        gather = self.at > self.whole
        with_small = SUMS if small and ends else 0

        def body(own, recv, after_ref, *refs):
            small_refs, outs = refs[: len(small) if ends else 0], refs[len(small) if ends else 0 :]
            me = digit(bits)
            out = outs[0]
            if gather:
                out[part(me, head)] = own[...]
                out[part(1 - me, head)] = recv[...]
                return
            tails = []
            if halve:
                values, send = outs[-1], outs[1]
                values[...] = added(own[0:head], recv[0:head])
                index = digit(following)
                out[0 : head // 2] = values[part(index, head // 2)]
                send[0 : head // 2] = values[part(1 - index, head // 2)]
                tails = [(out, head // 2), (send, head // 2)]
            else:
                out[0:head] = added(own[0:head], recv[0:head])
                if with_small:
                    out[head : head + SUMS] = (small_refs[0][...] + small_refs[1][...]).astype(BF16)
                tails = [(outs[-1], 0 if last else head + with_small)]
            if rest:
                low = me == 0
                mine, theirs = own[head:], recv[head:]
                for ref, at in tails:
                    ref[at : at + rest] = jnp.where(low, mine, theirs)
                    ref[at + rest : at + 2 * rest] = jnp.where(low, theirs, mine)

        def shape(rows):
            return ((rows, HALF), BF16)

        if gather:
            outs, self.rows = [shape(2 * head)], 2 * head
        elif halve:
            outs, self.rows = [shape(head // 2 + 2 * rest)] * 2, head // 2
        else:
            self.rows = head + with_small
            outs = [shape(self.rows), shape(2 * rest)] if last and rest else [shape(self.rows + 2 * rest)]
        args = (self.own, self.recv, after) + (tuple(small) if ends else ())
        scratch = [pltpu.VMEM((head, HALF), BF16)] if halve else []
        results = call(body, outs, *args, scratch=scratch, specs={2: ANYWHERE})
        self.own = results[0]
        if last and rest:
            self.gathered = results[1]
        self.recv = swap_dp(results[1] if halve else self.own, following)


def time_results(n, gathered, other, order, table, tw_own, tw_recv, after):
    steps, width = table.shape
    padded = -(-steps // HALF) * HALF
    blocks = gathered.shape[0] // EXTRA
    maps = 8 * 2 * blocks

    def owner(core, block):
        return sum((block >> i & 1) << bit for i, bit in enumerate(order[core]))

    def body(rows_ref, other_ref, table_ref, tw_own_ref, tw_recv_ref, after_ref, *refs):
        table_grad, tw_grad, time_b, turn, extra, act_high, act_low = refs
        me = lax.axis_index("mp")
        first = me == 0
        for block in range(blocks):
            rows = slice(block * EXTRA, (block + 1) * EXTRA)
            own_at = jnp.where(first, owner(0, block), owner(1, block))
            other_at = jnp.where(first, owner(1, block), owner(0, block))
            extra[2 * own_at + me] = rows_ref[rows].astype(F32)
            extra[2 * other_at + 1 - me] = other_ref[rows].astype(F32)
        lane = lax.broadcasted_iota(jnp.int32, (maps, HALF), 1)
        row = lax.broadcasted_iota(jnp.int32, (maps, HALF), 0) & 7
        held = row < n
        left = jnp.where(held, extra[:, 0:8].reshape(maps, HALF), 0.0)
        right = jnp.where(held, extra[:, 8:16].reshape(maps, HALF), 0.0)
        step_rows = jnp.broadcast_to(extra[:, n : n + 1], (2 * blocks, 8, HALF)).reshape(maps, HALF)
        weight = jnp.where(held & (lane == row), 32.0, jnp.where(held & (lane == row + n), 1.0, 0.0))
        step = jnp.sum(step_rows * weight, axis=1, keepdims=True).astype(jnp.int32)
        mine = jnp.where(first, left, right)
        time_b[...] = col_sum(mine)
        lane = lax.broadcasted_iota(jnp.int32, (maps, padded), 1)
        pick = jnp.where(lane == step, 1.0, 0.0).astype(BF16)
        tw = join(first, tw_own_ref[...], tw_recv_ref[...], 1)
        back = dot_bt(jnp.concatenate([left, right], axis=1).astype(BF16), tw)
        back_high = back.astype(BF16)
        back_low = (back - back_high.astype(F32)).astype(BF16)
        e = table_ref[...]
        sig = sigmoid(e)
        spread = (dot_at(pick, back_high) + dot_at(pick, back_low))[0:steps]
        table_grad[...] = spread * (sig * (1.0 + e * (1.0 - sig)))
        act = e * sig
        high = act.astype(BF16).astype(F32)
        act_high[steps:padded] = jnp.zeros((padded - steps, width), F32)
        act_low[steps:padded] = jnp.zeros((padded - steps, width), F32)
        act_high[0:steps] = high
        act_low[0:steps] = act - high
        by_step = dot_at(mine.astype(BF16), pick)
        step_high = by_step.astype(BF16)
        step_low = (by_step - step_high.astype(F32)).astype(BF16)
        high, low = act_high[...].astype(BF16), act_low[...].astype(BF16)
        tw_grad[...] = (dot(step_high, high) + dot(step_high, low) + dot(step_low, high)).T
        turn[...] = jnp.zeros_like(turn)

    outs = [(table.shape, F32), (tw_own.shape, F32), ((1, HALF), F32), ((8, HALF), F32)]
    scratch = [
        pltpu.VMEM((2 * blocks, EXTRA, HALF), F32),
        pltpu.VMEM((padded, width), F32),
        pltpu.VMEM((padded, width), F32),
    ]
    args = (gathered, other, table, tw_own, tw_recv, after)
    return call(body, outs, *args, scratch=scratch, specs={5: ANYWHERE}, limit=24)


def weight_results(chains, after):
    def body(after_ref, own1, recv1, own2, recv2, *refs):
        conv1, conv2, qkv, out_w, gains, biases, conv_b, qkv_b, out_b = refs[:9]
        reads = []
        for chain, own, recv, values in zip(chains, (own1, own2), (recv1, recv2), refs[9:]):
            me, rows = digit(chain.steps[-1]), own.shape[0]
            values[part(me, rows)] = own[...]
            values[part(1 - me, rows)] = recv[...]
            reads.append(row_reader(values, chain.piece, values.shape[0] >> chain.cut))
        cut = len(CONV2_TAPS[0])
        for t in range(9):
            read, at = (reads[1], t) if t < cut else (reads[0], t - cut)
            for h in range(2):
                conv2[t, :, h * HALF : (h + 1) * HALF] = read((2 * at + h) * HALF, HALF)
        conv1[...] = reads[0]((9 - cut) * C, 9 * C)
        at = cut * C
        for j in range(3):
            qkv[j] = reads[1](at + j * C, C)
        for h in range(2):
            out_w[:, h * HALF : (h + 1) * HALF] = reads[1](at + 3 * C + h * HALF, HALF)
        values, chain = refs[9], chains[0]
        full = values.shape[0] >> chain.cut
        small = None
        for p in range(1 << chain.cut):
            base = p * full + chain.piece
            block = values[base : base + SUMS].astype(F32)
            small = block if small is None else small + block
        gains[...] = small[0:3]
        biases[...] = small[3:6]
        conv_b[...] = small[6:8]
        qkv_b[...] = small[8:10]
        out_b[...] = small[10:11]

    outs = [
        ((9 * C, HALF), F32), ((9, HALF, C), F32), ((3, C, HALF), F32), ((HALF, C), F32),
        ((3, HALF), F32), ((3, HALF), F32), ((2, HALF), F32), ((2, HALF), F32), ((1, HALF), F32),
    ]
    scratch = [pltpu.VMEM((2 * chain.own.shape[0], HALF), BF16) for chain in chains]
    args = [v for chain in chains for v in (chain.own, chain.recv)]
    return call(body, outs, after, *args, scratch=scratch)


def row_reader(values, piece, full):
    def read(start, size):
        found = []
        while size:
            at, left = start % piece, piece - start % piece
            now = min(size, left)
            base = start // piece * full + at
            found.append(values[base : base + now].astype(F32))
            start, size = start + now, size - now
        return jnp.concatenate(found, axis=0)

    return read


def on_device(
    maps_in, timesteps, temb_table, norm_gain, norm_bias, conv1_weight, conv_bias, temb_weight,
    temb_bias, conv2_weight, qkv_weight, qkv_bias, out_weight, out_bias, out_grad,
):
    count = lax.axis_size("dp")
    orders = bits_of(count)
    total = maps_in.shape[0]
    n = total // 2
    maps_shape, half_shape = (n, PIX, C), (n, PIX, HALF)
    weight_shape = ((9, C, C), BF16)

    x_recv = swap_mp(maps_in)
    w1_own = conv1_weight.reshape(9, C, HALF)
    w1_recv = swap_mp(w1_own)
    blank = call(blank_kernel, [((4, HALF), F32)], flops=10**11)[0]
    pk_own = jnp.concatenate(
        [norm_gain, norm_bias, conv_bias, qkv_bias, out_bias[None], temb_bias[None], blank]
    )
    pk_own = call(
        time_kernel, [((PACK + total, HALF), F32)], timesteps, pk_own, temb_table, temb_weight, w1_own,
        specs={0: SCALAR},
    )[0]
    pk_recv = swap_mp(pk_own)
    tw_recv = swap_mp(temb_weight)
    w2_own = conv2_weight.reshape(9, HALF, C)
    w2_recv = swap_mp(w2_own)
    qw_own = jnp.transpose(qkv_weight, (1, 0, 2))
    qw_recv = swap_mp(qw_own)
    ow_recv = swap_mp(out_weight)
    g_recv = swap_mp(out_grad)

    hid, act1_t, act2_t, stat0, stat1, prm, w1_full, *win2 = call(
        first_kernel,
        [
            (maps_shape, F32), ((C, n * PIX), BF16), ((C, n * PIX), BF16),
            ((2 * n, C), F32), ((2 * n, C), F32), ((PACK, C), F32), weight_shape,
        ] + [WIN] * n,
        maps_in, x_recv, w1_own, w1_recv, pk_own, pk_recv,
        scratch=[pltpu.VMEM(*WIN)] * n + [pltpu.VMEM(w1_own.shape, BF16), pltpu.SemaphoreType.DMA],
        specs={3: ANYWHERE},
        flops=10**11,
    )
    tile_f32, tile_low = pltpu.VMEM((PIX, C), F32), pltpu.VMEM((PIX, C), BF16)
    three_low = pltpu.VMEM((3, PIX, C), BF16)
    out_keep, out_send, dmid, wg_keep, wg_send, sums3, w2_full, *win3 = call(
        middle_kernel,
        [
            (half_shape, BF16), (half_shape, BF16), (maps_shape, F32),
            ((4 * C, HALF), BF16), ((4 * C, HALF), BF16), ((8, C), F32), weight_shape,
        ] + [WIN] * n,
        maps_in, x_recv, w2_own, w2_recv, prm, out_grad, g_recv, qw_own, qw_recv, out_weight, ow_recv, *win2,
        scratch=[pltpu.VMEM((3, C, C), BF16), tile_low]
        + [tile_f32] * (3 * n) + [tile_low] * n + [three_low] * n + [tile_low] * (3 * n) + [three_low] * n,
    )
    def swapped(keep, send):
        return keep, swap_mp(send)

    shape = ((len(CONV2_TAPS[0]) * C + wg_keep.shape[0], HALF), BF16)
    late_pair = swapped(*call(conv2_grad_kernel, [shape, shape], act2_t, wg_keep, wg_send, *win3))
    sums2, time_rows, *win4 = call(
        hidden_back_kernel,
        [((8, C), F32), ((EXTRA, HALF), BF16)] + [WIN] * n,
        timesteps, late_pair[0], hid, stat1, w2_full, prm, *win3,
        specs={0: SCALAR, 1: ANYWHERE},
    )

    early, late = chains = [
        Exchange(order, rows) for order, rows in zip(orders, (11 * C, late_pair[0].shape[0]))
    ]
    start_exchange(late, (late_pair,), (), (sums2,))

    def conv1_grad(taps, others=(), after=()):
        shape = ((len(taps) * C + sum(v.shape[0] for v in others[:1]), HALF), BF16)
        specs = {1 + n + len(others) + i: ANYWHERE for i in range(len(after))}
        return call(conv1_grad_kernel(taps, len(others)), [shape, shape], act1_t, *win4, *others, *after, specs=specs)

    shape = ((len(CONV2_TAPS[1]) * C, HALF), BF16)
    part = call(last_conv2_kernel, [shape, shape], late.own, act2_t, *win3, specs={0: ANYWHERE})
    first_pair = swapped(*conv1_grad(CONV1_TAPS[0], part))
    part = conv1_grad(CONV1_TAPS[1], after=(first_pair[0],))
    last_pair = swapped(*conv1_grad(CONV1_TAPS[2], part, (first_pair[1],)))
    start_exchange(early, (first_pair, last_pair), (time_rows,), (late.own,))
    mg_keep, mg_send, out_send, rows_keep, rows_send = call(
        input_back_kernel,
        [(half_shape, F32), (half_shape, BF16), (half_shape, BF16), ((SUMS, HALF), F32), ((SUMS, HALF), F32)],
        early.own, maps_in, x_recv, stat0, w1_full, prm, dmid, sums2, sums3, out_send, *win4,
        specs={0: ANYWHERE},
        flops=10**10,
    )
    rows_recv = swap_mp(rows_send)
    mg_recv, out_recv = swap_mp(mg_send), swap_mp(out_send)
    turn = rows_keep
    for i in range(len(early.steps) - 1):
        early.step(turn, (rows_keep, rows_recv))
        late.step(early.own)
        if i == 0:
            maps_out, maps_grad, turn = call(
                maps_kernel, [(maps_in.shape, BF16), (maps_in.shape, F32), ((8, HALF), F32)],
                late.own, tw_recv, out_keep, out_recv, mg_keep, mg_recv,
                specs={0: ANYWHERE, 1: ANYWHERE},
            )
        if i == early.whole - 1:
            table_grad, tw_grad, time_b, turn = time_results(
                n, early.gathered, swap_mp(early.gathered), early.bits, temb_table, temb_weight, tw_recv, late.own,
            )
    conv1, conv2, qkv, out_w, gains, biases, conv_b, qkv_b, out_b = weight_results(chains, turn)
    return (
        maps_out, maps_grad, table_grad, gains, biases, conv1.reshape(3, 3, C, HALF), conv_b, tw_grad,
        time_b.reshape(HALF), conv2.reshape(3, 3, HALF, C), jnp.transpose(qkv, (1, 0, 2)), qkv_b, out_w,
        out_b.reshape(HALF),
    )


def solution(mesh):
    args = (
        P("dp", None, "mp"), P("dp"), P(), P(None, "mp"), P(None, "mp"), P(None, None, None, "mp"),
        P(None, "mp"), P(None, "mp"), P("mp"), P(None, None, "mp", None), P(None, None, "mp"),
        P(None, "mp"), P("mp", None), P("mp"), P("dp", None, "mp"),
    )
    outs = (
        P("dp", None, "mp"), P("dp", None, "mp"), P(), P(None, "mp"), P(None, "mp"),
        P(None, None, None, "mp"), P(None, "mp"), P(None, "mp"), P("mp"), P(None, None, "mp", None),
        P(None, None, "mp"), P(None, "mp"), P("mp", None), P("mp"),
    )
    return jax.shard_map(on_device, mesh=mesh, in_specs=args, out_specs=outs, check_vma=False)
```

```python
import jax
import jax.numpy as jnp
from jax import lax
from jax.experimental import pallas as pl
from jax.experimental.pallas import tpu as pltpu
from jax.sharding import PartitionSpec as P

C = 256
HALF = 128
SIDE = 16
PIX = 256
GROUP = 8
EPS = 1e-06
F32 = jnp.float32
BF16 = jnp.bfloat16
WHOLE = pl.BlockSpec(memory_space=pltpu.VMEM)
SCALAR = pl.BlockSpec(memory_space=pltpu.SMEM)
ANYWHERE = pl.BlockSpec(memory_space=pl.ANY)
IN_HBM = pl.BlockSpec(memory_space=pltpu.HBM)


def call(body, outs, *args, scratch=(), specs=None, limit=16, flops=1):
    specs = specs or {}
    return pl.pallas_call(
        body,
        out_shape=tuple(jax.ShapeDtypeStruct(s, d) for s, d in outs),
        in_specs=[specs.get(i, WHOLE) for i in range(len(args))],
        out_specs=tuple(WHOLE for _ in outs),
        scratch_shapes=list(scratch),
        compiler_params=pltpu.CompilerParams(vmem_limit_bytes=limit << 20),
        cost_estimate=pl.CostEstimate(flops=flops, bytes_accessed=0, transcendentals=0),
    )(*args)


def dot(a, b):
    return jnp.dot(a, b, preferred_element_type=F32)


def dot_bt(a, b):
    return lax.dot_general(a, b, (((1,), (1,)), ((), ())), preferred_element_type=F32)


def dot_at(a, b):
    return lax.dot_general(a, b, (((0,), (0,)), ((), ())), preferred_element_type=F32)


def join(first, own, recv, axis):
    low = jnp.where(first, own, recv)
    high = jnp.where(first, recv, own)
    return jnp.concatenate([low, high], axis=axis)


def split(first, values, axis=1):
    low, high = jnp.split(values, 2, axis)
    return jnp.where(first, low, high), jnp.where(first, high, low)


def group_merge(mean, square, count):
    lane = lax.broadcasted_iota(jnp.int32, mean.shape, 1)
    width = mean.shape[1]

    def partner(rows, step):
        up = pltpu.roll(rows, width - step, 1)
        down = pltpu.roll(rows, step, 1)
        return jnp.where((lane & step) == 0, up, down)

    for step in (1, 2, 4):
        other = partner(mean, step)
        gap = mean - other
        square = square + partner(square, step) + gap * gap * (0.5 * count * step)
        mean = 0.5 * (mean + other)
    return mean, square


def group_sum(rows):
    lane = lax.broadcasted_iota(jnp.int32, rows.shape, 1)
    width = rows.shape[1]
    for step in (1, 2, 4):
        up = pltpu.roll(rows, width - step, 1)
        down = pltpu.roll(rows, step, 1)
        rows = rows + jnp.where((lane & step) == 0, up, down)
    return rows


def col_sum(values):
    return jnp.sum(values, axis=0, keepdims=True)


def norm_stats(values):
    mean = col_sum(values) * (1.0 / PIX)
    square = col_sum((values - mean) ** 2)
    mean, square = group_merge(mean, square, PIX)
    return mean, lax.rsqrt(square * (1.0 / (PIX * GROUP)) + EPS)


def all_stats(maps):
    means = [col_sum(v) * (1.0 / PIX) for v in maps]
    squares = [col_sum((v - mean) ** 2) for v, mean in zip(maps, means)]
    mean, square = group_merge(jnp.concatenate(means, axis=0), jnp.concatenate(squares, axis=0), PIX)
    return mean, lax.rsqrt(square * (1.0 / (PIX * GROUP)) + EPS)


def norm_back(grad, unit, gain, rstd):
    plain = col_sum(grad)
    scaled = col_sum(grad * unit)
    both = group_sum(jnp.concatenate([plain * gain, scaled * gain], axis=0)) * (1.0 / (PIX * GROUP))
    inner = grad * gain - both[0:1] - unit * both[1:2]
    return inner * rstd, scaled, plain


def sigmoid(v):
    return 0.5 + 0.5 * jnp.tanh(0.5 * v)


def put_windows(win, values):
    col = lax.broadcasted_iota(jnp.int32, (PIX, 1), 0) & (SIDE - 1)
    before = jnp.where(col == 0, 0.0, pltpu.roll(values, 1, 0))
    after = jnp.where(col == SIDE - 1, 0.0, pltpu.roll(values, PIX - 1, 0))
    blank = jnp.zeros((SIDE, C), BF16)
    for c, shifted in enumerate((before, values, after)):
        win[c, 0:SIDE, :] = blank
        win[c, SIDE + PIX : 2 * SIDE + PIX, :] = blank
        win[c, SIDE : SIDE + PIX, :] = shifted.astype(BF16)


def window(win, r, c):
    return win[c, SIDE * r : SIDE * r + PIX, :]


def conv_forward(win, w_ref):
    total = None
    for r in range(3):
        for c in range(3):
            part = dot(window(win, r, c), w_ref[3 * r + c])
            total = part if total is None else total + part
    return total


def conv_transposed(win, w_ref):
    total = None
    for r in range(3):
        for c in range(3):
            part = dot_bt(window(win, 2 - r, 2 - c), w_ref[3 * r + c])
            total = part if total is None else total + part
    return total


WIN = ((3, PIX + 2 * SIDE, C), BF16)

GAIN, BIAS, CONV_B, QKV_B, OUT_B, TIME_B, PACK = 0, 3, 6, 8, 10, 11, 16


def blank_kernel(result):
    result[...] = jnp.zeros_like(result)


def time_kernel(steps, pk, table, tw, w1, result):
    total = result.shape[0] - PACK
    result[0:PACK] = pk[...]
    rows = jnp.concatenate([table[pl.ds(steps[i], 1)] for i in range(total)], axis=0)
    e = rows * sigmoid(rows)
    e_high = e.astype(BF16)
    e_low = (e - e_high.astype(F32)).astype(BF16)
    shift = pk[TIME_B : TIME_B + 1] + pk[CONV_B : CONV_B + 1]
    result[PACK : PACK + total] = dot(e_high, tw[...]) + dot(e_low, tw[...]) + shift


def first_kernel(x_own, x_recv, w_own, w_recv, pk_own, pk_recv, *rest):
    n = x_own.shape[0] // 2
    hid, act_t, act2_t, stat0, stat1, prm_out, wfull = rest[:7]
    win2, (*wins, w_here, w_sem) = rest[7 : 7 + n], rest[7 + n :]
    me = lax.axis_index("mp")
    first = me == 0
    w_copy = pltpu.make_async_copy(w_recv, w_here, w_sem)
    w_copy.start()
    pk = join(first, pk_own[0:PACK], pk_recv[0:PACK], 1)
    prm_out[...] = pk
    xs = [join(first, x_own[me * n + m], x_recv[me * n + m], 1).astype(F32) for m in range(n)]
    mean, rstd = all_stats(xs)
    stat0[0:n] = mean
    stat0[n : 2 * n] = rstd
    scale = rstd * pk[GAIN : GAIN + 1]
    shift = pk[BIAS : BIAS + 1] - mean * scale
    for m in range(n):
        u = xs[m] * scale[m : m + 1] + shift[m : m + 1]
        a = u * sigmoid(u)
        act_t[:, m * PIX : (m + 1) * PIX] = a.astype(BF16).T
        put_windows(wins[m], a)
    w_copy.wait()
    for t in range(9):
        wfull[t] = join(first, w_own[t], w_here[t], 1)
    both = join(first, pk_own[PACK:], pk_recv[PACK:], 1)
    time_row = jnp.where(first, both[0:n], both[n : 2 * n])
    for m in range(n):
        h = conv_forward(wins[m], wfull) + time_row[m : m + 1]
        hid[m] = h
        mean, rstd = norm_stats(h)
        stat1[m : m + 1] = mean
        stat1[n + m : n + m + 1] = rstd
        u = (h - mean) * (rstd * pk[GAIN + 1 : GAIN + 2]) + pk[BIAS + 1 : BIAS + 2]
        a = u * sigmoid(u)
        act2_t[:, m * PIX : (m + 1) * PIX] = a.astype(BF16).T
        put_windows(win2[m], a)


def middle_kernel(x_own, x_recv, w_own, w_recv, prm, g_own, g_recv, qw_own, qw_recv, ow_own, ow_recv, *rest):
    n = g_own.shape[0] // 2
    win2, rest = rest[:n], rest[n:]
    out_keep, out_send, dmid, wg_keep, wg_send, sums, wfull = rest[:7]
    win3, rest = rest[7 : 7 + n], rest[7 + n :]
    qw, ow, rest = rest[0], rest[1], rest[2:]
    mids, units, probs = rest[:n], rest[n : 2 * n], rest[2 * n : 3 * n]
    thirds, qkvs, lows, douts, atts, grads = [rest[(3 + i) * n : (4 + i) * n] for i in range(6)]
    me = lax.axis_index("mp")
    first = me == 0
    scale = 1.0 / 16.0
    for t in range(9):
        wfull[t] = join(first, w_own[t], w_recv[t], 0)
    for j in range(3):
        qw[j] = join(first, qw_own[j], qw_recv[j], 1)
    ow[...] = join(first, ow_own[...], ow_recv[...], 0)
    rstds = []
    for m in range(n):
        at = me * n + m
        x = join(first, x_own[at], x_recv[at], 1).astype(F32)
        mid = x + conv_forward(win2[m], wfull) + prm[CONV_B + 1 : CONV_B + 2]
        mids[m][...] = mid
        mean, rstd = norm_stats(mid)
        rstds.append(rstd)
        unit = (mid - mean) * rstd
        units[m][...] = unit
        thirds[m][...] = (unit * prm[GAIN + 2 : GAIN + 3] + prm[BIAS + 2 : BIAS + 3]).astype(BF16)
    for m in range(n):
        a3 = thirds[m][...]
        q = (dot(a3, qw[0]) + prm[QKV_B : QKV_B + 1]).astype(BF16)
        k = dot(a3, qw[1]).astype(BF16) * BF16(scale)
        qkvs[m][0] = q * BF16(scale)
        qkvs[m][1] = k
        qkvs[m][2] = (dot(a3, qw[2]) + prm[QKV_B + 1 : QKV_B + 2]).astype(BF16)
        s = dot_bt(q, k)
        e = jnp.exp(s - jnp.max(s, axis=1, keepdims=True))
        p = e * (1.0 / jnp.sum(e, axis=1, keepdims=True))
        probs[m][...] = p
        lows[m][...] = p.astype(BF16)
        gb = join(first, g_own[me * n + m], g_recv[me * n + m], 1)
        douts[m][...] = dot_bt(gb, ow[...]).astype(BF16)
    for m in range(n):
        p_low, p, do, v = lows[m][...], probs[m][...], douts[m][...], qkvs[m][2]
        a = dot(p_low, v).astype(BF16)
        atts[m][...] = a
        dp = dot_bt(do, v)
        ds = (p * (dp - jnp.sum(p * dp, axis=1, keepdims=True))).astype(BF16)
        grads[m][2] = dot_at(p_low, do).astype(BF16)
        lows[m][...] = ds
    for m in range(n):
        ds = lows[m][...]
        grads[m][0] = dot(ds, qkvs[m][1]).astype(BF16)
        grads[m][1] = dot_at(ds, qkvs[m][0]).astype(BF16)
        result = mids[m][...] + dot(atts[m][...], ow[...]) + prm[OUT_B : OUT_B + 1]
        keep, send = split(first, result.astype(BF16))
        out_keep[m] = keep
        out_send[m] = send
    gains, biases, mid_bias, out_bias = [], [], [], []
    for m in range(n):
        grad = dot_bt(grads[m][0], qw[0]) + dot_bt(grads[m][1], qw[1]) + dot_bt(grads[m][2], qw[2])
        back, gain_grad, bias_grad = norm_back(grad, units[m][...], prm[GAIN + 2 : GAIN + 3], rstds[m])
        gains.append(gain_grad)
        biases.append(bias_grad)
        g = join(first, g_own[me * n + m], g_recv[me * n + m], 1).astype(F32)
        out_bias.append(col_sum(g))
        d = back + g
        dmid[m] = d
        mid_bias.append(col_sum(d))
        put_windows(win3[m], d)
    third_t = jnp.concatenate([thirds[m][...].T for m in range(n)], axis=1)
    for j in range(3):
        d = jnp.concatenate([grads[m][j] for m in range(n)], axis=0)
        keep, send = split(first, dot(third_t, d).astype(BF16))
        wg_keep[j * C : (j + 1) * C] = keep
        wg_send[j * C : (j + 1) * C] = send
    att_t = jnp.concatenate([atts[m][...].T for m in range(n)], axis=1)
    g_all = jnp.concatenate([join(first, g_own[me * n + m], g_recv[me * n + m], 1) for m in range(n)], axis=0)
    keep, send = split(first, dot(att_t, g_all).astype(BF16), 0)
    for h in range(2):
        lanes, rows = slice(h * HALF, (h + 1) * HALF), slice(3 * C + h * HALF, 3 * C + (h + 1) * HALF)
        wg_keep[rows] = keep[:, lanes]
        wg_send[rows] = send[:, lanes]
    sums[0:1] = sum(gains)
    sums[1:2] = sum(biases)
    sums[2:3] = sum(mid_bias)
    sums[3:4] = sum(col_sum(grads[m][0].astype(F32)) for m in range(n))
    sums[4:5] = sum(col_sum(grads[m][2].astype(F32)) for m in range(n))
    sums[5:6] = sum(out_bias)
    sums[6:8] = jnp.zeros((2, C), F32)


CONV2_TAPS = (range(0, 7), range(7, 9))


def conv2_rows(taps, first, act_t, win, keep, send):
    for i, t in enumerate(taps):
        shifted = jnp.concatenate([window(w, 2 - t // 3, 2 - t % 3) for w in win], axis=0)
        g_keep, g_send = split(first, dot(act_t[...], shifted).astype(BF16), 0)
        for h in range(2):
            lanes = slice(h * HALF, (h + 1) * HALF)
            rows = slice((2 * i + h) * HALF, (2 * i + h + 1) * HALF)
            keep[rows] = g_keep[:, lanes]
            send[rows] = g_send[:, lanes]


def conv2_grad_kernel(act_t, wg_keep, wg_send, *rest):
    win, (keep, send) = rest[:-2], rest[-2:]
    at = len(CONV2_TAPS[0]) * C
    keep[at:] = wg_keep[...]
    send[at:] = wg_send[...]
    conv2_rows(CONV2_TAPS[0], lax.axis_index("mp") == 0, act_t, win, keep, send)


def last_grad_kernel(after, act2_t, act1_t, *rest):
    n = act1_t.shape[1] // PIX
    win3, win4, (keep, send) = rest[:n], rest[n : 2 * n], rest[2 * n :]
    first = lax.axis_index("mp") == 0
    conv2_rows(CONV2_TAPS[1], first, act2_t, win3, keep, send)
    at = len(CONV2_TAPS[1]) * C
    for t in range(9):
        shifted = jnp.concatenate([window(w, 2 - t // 3, 2 - t % 3) for w in win4], axis=0)
        g_keep, g_send = split(first, dot(act1_t[...], shifted).astype(BF16))
        keep[at + t * C : at + (t + 1) * C] = g_keep
        send[at + t * C : at + (t + 1) * C] = g_send


def hidden_back_kernel(steps, after, hid, stat, wfull, prm, *rest):
    n = hid.shape[0]
    win3, (sums, time_rows), win4 = rest[:n], rest[n : n + 2], rest[n + 2 :]
    gain, bias = prm[GAIN + 1 : GAIN + 2], prm[BIAS + 1 : BIAS + 2]
    gains, biases, times = [], [], []
    for m in range(n):
        rstd = stat[n + m : n + m + 1]
        unit = (hid[m] - stat[m : m + 1]) * rstd
        u = unit * gain + bias
        sig = sigmoid(u)
        slope = sig * (1.0 + u * (1.0 - sig))
        grad = conv_transposed(win3[m], wfull) * slope
        back, gain_grad, bias_grad = norm_back(grad, unit, gain, rstd)
        gains.append(gain_grad)
        biases.append(bias_grad)
        times.append(col_sum(back))
        put_windows(win4[m], back)
    me = lax.axis_index("mp")
    lane = lax.broadcasted_iota(jnp.int32, (1, HALF), 1)
    step_row = jnp.zeros((1, HALF), jnp.int32)
    for i in range(n):
        step = steps[me * n + i]
        step_row = jnp.where(lane == i, step >> 5, jnp.where(lane == n + i, step & 31, step_row))
    rows = jnp.concatenate(times, axis=0)
    blank = jnp.zeros((8 - n, HALF), F32)
    left = [rows[:, :HALF], step_row.astype(F32), blank[1:]]
    time_rows[...] = jnp.concatenate(left + [rows[:, HALF:], blank], axis=0).astype(BF16)
    sums[0:1] = sum(gains)
    sums[1:2] = sum(biases)
    sums[2:3] = sum(times)
    sums[3:8] = jnp.zeros((5, C), F32)


def input_back_kernel(after, x_own, x_recv, stat, wfull, prm, dmid, sums2, sums3, out_send, *rest):
    n = dmid.shape[0]
    win4, (keep, send, out_pass, rows_keep, rows_send) = rest[:n], rest[n:]
    me = lax.axis_index("mp")
    first = me == 0
    gain, bias = prm[GAIN : GAIN + 1], prm[BIAS : BIAS + 1]
    gains, biases = [], []
    for m in range(n):
        at = me * n + m
        rstd = stat[n + m : n + m + 1]
        x = join(first, x_own[at], x_recv[at], 1).astype(F32)
        unit = (x - stat[m : m + 1]) * rstd
        u = unit * gain + bias
        sig = sigmoid(u)
        slope = sig * (1.0 + u * (1.0 - sig))
        grad = conv_transposed(win4[m], wfull) * slope
        back, gain_grad, bias_grad = norm_back(grad, unit, gain, rstd)
        gains.append(gain_grad)
        biases.append(bias_grad)
        d_keep, d_send = split(first, back + dmid[m])
        keep[m] = d_keep
        send[m] = d_send.astype(BF16)
        out_pass[m] = out_send[m]
    small = [
        sum(gains), sums2[0:1], sums3[0:1], sum(biases), sums2[1:2], sums3[1:2], sums2[2:3], sums3[2:6],
        jnp.zeros((5, C), F32),
    ]
    rows_keep[...], rows_send[...] = split(first, jnp.concatenate(small, axis=0))


def maps_kernel(after, tw_recv, out_keep, out_recv, grad_keep, grad_recv, out, grad, turn):
    n = out_keep.shape[0]
    me = lax.axis_index("mp")
    for m in range(n):
        out[me * n + m] = out_keep[m]
        out[(1 - me) * n + m] = out_recv[m]
        grad[me * n + m] = grad_keep[m]
        grad[(1 - me) * n + m] = grad_recv[m].astype(F32)
    turn[...] = jnp.zeros_like(turn)


EXTRA, SUMS = 16, 16


def bits_of(count):
    bits = list(range(count.bit_length() - 1))
    cut = len(bits) // 2
    orders = [[(1, 3, 0, 2), (2, 1, 0, 3)], [(0, 2, 1, 3), (2, 0, 3, 1)]]
    if len(bits) != 4:
        orders = [[bits, bits[::-1]], [bits[cut:] + bits[:cut], bits[:cut][::-1] + bits[cut:]]]
    return [[(list(order[:cut]), list(order[cut:])) for order in group] for group in orders]


def digit(bits):
    first = lax.axis_index("mp") == 0
    return (lax.axis_index("dp") >> jnp.where(first, bits[0], bits[1])) & 1


def swap_dp(values, bits):
    pairs = []
    for i in range(lax.axis_size("dp")):
        for core in range(2):
            pairs.append((2 * i + core, 2 * (i ^ (1 << bits[core])) + core))
    return lax.ppermute(values, ("dp", "mp"), pairs)


def swap_mp(values):
    return lax.ppermute(values, "mp", [(0, 1), (1, 0)])


def part(index, rows):
    return pl.ds(pl.multiple_of(index * rows, 16), rows)


def added(a, b):
    return (a.astype(F32) + b.astype(F32)).astype(BF16)


def start_exchange(chain, pairs, time_rows, after):
    rows = chain.rows
    half, extra = rows // 2, EXTRA if time_rows else 0

    def body(*refs):
        refs = list(refs)
        sources = [(refs.pop(0), refs.pop(0)) for _ in pairs]
        outs, values = refs[-3:-1], refs[-1]
        end = 0
        for keep, recv in sources:
            size = keep.shape[0]
            values[end : end + size] = added(keep[...], recv[...])
            end += size
        if end < rows:
            values[end:rows] = jnp.zeros((rows - end, HALF), BF16)
        me = digit(chain.steps[0])
        for index, ref in zip((me, 1 - me), outs):
            ref[0:half] = values[part(index, half)]
            if extra:
                ref[half:] = refs[0][...]

    args = [v for pair in pairs for v in pair] + list(time_rows)
    specs = {len(args) + i: ANYWHERE for i in range(len(after))}
    shape = ((half + extra, HALF), BF16)
    scratch = [pltpu.VMEM((rows, HALF), BF16)]
    chain.own, send = call(body, [shape, shape], *args, *after, scratch=scratch, specs=specs)
    chain.recv = swap_dp(send, chain.steps[0])
    chain.rows = half


class Exchange:
    def __init__(self, order, rows):
        halving, whole = [list(zip(*[core[i] for core in order])) for i in range(2)]
        self.cut, self.whole = len(halving), len(halving) + len(whole)
        self.steps = halving + whole + halving[::-1]
        self.bits = [[core[0] + core[1] for core in order][c] for c in range(2)]
        self.at = 0
        pieces = 1 << self.cut
        self.piece = -(-rows // (16 * pieces)) * 16
        self.rows = self.piece * pieces

    def step(self, after, small=()):
        bits, following = self.steps[self.at : self.at + 2]
        self.at += 1
        head, rest = self.rows, self.own.shape[0] - self.rows
        halve, ends, last = self.at < self.cut, self.at == self.cut, self.at == self.whole
        gather = self.at > self.whole
        with_small = SUMS if small and ends else 0

        def body(own, recv, after_ref, *refs):
            small_refs, outs = refs[: len(small) if ends else 0], refs[len(small) if ends else 0 :]
            me = digit(bits)
            out = outs[0]
            if gather:
                out[part(me, head)] = own[...]
                out[part(1 - me, head)] = recv[...]
                return
            tails = []
            if halve:
                values, send = outs[-1], outs[1]
                values[...] = added(own[0:head], recv[0:head])
                index = digit(following)
                out[0 : head // 2] = values[part(index, head // 2)]
                send[0 : head // 2] = values[part(1 - index, head // 2)]
                tails = [(out, head // 2), (send, head // 2)]
            else:
                out[0:head] = added(own[0:head], recv[0:head])
                if with_small:
                    out[head : head + SUMS] = (small_refs[0][...] + small_refs[1][...]).astype(BF16)
                tails = [(outs[-1], 0 if last else head + with_small)]
            if rest:
                low = me == 0
                mine, theirs = own[head:], recv[head:]
                for ref, at in tails:
                    ref[at : at + rest] = jnp.where(low, mine, theirs)
                    ref[at + rest : at + 2 * rest] = jnp.where(low, theirs, mine)

        def shape(rows):
            return ((rows, HALF), BF16)

        if gather:
            outs, self.rows = [shape(2 * head)], 2 * head
        elif halve:
            outs, self.rows = [shape(head // 2 + 2 * rest)] * 2, head // 2
        else:
            self.rows = head + with_small
            outs = [shape(self.rows), shape(2 * rest)] if last and rest else [shape(self.rows + 2 * rest)]
        args = (self.own, self.recv, after) + (tuple(small) if ends else ())
        scratch = [pltpu.VMEM((head, HALF), BF16)] if halve else []
        results = call(body, outs, *args, scratch=scratch, specs={2: ANYWHERE})
        self.own = results[0]
        if last and rest:
            self.gathered = results[1]
        self.recv = swap_dp(results[1] if halve else self.own, following)


def time_results(n, gathered, other, order, table, tw_own, tw_recv, after):
    steps, width = table.shape
    padded = -(-steps // HALF) * HALF
    blocks = gathered.shape[0] // EXTRA
    maps = 8 * 2 * blocks

    def owner(core, block):
        return sum((block >> i & 1) << bit for i, bit in enumerate(order[core]))

    def body(rows_ref, other_ref, table_ref, tw_own_ref, tw_recv_ref, after_ref, *refs):
        table_grad, tw_grad, time_b, turn, extra, act_high, act_low = refs
        me = lax.axis_index("mp")
        first = me == 0
        for block in range(blocks):
            rows = slice(block * EXTRA, (block + 1) * EXTRA)
            own_at = jnp.where(first, owner(0, block), owner(1, block))
            other_at = jnp.where(first, owner(1, block), owner(0, block))
            extra[2 * own_at + me] = rows_ref[rows].astype(F32)
            extra[2 * other_at + 1 - me] = other_ref[rows].astype(F32)
        lane = lax.broadcasted_iota(jnp.int32, (maps, HALF), 1)
        row = lax.broadcasted_iota(jnp.int32, (maps, HALF), 0) & 7
        held = row < n
        left = jnp.where(held, extra[:, 0:8].reshape(maps, HALF), 0.0)
        right = jnp.where(held, extra[:, 8:16].reshape(maps, HALF), 0.0)
        step_rows = jnp.broadcast_to(extra[:, n : n + 1], (2 * blocks, 8, HALF)).reshape(maps, HALF)
        weight = jnp.where(held & (lane == row), 32.0, jnp.where(held & (lane == row + n), 1.0, 0.0))
        step = jnp.sum(step_rows * weight, axis=1, keepdims=True).astype(jnp.int32)
        mine = jnp.where(first, left, right)
        time_b[...] = col_sum(mine)
        lane = lax.broadcasted_iota(jnp.int32, (maps, padded), 1)
        pick = jnp.where(lane == step, 1.0, 0.0).astype(BF16)
        tw = join(first, tw_own_ref[...], tw_recv_ref[...], 1)
        back = dot_bt(jnp.concatenate([left, right], axis=1).astype(BF16), tw)
        back_high = back.astype(BF16)
        back_low = (back - back_high.astype(F32)).astype(BF16)
        e = table_ref[...]
        sig = sigmoid(e)
        spread = (dot_at(pick, back_high) + dot_at(pick, back_low))[0:steps]
        table_grad[...] = spread * (sig * (1.0 + e * (1.0 - sig)))
        act = e * sig
        high = act.astype(BF16).astype(F32)
        act_high[steps:padded] = jnp.zeros((padded - steps, width), F32)
        act_low[steps:padded] = jnp.zeros((padded - steps, width), F32)
        act_high[0:steps] = high
        act_low[0:steps] = act - high
        by_step = dot_at(mine.astype(BF16), pick)
        step_high = by_step.astype(BF16)
        step_low = (by_step - step_high.astype(F32)).astype(BF16)
        high, low = act_high[...].astype(BF16), act_low[...].astype(BF16)
        tw_grad[...] = (dot(step_high, high) + dot(step_high, low) + dot(step_low, high)).T
        turn[...] = jnp.zeros_like(turn)

    outs = [(table.shape, F32), (tw_own.shape, F32), ((1, HALF), F32), ((8, HALF), F32)]
    scratch = [
        pltpu.VMEM((2 * blocks, EXTRA, HALF), F32),
        pltpu.VMEM((padded, width), F32),
        pltpu.VMEM((padded, width), F32),
    ]
    args = (gathered, other, table, tw_own, tw_recv, after)
    return call(body, outs, *args, scratch=scratch, specs={5: ANYWHERE}, limit=24)


def laid(chain, own, recv, values):
    me, rows = digit(chain.steps[-1]), own.shape[0]
    values[part(me, rows)] = own[...]
    values[part(1 - me, rows)] = recv[...]
    return row_reader(values, chain.piece, values.shape[0] >> chain.cut)


def put_taps(conv2, at, taps, read):
    for i in range(taps):
        for h in range(2):
            conv2[at + i, :, h * HALF : (h + 1) * HALF] = read((2 * i + h) * HALF, HALF)


def early_results(chain, after):
    taps = len(CONV2_TAPS[1])

    def body(after_ref, own, recv, conv1, last, gains, biases, conv_b, qkv_b, out_b, values):
        read = laid(chain, own, recv, values)
        put_taps(last, 0, taps, read)
        conv1[...] = read(taps * C, 9 * C)
        full = values.shape[0] >> chain.cut
        small = None
        for p in range(1 << chain.cut):
            base = p * full + chain.piece
            block = values[base : base + SUMS].astype(F32)
            small = block if small is None else small + block
        gains[...] = small[0:3]
        biases[...] = small[3:6]
        conv_b[...] = small[6:8]
        qkv_b[...] = small[8:10]
        out_b[...] = small[10:11]

    outs = [
        ((9 * C, HALF), F32), ((taps, HALF, C), F32),
        ((3, HALF), F32), ((3, HALF), F32), ((2, HALF), F32), ((2, HALF), F32), ((1, HALF), F32),
    ]
    scratch = [pltpu.VMEM((2 * chain.own.shape[0], HALF), BF16)]
    return call(body, outs, after, chain.own, chain.recv, scratch=scratch)


def late_results(chain, last):
    taps = len(CONV2_TAPS[0])

    def body(last_ref, own, recv, conv2, qkv, out_w, values):
        read = laid(chain, own, recv, values)
        put_taps(conv2, 0, taps, read)
        conv2[taps:9] = last_ref[...]
        at = taps * C
        for j in range(3):
            qkv[j] = read(at + j * C, C)
        for h in range(2):
            out_w[:, h * HALF : (h + 1) * HALF] = read(at + 3 * C + h * HALF, HALF)

    outs = [((9, HALF, C), F32), ((3, C, HALF), F32), ((HALF, C), F32)]
    scratch = [pltpu.VMEM((2 * chain.own.shape[0], HALF), BF16)]
    return call(body, outs, last, chain.own, chain.recv, scratch=scratch)


def row_reader(values, piece, full):
    def read(start, size):
        found = []
        while size:
            at, left = start % piece, piece - start % piece
            now = min(size, left)
            base = start // piece * full + at
            found.append(values[base : base + now].astype(F32))
            start, size = start + now, size - now
        return jnp.concatenate(found, axis=0)

    return read


def on_device(
    maps_in, timesteps, temb_table, norm_gain, norm_bias, conv1_weight, conv_bias, temb_weight,
    temb_bias, conv2_weight, qkv_weight, qkv_bias, out_weight, out_bias, out_grad,
):
    count = lax.axis_size("dp")
    orders = bits_of(count)
    total = maps_in.shape[0]
    n = total // 2
    maps_shape, half_shape = (n, PIX, C), (n, PIX, HALF)
    weight_shape = ((9, C, C), BF16)

    x_recv = swap_mp(maps_in)
    w1_own = conv1_weight.reshape(9, C, HALF)
    w1_recv = swap_mp(w1_own)
    blank = call(blank_kernel, [((4, HALF), F32)], flops=10**11)[0]
    pk_own = jnp.concatenate(
        [norm_gain, norm_bias, conv_bias, qkv_bias, out_bias[None], temb_bias[None], blank]
    )
    pk_own = call(
        time_kernel, [((PACK + total, HALF), F32)], timesteps, pk_own, temb_table, temb_weight, w1_own,
        specs={0: SCALAR},
    )[0]
    pk_recv = swap_mp(pk_own)
    tw_recv = swap_mp(temb_weight)
    w2_own = conv2_weight.reshape(9, HALF, C)
    w2_recv = swap_mp(w2_own)
    qw_own = jnp.transpose(qkv_weight, (1, 0, 2))
    qw_recv = swap_mp(qw_own)
    ow_recv = swap_mp(out_weight)
    g_recv = swap_mp(out_grad)

    hid, act1_t, act2_t, stat0, stat1, prm, w1_full, *win2 = call(
        first_kernel,
        [
            (maps_shape, F32), ((C, n * PIX), BF16), ((C, n * PIX), BF16),
            ((2 * n, C), F32), ((2 * n, C), F32), ((PACK, C), F32), weight_shape,
        ] + [WIN] * n,
        maps_in, x_recv, w1_own, w1_recv, pk_own, pk_recv,
        scratch=[pltpu.VMEM(*WIN)] * n + [pltpu.VMEM(w1_own.shape, BF16), pltpu.SemaphoreType.DMA],
        specs={3: ANYWHERE},
        flops=10**11,
    )
    tile_f32, tile_low = pltpu.VMEM((PIX, C), F32), pltpu.VMEM((PIX, C), BF16)
    three_low = pltpu.VMEM((3, PIX, C), BF16)
    out_keep, out_send, dmid, wg_keep, wg_send, sums3, w2_full, *win3 = call(
        middle_kernel,
        [
            (half_shape, BF16), (half_shape, BF16), (maps_shape, F32),
            ((4 * C, HALF), BF16), ((4 * C, HALF), BF16), ((8, C), F32), weight_shape,
        ] + [WIN] * n,
        maps_in, x_recv, w2_own, w2_recv, prm, out_grad, g_recv, qw_own, qw_recv, out_weight, ow_recv, *win2,
        scratch=[pltpu.VMEM((3, C, C), BF16), tile_low]
        + [tile_f32] * (3 * n) + [tile_low] * n + [three_low] * n + [tile_low] * (3 * n) + [three_low] * n,
    )
    def swapped(keep, send):
        return keep, swap_mp(send)

    shape = ((len(CONV2_TAPS[0]) * C + wg_keep.shape[0], HALF), BF16)
    late_pair = swapped(*call(conv2_grad_kernel, [shape, shape], act2_t, wg_keep, wg_send, *win3))
    sums2, time_rows, *win4 = call(
        hidden_back_kernel,
        [((8, C), F32), ((EXTRA, HALF), BF16)] + [WIN] * n,
        timesteps, late_pair[0], hid, stat1, w2_full, prm, *win3,
        specs={0: SCALAR, 1: ANYWHERE},
    )

    early, late = chains = [
        Exchange(order, rows) for order, rows in zip(orders, (11 * C, late_pair[0].shape[0]))
    ]
    start_exchange(late, (late_pair,), (), (sums2,))

    shape = ((11 * C, HALF), BF16)
    early_pair = swapped(
        *call(last_grad_kernel, [shape, shape], late.own, act2_t, act1_t, *win3, *win4, specs={0: ANYWHERE})
    )
    start_exchange(early, (early_pair,), (time_rows,), (late.own,))
    mg_keep, mg_send, out_send, rows_keep, rows_send = call(
        input_back_kernel,
        [(half_shape, F32), (half_shape, BF16), (half_shape, BF16), ((SUMS, HALF), F32), ((SUMS, HALF), F32)],
        early.own, maps_in, x_recv, stat0, w1_full, prm, dmid, sums2, sums3, out_send, *win4,
        specs={0: ANYWHERE},
        flops=10**10,
    )
    rows_recv = swap_mp(rows_send)
    mg_recv, out_recv = swap_mp(mg_send), swap_mp(out_send)
    turn = rows_keep
    for i in range(len(early.steps) - 1):
        early.step(turn, (rows_keep, rows_recv))
        late.step(early.own)
        if i == 0:
            maps_out, maps_grad, turn = call(
                maps_kernel, [(maps_in.shape, BF16), (maps_in.shape, F32), ((8, HALF), F32)],
                late.own, tw_recv, out_keep, out_recv, mg_keep, mg_recv,
                specs={0: ANYWHERE, 1: ANYWHERE},
            )
        if i == early.whole - 1:
            table_grad, tw_grad, time_b, turn = time_results(
                n, early.gathered, swap_mp(early.gathered), early.bits, temb_table, temb_weight, tw_recv, late.own,
            )
    conv1, last_taps, gains, biases, conv_b, qkv_b, out_b = early_results(early, turn)
    conv2, qkv, out_w = late_results(late, last_taps)
    return (
        maps_out, maps_grad, table_grad, gains, biases, conv1.reshape(3, 3, C, HALF), conv_b, tw_grad,
        time_b.reshape(HALF), conv2.reshape(3, 3, HALF, C), jnp.transpose(qkv, (1, 0, 2)), qkv_b, out_w,
        out_b.reshape(HALF),
    )


def solution(mesh):
    args = (
        P("dp", None, "mp"), P("dp"), P(), P(None, "mp"), P(None, "mp"), P(None, None, None, "mp"),
        P(None, "mp"), P(None, "mp"), P("mp"), P(None, None, "mp", None), P(None, None, "mp"),
        P(None, "mp"), P("mp", None), P("mp"), P("dp", None, "mp"),
    )
    outs = (
        P("dp", None, "mp"), P("dp", None, "mp"), P(), P(None, "mp"), P(None, "mp"),
        P(None, None, None, "mp"), P(None, "mp"), P(None, "mp"), P("mp"), P(None, None, "mp", None),
        P(None, None, "mp"), P(None, "mp"), P("mp", None), P("mp"),
    )
    return jax.shard_map(on_device, mesh=mesh, in_specs=args, out_specs=outs, check_vma=False)
```

```python
import jax
import jax.numpy as jnp
from jax import lax
from jax.experimental import pallas as pl
from jax.experimental.pallas import tpu as pltpu
from jax.sharding import PartitionSpec as P

C = 256
HALF = 128
SIDE = 16
PIX = 256
GROUP = 8
EPS = 1e-06
F32 = jnp.float32
BF16 = jnp.bfloat16
WHOLE = pl.BlockSpec(memory_space=pltpu.VMEM)
SCALAR = pl.BlockSpec(memory_space=pltpu.SMEM)
ANYWHERE = pl.BlockSpec(memory_space=pl.ANY)
IN_HBM = pl.BlockSpec(memory_space=pltpu.HBM)


def call(body, outs, *args, scratch=(), specs=None, limit=16, flops=1):
    specs = specs or {}
    return pl.pallas_call(
        body,
        out_shape=tuple(jax.ShapeDtypeStruct(s, d) for s, d in outs),
        in_specs=[specs.get(i, WHOLE) for i in range(len(args))],
        out_specs=tuple(WHOLE for _ in outs),
        scratch_shapes=list(scratch),
        compiler_params=pltpu.CompilerParams(vmem_limit_bytes=limit << 20),
        cost_estimate=pl.CostEstimate(flops=flops, bytes_accessed=0, transcendentals=0),
    )(*args)


def dot(a, b):
    return jnp.dot(a, b, preferred_element_type=F32)


def dot_bt(a, b):
    return lax.dot_general(a, b, (((1,), (1,)), ((), ())), preferred_element_type=F32)


def dot_at(a, b):
    return lax.dot_general(a, b, (((0,), (0,)), ((), ())), preferred_element_type=F32)


def join(first, own, recv, axis):
    low = jnp.where(first, own, recv)
    high = jnp.where(first, recv, own)
    return jnp.concatenate([low, high], axis=axis)


def split(first, values, axis=1):
    low, high = jnp.split(values, 2, axis)
    return jnp.where(first, low, high), jnp.where(first, high, low)


def group_merge(mean, square, count):
    lane = lax.broadcasted_iota(jnp.int32, mean.shape, 1)
    width = mean.shape[1]

    def partner(rows, step):
        up = pltpu.roll(rows, width - step, 1)
        down = pltpu.roll(rows, step, 1)
        return jnp.where((lane & step) == 0, up, down)

    for step in (1, 2, 4):
        other = partner(mean, step)
        gap = mean - other
        square = square + partner(square, step) + gap * gap * (0.5 * count * step)
        mean = 0.5 * (mean + other)
    return mean, square


def group_sum(rows):
    lane = lax.broadcasted_iota(jnp.int32, rows.shape, 1)
    width = rows.shape[1]
    for step in (1, 2, 4):
        up = pltpu.roll(rows, width - step, 1)
        down = pltpu.roll(rows, step, 1)
        rows = rows + jnp.where((lane & step) == 0, up, down)
    return rows


def col_sum(values):
    return jnp.sum(values, axis=0, keepdims=True)


def norm_stats(values):
    mean = col_sum(values) * (1.0 / PIX)
    square = col_sum((values - mean) ** 2)
    mean, square = group_merge(mean, square, PIX)
    return mean, lax.rsqrt(square * (1.0 / (PIX * GROUP)) + EPS)


def all_stats(maps):
    means = [col_sum(v) * (1.0 / PIX) for v in maps]
    squares = [col_sum((v - mean) ** 2) for v, mean in zip(maps, means)]
    mean, square = group_merge(jnp.concatenate(means, axis=0), jnp.concatenate(squares, axis=0), PIX)
    return mean, lax.rsqrt(square * (1.0 / (PIX * GROUP)) + EPS)


def norm_back(grad, unit, gain, rstd):
    plain = col_sum(grad)
    scaled = col_sum(grad * unit)
    both = group_sum(jnp.concatenate([plain * gain, scaled * gain], axis=0)) * (1.0 / (PIX * GROUP))
    inner = grad * gain - both[0:1] - unit * both[1:2]
    return inner * rstd, scaled, plain


def sigmoid(v):
    return 0.5 + 0.5 * jnp.tanh(0.5 * v)


def put_windows(win, values):
    col = lax.broadcasted_iota(jnp.int32, (PIX, 1), 0) & (SIDE - 1)
    before = jnp.where(col == 0, 0.0, pltpu.roll(values, 1, 0))
    after = jnp.where(col == SIDE - 1, 0.0, pltpu.roll(values, PIX - 1, 0))
    blank = jnp.zeros((SIDE, C), BF16)
    for c, shifted in enumerate((before, values, after)):
        win[c, 0:SIDE, :] = blank
        win[c, SIDE + PIX : 2 * SIDE + PIX, :] = blank
        win[c, SIDE : SIDE + PIX, :] = shifted.astype(BF16)


def window(win, r, c):
    return win[c, SIDE * r : SIDE * r + PIX, :]


def conv_forward(win, w_ref):
    total = None
    for r in range(3):
        for c in range(3):
            part = dot(window(win, r, c), w_ref[3 * r + c])
            total = part if total is None else total + part
    return total


def conv_transposed(win, w_ref):
    total = None
    for r in range(3):
        for c in range(3):
            part = dot_bt(window(win, 2 - r, 2 - c), w_ref[3 * r + c])
            total = part if total is None else total + part
    return total


WIN = ((3, PIX + 2 * SIDE, C), BF16)

GAIN, BIAS, CONV_B, QKV_B, OUT_B, TIME_B, PACK = 0, 3, 6, 8, 10, 11, 16


def blank_kernel(result):
    result[...] = jnp.zeros_like(result)


def time_kernel(steps, pk, table, tw, w1, result, step_out):
    total = result.shape[0] - PACK
    n = total // 2
    result[0:PACK] = pk[...]
    me = lax.axis_index("mp")
    lane = lax.broadcasted_iota(jnp.int32, (1, HALF), 1)
    step_row = jnp.zeros((1, HALF), jnp.int32)
    for i in range(n):
        step = steps[me * n + i]
        step_row = jnp.where(lane == i, step >> 5, jnp.where(lane == n + i, step & 31, step_row))
    step_out[...] = jnp.broadcast_to(step_row, (8, HALF)).astype(F32)
    rows = jnp.concatenate([table[pl.ds(steps[i], 1)] for i in range(total)], axis=0)
    e = rows * sigmoid(rows)
    e_high = e.astype(BF16)
    e_low = (e - e_high.astype(F32)).astype(BF16)
    shift = pk[TIME_B : TIME_B + 1] + pk[CONV_B : CONV_B + 1]
    result[PACK : PACK + total] = dot(e_high, tw[...]) + dot(e_low, tw[...]) + shift


def first_kernel(x_own, x_recv, w_own, w_recv, pk_own, pk_recv, *rest):
    n = x_own.shape[0] // 2
    hid, act_t, act2_t, stat0, stat1, prm_out, wfull = rest[:7]
    win2, (*wins, w_here, w_sem) = rest[7 : 7 + n], rest[7 + n :]
    me = lax.axis_index("mp")
    first = me == 0
    w_copy = pltpu.make_async_copy(w_recv, w_here, w_sem)
    w_copy.start()
    pk = join(first, pk_own[0:PACK], pk_recv[0:PACK], 1)
    prm_out[...] = pk
    xs = [join(first, x_own[me * n + m], x_recv[me * n + m], 1).astype(F32) for m in range(n)]
    mean, rstd = all_stats(xs)
    stat0[0:n] = mean
    stat0[n : 2 * n] = rstd
    scale = rstd * pk[GAIN : GAIN + 1]
    shift = pk[BIAS : BIAS + 1] - mean * scale
    for m in range(n):
        u = xs[m] * scale[m : m + 1] + shift[m : m + 1]
        a = u * sigmoid(u)
        act_t[:, m * PIX : (m + 1) * PIX] = a.astype(BF16).T
        put_windows(wins[m], a)
    w_copy.wait()
    for t in range(9):
        wfull[t] = join(first, w_own[t], w_here[t], 1)
    both = join(first, pk_own[PACK:], pk_recv[PACK:], 1)
    time_row = jnp.where(first, both[0:n], both[n : 2 * n])
    for m in range(n):
        h = conv_forward(wins[m], wfull) + time_row[m : m + 1]
        hid[m] = h
        mean, rstd = norm_stats(h)
        stat1[m : m + 1] = mean
        stat1[n + m : n + m + 1] = rstd
        u = (h - mean) * (rstd * pk[GAIN + 1 : GAIN + 2]) + pk[BIAS + 1 : BIAS + 2]
        a = u * sigmoid(u)
        act2_t[:, m * PIX : (m + 1) * PIX] = a.astype(BF16).T
        put_windows(win2[m], a)


def middle_kernel(x_own, x_recv, w_own, w_recv, prm, g_own, g_recv, qw_own, qw_recv, ow_own, ow_recv, *rest):
    n = g_own.shape[0] // 2
    win2, rest = rest[:n], rest[n:]
    out_keep, out_send, dmid, wg_keep, wg_send, sums, wfull = rest[:7]
    win3, rest = rest[7 : 7 + n], rest[7 + n :]
    qw, ow, rest = rest[0], rest[1], rest[2:]
    mids, units, probs = rest[:n], rest[n : 2 * n], rest[2 * n : 3 * n]
    thirds, qkvs, lows, douts, atts, grads = [rest[(3 + i) * n : (4 + i) * n] for i in range(6)]
    me = lax.axis_index("mp")
    first = me == 0
    scale = 1.0 / 16.0
    for t in range(9):
        wfull[t] = join(first, w_own[t], w_recv[t], 0)
    for j in range(3):
        qw[j] = join(first, qw_own[j], qw_recv[j], 1)
    ow[...] = join(first, ow_own[...], ow_recv[...], 0)
    rstds = []
    for m in range(n):
        at = me * n + m
        x = join(first, x_own[at], x_recv[at], 1).astype(F32)
        mid = x + conv_forward(win2[m], wfull) + prm[CONV_B + 1 : CONV_B + 2]
        mids[m][...] = mid
        mean, rstd = norm_stats(mid)
        rstds.append(rstd)
        unit = (mid - mean) * rstd
        units[m][...] = unit
        thirds[m][...] = (unit * prm[GAIN + 2 : GAIN + 3] + prm[BIAS + 2 : BIAS + 3]).astype(BF16)
    for m in range(n):
        a3 = thirds[m][...]
        q = (dot(a3, qw[0]) + prm[QKV_B : QKV_B + 1]).astype(BF16)
        k = dot(a3, qw[1]).astype(BF16) * BF16(scale)
        qkvs[m][0] = q * BF16(scale)
        qkvs[m][1] = k
        qkvs[m][2] = (dot(a3, qw[2]) + prm[QKV_B + 1 : QKV_B + 2]).astype(BF16)
        s = dot_bt(q, k)
        e = jnp.exp(s - jnp.max(s, axis=1, keepdims=True))
        p = e * (1.0 / jnp.sum(e, axis=1, keepdims=True))
        probs[m][...] = p
        lows[m][...] = p.astype(BF16)
        gb = join(first, g_own[me * n + m], g_recv[me * n + m], 1)
        douts[m][...] = dot_bt(gb, ow[...]).astype(BF16)
    for m in range(n):
        p_low, p, do, v = lows[m][...], probs[m][...], douts[m][...], qkvs[m][2]
        a = dot(p_low, v).astype(BF16)
        atts[m][...] = a
        dp = dot_bt(do, v)
        ds = (p * (dp - jnp.sum(p * dp, axis=1, keepdims=True))).astype(BF16)
        grads[m][2] = dot_at(p_low, do).astype(BF16)
        lows[m][...] = ds
    for m in range(n):
        ds = lows[m][...]
        grads[m][0] = dot(ds, qkvs[m][1]).astype(BF16)
        grads[m][1] = dot_at(ds, qkvs[m][0]).astype(BF16)
        result = mids[m][...] + dot(atts[m][...], ow[...]) + prm[OUT_B : OUT_B + 1]
        keep, send = split(first, result.astype(BF16))
        out_keep[m] = keep
        out_send[m] = send
    gains, biases, mid_bias, out_bias = [], [], [], []
    for m in range(n):
        grad = dot_bt(grads[m][0], qw[0]) + dot_bt(grads[m][1], qw[1]) + dot_bt(grads[m][2], qw[2])
        back, gain_grad, bias_grad = norm_back(grad, units[m][...], prm[GAIN + 2 : GAIN + 3], rstds[m])
        gains.append(gain_grad)
        biases.append(bias_grad)
        g = join(first, g_own[me * n + m], g_recv[me * n + m], 1).astype(F32)
        out_bias.append(col_sum(g))
        d = back + g
        dmid[m] = d
        mid_bias.append(col_sum(d))
        put_windows(win3[m], d)
    third_t = jnp.concatenate([thirds[m][...].T for m in range(n)], axis=1)
    for j in range(3):
        d = jnp.concatenate([grads[m][j] for m in range(n)], axis=0)
        keep, send = split(first, dot(third_t, d).astype(BF16))
        wg_keep[j * C : (j + 1) * C] = keep
        wg_send[j * C : (j + 1) * C] = send
    att_t = jnp.concatenate([atts[m][...].T for m in range(n)], axis=1)
    g_all = jnp.concatenate([join(first, g_own[me * n + m], g_recv[me * n + m], 1) for m in range(n)], axis=0)
    keep, send = split(first, dot(att_t, g_all).astype(BF16), 0)
    for h in range(2):
        lanes, rows = slice(h * HALF, (h + 1) * HALF), slice(3 * C + h * HALF, 3 * C + (h + 1) * HALF)
        wg_keep[rows] = keep[:, lanes]
        wg_send[rows] = send[:, lanes]
    sums[0:1] = sum(gains)
    sums[1:2] = sum(biases)
    sums[2:3] = sum(mid_bias)
    sums[3:4] = sum(col_sum(grads[m][0].astype(F32)) for m in range(n))
    sums[4:5] = sum(col_sum(grads[m][2].astype(F32)) for m in range(n))
    sums[5:6] = sum(out_bias)
    sums[6:8] = jnp.zeros((2, C), F32)


CONV2_TAPS = (range(0, 7), range(7, 9))


def conv2_rows(taps, first, act_t, win, keep, send):
    for i, t in enumerate(taps):
        shifted = jnp.concatenate([window(w, 2 - t // 3, 2 - t % 3) for w in win], axis=0)
        g_keep, g_send = split(first, dot(act_t[...], shifted).astype(BF16), 0)
        for h in range(2):
            lanes = slice(h * HALF, (h + 1) * HALF)
            rows = slice((2 * i + h) * HALF, (2 * i + h + 1) * HALF)
            keep[rows] = g_keep[:, lanes]
            send[rows] = g_send[:, lanes]


def conv2_grad_kernel(act_t, wg_keep, wg_send, *rest):
    win, (keep, send) = rest[:-2], rest[-2:]
    at = len(CONV2_TAPS[0]) * C
    keep[at:] = wg_keep[...]
    send[at:] = wg_send[...]
    conv2_rows(CONV2_TAPS[0], lax.axis_index("mp") == 0, act_t, win, keep, send)


def last_grad_kernel(after, act2_t, act1_t, *rest):
    n = act1_t.shape[1] // PIX
    win3, win4, (keep, send) = rest[:n], rest[n : 2 * n], rest[2 * n :]
    first = lax.axis_index("mp") == 0
    conv2_rows(CONV2_TAPS[1], first, act2_t, win3, keep, send)
    at = len(CONV2_TAPS[1]) * C
    for t in range(9):
        shifted = jnp.concatenate([window(w, 2 - t // 3, 2 - t % 3) for w in win4], axis=0)
        g_keep, g_send = split(first, dot(act1_t[...], shifted).astype(BF16))
        keep[at + t * C : at + (t + 1) * C] = g_keep
        send[at + t * C : at + (t + 1) * C] = g_send


def hidden_back_kernel(step_row, after, hid, stat, wfull, prm, *rest):
    n = hid.shape[0]
    win3, (sums, time_rows), win4 = rest[:n], rest[n : n + 2], rest[n + 2 :]
    gain, bias = prm[GAIN + 1 : GAIN + 2], prm[BIAS + 1 : BIAS + 2]
    gains, biases, times = [], [], []
    for m in range(n):
        rstd = stat[n + m : n + m + 1]
        unit = (hid[m] - stat[m : m + 1]) * rstd
        u = unit * gain + bias
        sig = sigmoid(u)
        slope = sig * (1.0 + u * (1.0 - sig))
        grad = conv_transposed(win3[m], wfull) * slope
        back, gain_grad, bias_grad = norm_back(grad, unit, gain, rstd)
        gains.append(gain_grad)
        biases.append(bias_grad)
        times.append(col_sum(back))
        put_windows(win4[m], back)
    rows = jnp.concatenate(times, axis=0)
    blank = jnp.zeros((8 - n, HALF), F32)
    left = [rows[:, :HALF], step_row[0:1], blank[1:]]
    time_rows[...] = jnp.concatenate(left + [rows[:, HALF:], blank], axis=0).astype(BF16)
    sums[0:1] = sum(gains)
    sums[1:2] = sum(biases)
    sums[2:3] = sum(times)
    sums[3:8] = jnp.zeros((5, C), F32)


def input_back_kernel(after, x_own, x_recv, stat, wfull, prm, dmid, sums2, sums3, out_send, *rest):
    n = dmid.shape[0]
    win4, (keep, send, out_pass, rows_keep, rows_send) = rest[:n], rest[n:]
    me = lax.axis_index("mp")
    first = me == 0
    gain, bias = prm[GAIN : GAIN + 1], prm[BIAS : BIAS + 1]
    gains, biases = [], []
    for m in range(n):
        at = me * n + m
        rstd = stat[n + m : n + m + 1]
        x = join(first, x_own[at], x_recv[at], 1).astype(F32)
        unit = (x - stat[m : m + 1]) * rstd
        u = unit * gain + bias
        sig = sigmoid(u)
        slope = sig * (1.0 + u * (1.0 - sig))
        grad = conv_transposed(win4[m], wfull) * slope
        back, gain_grad, bias_grad = norm_back(grad, unit, gain, rstd)
        gains.append(gain_grad)
        biases.append(bias_grad)
        d_keep, d_send = split(first, back + dmid[m])
        keep[m] = d_keep
        send[m] = d_send.astype(BF16)
        out_pass[m] = out_send[m]
    small = [
        sum(gains), sums2[0:1], sums3[0:1], sum(biases), sums2[1:2], sums3[1:2], sums2[2:3], sums3[2:6],
        jnp.zeros((5, C), F32),
    ]
    rows_keep[...], rows_send[...] = split(first, jnp.concatenate(small, axis=0))


def maps_kernel(after, tw_recv, out_keep, out_recv, grad_keep, grad_recv, out, grad, turn):
    n = out_keep.shape[0]
    me = lax.axis_index("mp")
    for m in range(n):
        out[me * n + m] = out_keep[m]
        out[(1 - me) * n + m] = out_recv[m]
        grad[me * n + m] = grad_keep[m]
        grad[(1 - me) * n + m] = grad_recv[m].astype(F32)
    turn[...] = jnp.zeros_like(turn)


EXTRA, SUMS = 16, 16


def bits_of(count):
    bits = list(range(count.bit_length() - 1))
    cut = len(bits) // 2
    orders = [[(1, 3, 0, 2), (2, 1, 0, 3)], [(0, 2, 1, 3), (2, 0, 3, 1)]]
    if len(bits) != 4:
        orders = [[bits, bits[::-1]], [bits[cut:] + bits[:cut], bits[:cut][::-1] + bits[cut:]]]
    return [[(list(order[:cut]), list(order[cut:])) for order in group] for group in orders]


def digit(bits):
    first = lax.axis_index("mp") == 0
    return (lax.axis_index("dp") >> jnp.where(first, bits[0], bits[1])) & 1


def swap_dp(values, bits):
    pairs = []
    for i in range(lax.axis_size("dp")):
        for core in range(2):
            pairs.append((2 * i + core, 2 * (i ^ (1 << bits[core])) + core))
    return lax.ppermute(values, ("dp", "mp"), pairs)


def swap_mp(values):
    return lax.ppermute(values, "mp", [(0, 1), (1, 0)])


def part(index, rows):
    return pl.ds(pl.multiple_of(index * rows, 16), rows)


def added(a, b):
    return (a.astype(F32) + b.astype(F32)).astype(BF16)


def start_exchange(chain, pairs, time_rows, after):
    rows = chain.rows
    half, extra = rows // 2, EXTRA if time_rows else 0

    def body(*refs):
        refs = list(refs)
        sources = [(refs.pop(0), refs.pop(0)) for _ in pairs]
        outs, values = refs[-3:-1], refs[-1]
        end = 0
        for keep, recv in sources:
            size = keep.shape[0]
            values[end : end + size] = added(keep[...], recv[...])
            end += size
        if end < rows:
            values[end:rows] = jnp.zeros((rows - end, HALF), BF16)
        me = digit(chain.steps[0])
        for index, ref in zip((me, 1 - me), outs):
            ref[0:half] = values[part(index, half)]
            if extra:
                ref[half:] = refs[0][...]

    args = [v for pair in pairs for v in pair] + list(time_rows)
    specs = {len(args) + i: ANYWHERE for i in range(len(after))}
    shape = ((half + extra, HALF), BF16)
    scratch = [pltpu.VMEM((rows, HALF), BF16)]
    chain.own, send = call(body, [shape, shape], *args, *after, scratch=scratch, specs=specs)
    chain.recv = swap_dp(send, chain.steps[0])
    chain.rows = half


class Exchange:
    def __init__(self, order, rows):
        halving, whole = [list(zip(*[core[i] for core in order])) for i in range(2)]
        self.cut, self.whole = len(halving), len(halving) + len(whole)
        self.steps = halving + whole + halving[::-1]
        self.bits = [[core[0] + core[1] for core in order][c] for c in range(2)]
        self.at = 0
        pieces = 1 << self.cut
        self.piece = -(-rows // (16 * pieces)) * 16
        self.rows = self.piece * pieces

    def step(self, after, small=()):
        bits, following = self.steps[self.at : self.at + 2]
        self.at += 1
        head, rest = self.rows, self.own.shape[0] - self.rows
        halve, ends, last = self.at < self.cut, self.at == self.cut, self.at == self.whole
        gather = self.at > self.whole
        with_small = SUMS if small and ends else 0

        def body(own, recv, after_ref, *refs):
            small_refs, outs = refs[: len(small) if ends else 0], refs[len(small) if ends else 0 :]
            me = digit(bits)
            out = outs[0]
            if gather:
                out[part(me, head)] = own[...]
                out[part(1 - me, head)] = recv[...]
                return
            tails = []
            if halve:
                values, send = outs[-1], outs[1]
                values[...] = added(own[0:head], recv[0:head])
                index = digit(following)
                out[0 : head // 2] = values[part(index, head // 2)]
                send[0 : head // 2] = values[part(1 - index, head // 2)]
                tails = [(out, head // 2), (send, head // 2)]
            else:
                out[0:head] = added(own[0:head], recv[0:head])
                if with_small:
                    out[head : head + SUMS] = (small_refs[0][...] + small_refs[1][...]).astype(BF16)
                tails = [(outs[-1], 0 if last else head + with_small)]
            if rest:
                low = me == 0
                mine, theirs = own[head:], recv[head:]
                for ref, at in tails:
                    ref[at : at + rest] = jnp.where(low, mine, theirs)
                    ref[at + rest : at + 2 * rest] = jnp.where(low, theirs, mine)

        def shape(rows):
            return ((rows, HALF), BF16)

        if gather:
            outs, self.rows = [shape(2 * head)], 2 * head
        elif halve:
            outs, self.rows = [shape(head // 2 + 2 * rest)] * 2, head // 2
        else:
            self.rows = head + with_small
            outs = [shape(self.rows), shape(2 * rest)] if last and rest else [shape(self.rows + 2 * rest)]
        args = (self.own, self.recv, after) + (tuple(small) if ends else ())
        scratch = [pltpu.VMEM((head, HALF), BF16)] if halve else []
        results = call(body, outs, *args, scratch=scratch, specs={2: ANYWHERE})
        self.own = results[0]
        if last and rest:
            self.gathered = results[1]
        self.recv = swap_dp(results[1] if halve else self.own, following)


def time_results(n, gathered, other, order, table, tw_own, tw_recv, after):
    steps, width = table.shape
    padded = -(-steps // HALF) * HALF
    blocks = gathered.shape[0] // EXTRA
    maps = 8 * 2 * blocks

    def owner(core, block):
        return sum((block >> i & 1) << bit for i, bit in enumerate(order[core]))

    def body(rows_ref, other_ref, table_ref, tw_own_ref, tw_recv_ref, after_ref, *refs):
        table_grad, tw_grad, time_b, turn, extra, act_high, act_low = refs
        me = lax.axis_index("mp")
        first = me == 0
        for block in range(blocks):
            rows = slice(block * EXTRA, (block + 1) * EXTRA)
            own_at = jnp.where(first, owner(0, block), owner(1, block))
            other_at = jnp.where(first, owner(1, block), owner(0, block))
            extra[2 * own_at + me] = rows_ref[rows].astype(F32)
            extra[2 * other_at + 1 - me] = other_ref[rows].astype(F32)
        lane = lax.broadcasted_iota(jnp.int32, (maps, HALF), 1)
        row = lax.broadcasted_iota(jnp.int32, (maps, HALF), 0) & 7
        held = row < n
        left = jnp.where(held, extra[:, 0:8].reshape(maps, HALF), 0.0)
        right = jnp.where(held, extra[:, 8:16].reshape(maps, HALF), 0.0)
        step_rows = jnp.broadcast_to(extra[:, n : n + 1], (2 * blocks, 8, HALF)).reshape(maps, HALF)
        weight = jnp.where(held & (lane == row), 32.0, jnp.where(held & (lane == row + n), 1.0, 0.0))
        step = jnp.sum(step_rows * weight, axis=1, keepdims=True).astype(jnp.int32)
        mine = jnp.where(first, left, right)
        time_b[...] = col_sum(mine)
        lane = lax.broadcasted_iota(jnp.int32, (maps, padded), 1)
        pick = jnp.where(lane == step, 1.0, 0.0).astype(BF16)
        tw = join(first, tw_own_ref[...], tw_recv_ref[...], 1)
        back = dot_bt(jnp.concatenate([left, right], axis=1).astype(BF16), tw)
        back_high = back.astype(BF16)
        back_low = (back - back_high.astype(F32)).astype(BF16)
        e = table_ref[...]
        sig = sigmoid(e)
        spread = (dot_at(pick, back_high) + dot_at(pick, back_low))[0:steps]
        table_grad[...] = spread * (sig * (1.0 + e * (1.0 - sig)))
        act = e * sig
        high = act.astype(BF16).astype(F32)
        act_high[steps:padded] = jnp.zeros((padded - steps, width), F32)
        act_low[steps:padded] = jnp.zeros((padded - steps, width), F32)
        act_high[0:steps] = high
        act_low[0:steps] = act - high
        by_step = dot_at(mine.astype(BF16), pick)
        step_high = by_step.astype(BF16)
        step_low = (by_step - step_high.astype(F32)).astype(BF16)
        high, low = act_high[...].astype(BF16), act_low[...].astype(BF16)
        tw_grad[...] = (dot(step_high, high) + dot(step_high, low) + dot(step_low, high)).T
        turn[...] = jnp.zeros_like(turn)

    outs = [(table.shape, F32), (tw_own.shape, F32), ((1, HALF), F32), ((8, HALF), F32)]
    scratch = [
        pltpu.VMEM((2 * blocks, EXTRA, HALF), F32),
        pltpu.VMEM((padded, width), F32),
        pltpu.VMEM((padded, width), F32),
    ]
    args = (gathered, other, table, tw_own, tw_recv, after)
    return call(body, outs, *args, scratch=scratch, specs={5: ANYWHERE}, limit=24)


def laid(chain, own, recv, values):
    me, rows = digit(chain.steps[-1]), own.shape[0]
    values[part(me, rows)] = own[...]
    values[part(1 - me, rows)] = recv[...]
    return row_reader(values, chain.piece, values.shape[0] >> chain.cut)


def put_taps(conv2, at, taps, read):
    for i in range(taps):
        for h in range(2):
            conv2[at + i, :, h * HALF : (h + 1) * HALF] = read((2 * i + h) * HALF, HALF)


def early_results(chain, after):
    taps = len(CONV2_TAPS[1])

    def body(after_ref, own, recv, conv1, last, gains, biases, conv_b, qkv_b, out_b, values):
        read = laid(chain, own, recv, values)
        put_taps(last, 0, taps, read)
        conv1[...] = read(taps * C, 9 * C)
        full = values.shape[0] >> chain.cut
        small = None
        for p in range(1 << chain.cut):
            base = p * full + chain.piece
            block = values[base : base + SUMS].astype(F32)
            small = block if small is None else small + block
        gains[...] = small[0:3]
        biases[...] = small[3:6]
        conv_b[...] = small[6:8]
        qkv_b[...] = small[8:10]
        out_b[...] = small[10:11]

    outs = [
        ((9 * C, HALF), F32), ((taps, HALF, C), F32),
        ((3, HALF), F32), ((3, HALF), F32), ((2, HALF), F32), ((2, HALF), F32), ((1, HALF), F32),
    ]
    scratch = [pltpu.VMEM((2 * chain.own.shape[0], HALF), BF16)]
    return call(body, outs, after, chain.own, chain.recv, scratch=scratch)


def late_results(chain, last):
    taps = len(CONV2_TAPS[0])

    def body(last_ref, own, recv, conv2, qkv, out_w, values):
        read = laid(chain, own, recv, values)
        put_taps(conv2, 0, taps, read)
        conv2[taps:9] = last_ref[...]
        at = taps * C
        for j in range(3):
            qkv[j] = read(at + j * C, C)
        for h in range(2):
            out_w[:, h * HALF : (h + 1) * HALF] = read(at + 3 * C + h * HALF, HALF)

    outs = [((9, HALF, C), F32), ((3, C, HALF), F32), ((HALF, C), F32)]
    scratch = [pltpu.VMEM((2 * chain.own.shape[0], HALF), BF16)]
    return call(body, outs, last, chain.own, chain.recv, scratch=scratch)


def row_reader(values, piece, full):
    def read(start, size):
        found = []
        while size:
            at, left = start % piece, piece - start % piece
            now = min(size, left)
            base = start // piece * full + at
            found.append(values[base : base + now].astype(F32))
            start, size = start + now, size - now
        return jnp.concatenate(found, axis=0)

    return read


def on_device(
    maps_in, timesteps, temb_table, norm_gain, norm_bias, conv1_weight, conv_bias, temb_weight,
    temb_bias, conv2_weight, qkv_weight, qkv_bias, out_weight, out_bias, out_grad,
):
    count = lax.axis_size("dp")
    orders = bits_of(count)
    total = maps_in.shape[0]
    n = total // 2
    maps_shape, half_shape = (n, PIX, C), (n, PIX, HALF)
    weight_shape = ((9, C, C), BF16)

    x_recv = swap_mp(maps_in)
    w1_own = conv1_weight.reshape(9, C, HALF)
    w1_recv = swap_mp(w1_own)
    blank = call(blank_kernel, [((4, HALF), F32)], flops=10**11)[0]
    pk_own = jnp.concatenate(
        [norm_gain, norm_bias, conv_bias, qkv_bias, out_bias[None], temb_bias[None], blank]
    )
    pk_own, step_row = call(
        time_kernel, [((PACK + total, HALF), F32), ((8, HALF), F32)],
        timesteps, pk_own, temb_table, temb_weight, w1_own,
        specs={0: SCALAR},
    )
    pk_recv = swap_mp(pk_own)
    tw_recv = swap_mp(temb_weight)
    w2_own = conv2_weight.reshape(9, HALF, C)
    w2_recv = swap_mp(w2_own)
    qw_own = jnp.transpose(qkv_weight, (1, 0, 2))
    qw_recv = swap_mp(qw_own)
    ow_recv = swap_mp(out_weight)
    g_recv = swap_mp(out_grad)

    hid, act1_t, act2_t, stat0, stat1, prm, w1_full, *win2 = call(
        first_kernel,
        [
            (maps_shape, F32), ((C, n * PIX), BF16), ((C, n * PIX), BF16),
            ((2 * n, C), F32), ((2 * n, C), F32), ((PACK, C), F32), weight_shape,
        ] + [WIN] * n,
        maps_in, x_recv, w1_own, w1_recv, pk_own, pk_recv,
        scratch=[pltpu.VMEM(*WIN)] * n + [pltpu.VMEM(w1_own.shape, BF16), pltpu.SemaphoreType.DMA],
        specs={3: ANYWHERE},
        flops=10**11,
    )
    tile_f32, tile_low = pltpu.VMEM((PIX, C), F32), pltpu.VMEM((PIX, C), BF16)
    three_low = pltpu.VMEM((3, PIX, C), BF16)
    out_keep, out_send, dmid, wg_keep, wg_send, sums3, w2_full, *win3 = call(
        middle_kernel,
        [
            (half_shape, BF16), (half_shape, BF16), (maps_shape, F32),
            ((4 * C, HALF), BF16), ((4 * C, HALF), BF16), ((8, C), F32), weight_shape,
        ] + [WIN] * n,
        maps_in, x_recv, w2_own, w2_recv, prm, out_grad, g_recv, qw_own, qw_recv, out_weight, ow_recv, *win2,
        scratch=[pltpu.VMEM((3, C, C), BF16), tile_low]
        + [tile_f32] * (3 * n) + [tile_low] * n + [three_low] * n + [tile_low] * (3 * n) + [three_low] * n,
    )
    def swapped(keep, send):
        return keep, swap_mp(send)

    shape = ((len(CONV2_TAPS[0]) * C + wg_keep.shape[0], HALF), BF16)
    late_pair = swapped(*call(conv2_grad_kernel, [shape, shape], act2_t, wg_keep, wg_send, *win3))
    sums2, time_rows, *win4 = call(
        hidden_back_kernel,
        [((8, C), F32), ((EXTRA, HALF), BF16)] + [WIN] * n,
        step_row, late_pair[0], hid, stat1, w2_full, prm, *win3,
        specs={1: ANYWHERE},
    )

    early, late = chains = [
        Exchange(order, rows) for order, rows in zip(orders, (11 * C, late_pair[0].shape[0]))
    ]
    start_exchange(late, (late_pair,), (), (sums2,))

    shape = ((11 * C, HALF), BF16)
    early_pair = swapped(
        *call(last_grad_kernel, [shape, shape], late.own, act2_t, act1_t, *win3, *win4, specs={0: ANYWHERE})
    )
    start_exchange(early, (early_pair,), (time_rows,), (late.own,))
    mg_keep, mg_send, out_send, rows_keep, rows_send = call(
        input_back_kernel,
        [(half_shape, F32), (half_shape, BF16), (half_shape, BF16), ((SUMS, HALF), F32), ((SUMS, HALF), F32)],
        early.own, maps_in, x_recv, stat0, w1_full, prm, dmid, sums2, sums3, out_send, *win4,
        specs={0: ANYWHERE},
        flops=10**10,
    )
    rows_recv = swap_mp(rows_send)
    mg_recv, out_recv = swap_mp(mg_send), swap_mp(out_send)
    turn = rows_keep
    for i in range(len(early.steps) - 1):
        early.step(turn, (rows_keep, rows_recv))
        late.step(early.own)
        if i == 0:
            maps_out, maps_grad, turn = call(
                maps_kernel, [(maps_in.shape, BF16), (maps_in.shape, F32), ((8, HALF), F32)],
                late.own, tw_recv, out_keep, out_recv, mg_keep, mg_recv,
                specs={0: ANYWHERE, 1: ANYWHERE},
            )
        if i == early.whole - 1:
            table_grad, tw_grad, time_b, turn = time_results(
                n, early.gathered, swap_mp(early.gathered), early.bits, temb_table, temb_weight, tw_recv, late.own,
            )
    conv1, last_taps, gains, biases, conv_b, qkv_b, out_b = early_results(early, turn)
    conv2, qkv, out_w = late_results(late, last_taps)
    return (
        maps_out, maps_grad, table_grad, gains, biases, conv1.reshape(3, 3, C, HALF), conv_b, tw_grad,
        time_b.reshape(HALF), conv2.reshape(3, 3, HALF, C), jnp.transpose(qkv, (1, 0, 2)), qkv_b, out_w,
        out_b.reshape(HALF),
    )


def solution(mesh):
    args = (
        P("dp", None, "mp"), P("dp"), P(), P(None, "mp"), P(None, "mp"), P(None, None, None, "mp"),
        P(None, "mp"), P(None, "mp"), P("mp"), P(None, None, "mp", None), P(None, None, "mp"),
        P(None, "mp"), P("mp", None), P("mp"), P("dp", None, "mp"),
    )
    outs = (
        P("dp", None, "mp"), P("dp", None, "mp"), P(), P(None, "mp"), P(None, "mp"),
        P(None, None, None, "mp"), P(None, "mp"), P(None, "mp"), P("mp"), P(None, None, "mp", None),
        P(None, None, "mp"), P(None, "mp"), P("mp", None), P("mp"),
    )
    return jax.shard_map(on_device, mesh=mesh, in_specs=args, out_specs=outs, check_vma=False)
```

```python
import functools

import jax
import jax.numpy as jnp
from jax import lax
from jax.experimental import pallas as pl
from jax.experimental.pallas import tpu as pltpu
from jax.sharding import PartitionSpec as P

C = 256
HALF = 128
SIDE = 16
PIX = 256
GROUP = 8
EPS = 1e-06
F32 = jnp.float32
BF16 = jnp.bfloat16
WHOLE = pl.BlockSpec(memory_space=pltpu.VMEM)
SCALAR = pl.BlockSpec(memory_space=pltpu.SMEM)
ANYWHERE = pl.BlockSpec(memory_space=pl.ANY)
IN_HBM = pl.BlockSpec(memory_space=pltpu.HBM)


def call(body, outs, *args, scratch=(), specs=None, limit=16, flops=1):
    specs = specs or {}
    return pl.pallas_call(
        body,
        out_shape=tuple(jax.ShapeDtypeStruct(s, d) for s, d in outs),
        in_specs=[specs.get(i, WHOLE) for i in range(len(args))],
        out_specs=tuple(WHOLE for _ in outs),
        scratch_shapes=list(scratch),
        compiler_params=pltpu.CompilerParams(vmem_limit_bytes=limit << 20),
        cost_estimate=pl.CostEstimate(flops=flops, bytes_accessed=0, transcendentals=0),
    )(*args)


def dot(a, b):
    return jnp.dot(a, b, preferred_element_type=F32)


def dot_bt(a, b):
    return lax.dot_general(a, b, (((1,), (1,)), ((), ())), preferred_element_type=F32)


def dot_at(a, b):
    return lax.dot_general(a, b, (((0,), (0,)), ((), ())), preferred_element_type=F32)


def join(first, own, recv, axis):
    low = jnp.where(first, own, recv)
    high = jnp.where(first, recv, own)
    return jnp.concatenate([low, high], axis=axis)


def split(first, values, axis=1):
    low, high = jnp.split(values, 2, axis)
    return jnp.where(first, low, high), jnp.where(first, high, low)


def group_merge(mean, square, count):
    lane = lax.broadcasted_iota(jnp.int32, mean.shape, 1)
    width = mean.shape[1]

    def partner(rows, step):
        up = pltpu.roll(rows, width - step, 1)
        down = pltpu.roll(rows, step, 1)
        return jnp.where((lane & step) == 0, up, down)

    for step in (1, 2, 4):
        other = partner(mean, step)
        gap = mean - other
        square = square + partner(square, step) + gap * gap * (0.5 * count * step)
        mean = 0.5 * (mean + other)
    return mean, square


def group_sum(rows):
    lane = lax.broadcasted_iota(jnp.int32, rows.shape, 1)
    width = rows.shape[1]
    for step in (1, 2, 4):
        up = pltpu.roll(rows, width - step, 1)
        down = pltpu.roll(rows, step, 1)
        rows = rows + jnp.where((lane & step) == 0, up, down)
    return rows


def col_sum(values):
    return jnp.sum(values, axis=0, keepdims=True)


def norm_stats(values):
    mean = col_sum(values) * (1.0 / PIX)
    square = col_sum((values - mean) ** 2)
    mean, square = group_merge(mean, square, PIX)
    return mean, lax.rsqrt(square * (1.0 / (PIX * GROUP)) + EPS)


def all_stats(maps):
    means = [col_sum(v) * (1.0 / PIX) for v in maps]
    squares = [col_sum((v - mean) ** 2) for v, mean in zip(maps, means)]
    mean, square = group_merge(jnp.concatenate(means, axis=0), jnp.concatenate(squares, axis=0), PIX)
    return mean, lax.rsqrt(square * (1.0 / (PIX * GROUP)) + EPS)


def norm_back(grad, unit, gain, rstd):
    plain = col_sum(grad)
    scaled = col_sum(grad * unit)
    both = group_sum(jnp.concatenate([plain * gain, scaled * gain], axis=0)) * (1.0 / (PIX * GROUP))
    inner = grad * gain - both[0:1] - unit * both[1:2]
    return inner * rstd, scaled, plain


def sigmoid(v):
    return 0.5 + 0.5 * jnp.tanh(0.5 * v)


def put_windows(win, values):
    col = lax.broadcasted_iota(jnp.int32, (PIX, 1), 0) & (SIDE - 1)
    before = jnp.where(col == 0, 0.0, pltpu.roll(values, 1, 0))
    after = jnp.where(col == SIDE - 1, 0.0, pltpu.roll(values, PIX - 1, 0))
    blank = jnp.zeros((SIDE, C), BF16)
    for c, shifted in enumerate((before, values, after)):
        win[c, 0:SIDE, :] = blank
        win[c, SIDE + PIX : 2 * SIDE + PIX, :] = blank
        win[c, SIDE : SIDE + PIX, :] = shifted.astype(BF16)


def window(win, r, c):
    return win[c, SIDE * r : SIDE * r + PIX, :]


def conv_forward(win, w_ref):
    total = None
    for r in range(3):
        for c in range(3):
            part = dot(window(win, r, c), w_ref[3 * r + c])
            total = part if total is None else total + part
    return total


def conv_transposed(win, w_ref):
    total = None
    for r in range(3):
        for c in range(3):
            part = dot_bt(window(win, 2 - r, 2 - c), w_ref[3 * r + c])
            total = part if total is None else total + part
    return total


WIN = ((3, PIX + 2 * SIDE, C), BF16)

GAIN, BIAS, CONV_B, QKV_B, OUT_B, TIME_B, PACK = 0, 3, 6, 8, 10, 11, 16


def blank_kernel(result):
    result[...] = jnp.zeros_like(result)


def time_kernel(steps, pk, table, tw, w1, result, step_out):
    total = result.shape[0] - PACK
    n = total // 2
    result[0:PACK] = pk[...]
    me = lax.axis_index("mp")
    lane = lax.broadcasted_iota(jnp.int32, (1, HALF), 1)
    step_row = jnp.zeros((1, HALF), jnp.int32)
    for i in range(n):
        step = steps[me * n + i]
        step_row = jnp.where(lane == i, step >> 5, jnp.where(lane == n + i, step & 31, step_row))
    step_out[...] = jnp.broadcast_to(step_row, (8, HALF)).astype(F32)
    rows = jnp.concatenate([table[pl.ds(steps[i], 1)] for i in range(total)], axis=0)
    e = rows * sigmoid(rows)
    e_high = e.astype(BF16)
    e_low = (e - e_high.astype(F32)).astype(BF16)
    shift = pk[TIME_B : TIME_B + 1] + pk[CONV_B : CONV_B + 1]
    result[PACK : PACK + total] = dot(e_high, tw[...]) + dot(e_low, tw[...]) + shift


def first_kernel(x_own, x_recv, w_own, w_recv, pk_own, pk_recv, *rest):
    n = x_own.shape[0] // 2
    hid, act_t, act2_t, stat0, stat1, prm_out, wfull = rest[:7]
    win2, (*wins, w_here, w_sem) = rest[7 : 7 + n], rest[7 + n :]
    me = lax.axis_index("mp")
    first = me == 0
    w_copy = pltpu.make_async_copy(w_recv, w_here, w_sem)
    w_copy.start()
    pk = join(first, pk_own[0:PACK], pk_recv[0:PACK], 1)
    prm_out[...] = pk
    xs = [join(first, x_own[me * n + m], x_recv[me * n + m], 1).astype(F32) for m in range(n)]
    mean, rstd = all_stats(xs)
    stat0[0:n] = mean
    stat0[n : 2 * n] = rstd
    scale = rstd * pk[GAIN : GAIN + 1]
    shift = pk[BIAS : BIAS + 1] - mean * scale
    for m in range(n):
        u = xs[m] * scale[m : m + 1] + shift[m : m + 1]
        a = u * sigmoid(u)
        act_t[:, m * PIX : (m + 1) * PIX] = a.astype(BF16).T
        put_windows(wins[m], a)
    w_copy.wait()
    for t in range(9):
        wfull[t] = join(first, w_own[t], w_here[t], 1)
    both = join(first, pk_own[PACK:], pk_recv[PACK:], 1)
    time_row = jnp.where(first, both[0:n], both[n : 2 * n])
    for m in range(n):
        h = conv_forward(wins[m], wfull) + time_row[m : m + 1]
        hid[m] = h
        mean, rstd = norm_stats(h)
        stat1[m : m + 1] = mean
        stat1[n + m : n + m + 1] = rstd
        u = (h - mean) * (rstd * pk[GAIN + 1 : GAIN + 2]) + pk[BIAS + 1 : BIAS + 2]
        a = u * sigmoid(u)
        act2_t[:, m * PIX : (m + 1) * PIX] = a.astype(BF16).T
        put_windows(win2[m], a)


def middle_kernel(x_own, x_recv, w_own, w_recv, prm, g_own, g_recv, qw_own, qw_recv, ow_own, ow_recv, *rest):
    n = g_own.shape[0] // 2
    win2, rest = rest[:n], rest[n:]
    out_keep, out_send, dmid, wg_keep, wg_send, sums, wfull = rest[:7]
    win3, rest = rest[7 : 7 + n], rest[7 + n :]
    qw, ow, rest = rest[0], rest[1], rest[2:]
    mids, units, probs = rest[:n], rest[n : 2 * n], rest[2 * n : 3 * n]
    thirds, qkvs, lows, douts, atts, grads = [rest[(3 + i) * n : (4 + i) * n] for i in range(6)]
    me = lax.axis_index("mp")
    first = me == 0
    scale = 1.0 / 16.0
    for t in range(9):
        wfull[t] = join(first, w_own[t], w_recv[t], 0)
    for j in range(3):
        qw[j] = join(first, qw_own[j], qw_recv[j], 1)
    ow[...] = join(first, ow_own[...], ow_recv[...], 0)
    rstds = []
    for m in range(n):
        at = me * n + m
        x = join(first, x_own[at], x_recv[at], 1).astype(F32)
        mid = x + conv_forward(win2[m], wfull) + prm[CONV_B + 1 : CONV_B + 2]
        mids[m][...] = mid
        mean, rstd = norm_stats(mid)
        rstds.append(rstd)
        unit = (mid - mean) * rstd
        units[m][...] = unit
        thirds[m][...] = (unit * prm[GAIN + 2 : GAIN + 3] + prm[BIAS + 2 : BIAS + 3]).astype(BF16)
    for m in range(n):
        a3 = thirds[m][...]
        q = (dot(a3, qw[0]) + prm[QKV_B : QKV_B + 1]).astype(BF16)
        k = dot(a3, qw[1]).astype(BF16) * BF16(scale)
        qkvs[m][0] = q * BF16(scale)
        qkvs[m][1] = k
        qkvs[m][2] = (dot(a3, qw[2]) + prm[QKV_B + 1 : QKV_B + 2]).astype(BF16)
        s = dot_bt(q, k)
        e = jnp.exp(s - jnp.max(s, axis=1, keepdims=True))
        p = e * (1.0 / jnp.sum(e, axis=1, keepdims=True))
        probs[m][...] = p
        lows[m][...] = p.astype(BF16)
        gb = join(first, g_own[me * n + m], g_recv[me * n + m], 1)
        douts[m][...] = dot_bt(gb, ow[...]).astype(BF16)
    for m in range(n):
        p_low, p, do, v = lows[m][...], probs[m][...], douts[m][...], qkvs[m][2]
        a = dot(p_low, v).astype(BF16)
        atts[m][...] = a
        dp = dot_bt(do, v)
        ds = (p * (dp - jnp.sum(p * dp, axis=1, keepdims=True))).astype(BF16)
        grads[m][2] = dot_at(p_low, do).astype(BF16)
        lows[m][...] = ds
    for m in range(n):
        ds = lows[m][...]
        grads[m][0] = dot(ds, qkvs[m][1]).astype(BF16)
        grads[m][1] = dot_at(ds, qkvs[m][0]).astype(BF16)
        result = mids[m][...] + dot(atts[m][...], ow[...]) + prm[OUT_B : OUT_B + 1]
        keep, send = split(first, result.astype(BF16))
        out_keep[m] = keep
        out_send[m] = send
    gains, biases, mid_bias, out_bias = [], [], [], []
    for m in range(n):
        grad = dot_bt(grads[m][0], qw[0]) + dot_bt(grads[m][1], qw[1]) + dot_bt(grads[m][2], qw[2])
        back, gain_grad, bias_grad = norm_back(grad, units[m][...], prm[GAIN + 2 : GAIN + 3], rstds[m])
        gains.append(gain_grad)
        biases.append(bias_grad)
        g = join(first, g_own[me * n + m], g_recv[me * n + m], 1).astype(F32)
        out_bias.append(col_sum(g))
        d = back + g
        dmid[m] = d
        mid_bias.append(col_sum(d))
        put_windows(win3[m], d)
    third_t = jnp.concatenate([thirds[m][...].T for m in range(n)], axis=1)
    for j in range(3):
        d = jnp.concatenate([grads[m][j] for m in range(n)], axis=0)
        keep, send = split(first, dot(third_t, d).astype(BF16))
        wg_keep[j * C : (j + 1) * C] = keep
        wg_send[j * C : (j + 1) * C] = send
    att_t = jnp.concatenate([atts[m][...].T for m in range(n)], axis=1)
    g_all = jnp.concatenate([join(first, g_own[me * n + m], g_recv[me * n + m], 1) for m in range(n)], axis=0)
    keep, send = split(first, dot(att_t, g_all).astype(BF16), 0)
    for h in range(2):
        lanes, rows = slice(h * HALF, (h + 1) * HALF), slice(3 * C + h * HALF, 3 * C + (h + 1) * HALF)
        wg_keep[rows] = keep[:, lanes]
        wg_send[rows] = send[:, lanes]
    sums[0:1] = sum(gains)
    sums[1:2] = sum(biases)
    sums[2:3] = sum(mid_bias)
    sums[3:4] = sum(col_sum(grads[m][0].astype(F32)) for m in range(n))
    sums[4:5] = sum(col_sum(grads[m][2].astype(F32)) for m in range(n))
    sums[5:6] = sum(out_bias)
    sums[6:8] = jnp.zeros((2, C), F32)


CONV2_TAPS = (range(0, 7), range(7, 9))


def conv2_rows(taps, first, act_t, win, keep, send):
    for i, t in enumerate(taps):
        shifted = jnp.concatenate([window(w, 2 - t // 3, 2 - t % 3) for w in win], axis=0)
        g_keep, g_send = split(first, dot(act_t[...], shifted).astype(BF16), 0)
        for h in range(2):
            lanes = slice(h * HALF, (h + 1) * HALF)
            rows = slice((2 * i + h) * HALF, (2 * i + h + 1) * HALF)
            keep[rows] = g_keep[:, lanes]
            send[rows] = g_send[:, lanes]


def conv2_grad_kernel(act_t, wg_keep, wg_send, *rest):
    win, (keep, send) = rest[:-2], rest[-2:]
    at = len(CONV2_TAPS[0]) * C
    keep[at:] = wg_keep[...]
    send[at:] = wg_send[...]
    conv2_rows(CONV2_TAPS[0], lax.axis_index("mp") == 0, act_t, win, keep, send)


def last_grad_kernel(bits, act2_t, act1_t, late_keep, late_recv, *rest):
    n = act1_t.shape[1] // PIX
    win3, win4, (keep, send, late_own, late_send, values) = rest[:n], rest[n : 2 * n], rest[2 * n :]
    half = late_own.shape[0]
    values[...] = added(late_keep[...], late_recv[...])
    me = digit(bits)
    late_own[...] = values[part(me, half)]
    late_send[...] = values[part(1 - me, half)]
    first = lax.axis_index("mp") == 0
    conv2_rows(CONV2_TAPS[1], first, act2_t, win3, keep, send)
    at = len(CONV2_TAPS[1]) * C
    for t in range(9):
        shifted = jnp.concatenate([window(w, 2 - t // 3, 2 - t % 3) for w in win4], axis=0)
        g_keep, g_send = split(first, dot(act1_t[...], shifted).astype(BF16))
        keep[at + t * C : at + (t + 1) * C] = g_keep
        send[at + t * C : at + (t + 1) * C] = g_send


def hidden_back_kernel(step_row, after, hid, stat, wfull, prm, *rest):
    n = hid.shape[0]
    win3, (sums, time_rows), win4 = rest[:n], rest[n : n + 2], rest[n + 2 :]
    gain, bias = prm[GAIN + 1 : GAIN + 2], prm[BIAS + 1 : BIAS + 2]
    gains, biases, times = [], [], []
    for m in range(n):
        rstd = stat[n + m : n + m + 1]
        unit = (hid[m] - stat[m : m + 1]) * rstd
        u = unit * gain + bias
        sig = sigmoid(u)
        slope = sig * (1.0 + u * (1.0 - sig))
        grad = conv_transposed(win3[m], wfull) * slope
        back, gain_grad, bias_grad = norm_back(grad, unit, gain, rstd)
        gains.append(gain_grad)
        biases.append(bias_grad)
        times.append(col_sum(back))
        put_windows(win4[m], back)
    rows = jnp.concatenate(times, axis=0)
    blank = jnp.zeros((8 - n, HALF), F32)
    left = [rows[:, :HALF], step_row[0:1], blank[1:]]
    time_rows[...] = jnp.concatenate(left + [rows[:, HALF:], blank], axis=0).astype(BF16)
    sums[0:1] = sum(gains)
    sums[1:2] = sum(biases)
    sums[2:3] = sum(times)
    sums[3:8] = jnp.zeros((5, C), F32)


def input_back_kernel(after, x_own, x_recv, stat, wfull, prm, dmid, sums2, sums3, out_send, *rest):
    n = dmid.shape[0]
    win4, (keep, send, out_pass, rows_keep, rows_send) = rest[:n], rest[n:]
    me = lax.axis_index("mp")
    first = me == 0
    gain, bias = prm[GAIN : GAIN + 1], prm[BIAS : BIAS + 1]
    gains, biases = [], []
    for m in range(n):
        at = me * n + m
        rstd = stat[n + m : n + m + 1]
        x = join(first, x_own[at], x_recv[at], 1).astype(F32)
        unit = (x - stat[m : m + 1]) * rstd
        u = unit * gain + bias
        sig = sigmoid(u)
        slope = sig * (1.0 + u * (1.0 - sig))
        grad = conv_transposed(win4[m], wfull) * slope
        back, gain_grad, bias_grad = norm_back(grad, unit, gain, rstd)
        gains.append(gain_grad)
        biases.append(bias_grad)
        d_keep, d_send = split(first, back + dmid[m])
        keep[m] = d_keep
        send[m] = d_send.astype(BF16)
        out_pass[m] = out_send[m]
    small = [
        sum(gains), sums2[0:1], sums3[0:1], sum(biases), sums2[1:2], sums3[1:2], sums2[2:3], sums3[2:6],
        jnp.zeros((5, C), F32),
    ]
    rows_keep[...], rows_send[...] = split(first, jnp.concatenate(small, axis=0))


def maps_kernel(after, tw_recv, out_keep, out_recv, grad_keep, grad_recv, out, grad, turn):
    n = out_keep.shape[0]
    me = lax.axis_index("mp")
    for m in range(n):
        out[me * n + m] = out_keep[m]
        out[(1 - me) * n + m] = out_recv[m]
        grad[me * n + m] = grad_keep[m]
        grad[(1 - me) * n + m] = grad_recv[m].astype(F32)
    turn[...] = jnp.zeros_like(turn)


EXTRA, SUMS = 16, 16


def bits_of(count):
    bits = list(range(count.bit_length() - 1))
    cut = len(bits) // 2
    orders = [[(1, 3, 0, 2), (2, 1, 0, 3)], [(0, 2, 1, 3), (2, 0, 3, 1)]]
    if len(bits) != 4:
        orders = [[bits, bits[::-1]], [bits[cut:] + bits[:cut], bits[:cut][::-1] + bits[cut:]]]
    return [[(list(order[:cut]), list(order[cut:])) for order in group] for group in orders]


def digit(bits):
    first = lax.axis_index("mp") == 0
    return (lax.axis_index("dp") >> jnp.where(first, bits[0], bits[1])) & 1


def swap_dp(values, bits):
    pairs = []
    for i in range(lax.axis_size("dp")):
        for core in range(2):
            pairs.append((2 * i + core, 2 * (i ^ (1 << bits[core])) + core))
    return lax.ppermute(values, ("dp", "mp"), pairs)


def swap_mp(values):
    return lax.ppermute(values, "mp", [(0, 1), (1, 0)])


def part(index, rows):
    return pl.ds(pl.multiple_of(index * rows, 16), rows)


def added(a, b):
    return (a.astype(F32) + b.astype(F32)).astype(BF16)


def start_exchange(chain, pairs, time_rows, after):
    rows = chain.rows
    half, extra = rows // 2, EXTRA if time_rows else 0

    def body(*refs):
        refs = list(refs)
        sources = [(refs.pop(0), refs.pop(0)) for _ in pairs]
        outs, values = refs[-3:-1], refs[-1]
        end = 0
        for keep, recv in sources:
            size = keep.shape[0]
            values[end : end + size] = added(keep[...], recv[...])
            end += size
        if end < rows:
            values[end:rows] = jnp.zeros((rows - end, HALF), BF16)
        me = digit(chain.steps[0])
        for index, ref in zip((me, 1 - me), outs):
            ref[0:half] = values[part(index, half)]
            if extra:
                ref[half:] = refs[0][...]

    args = [v for pair in pairs for v in pair] + list(time_rows)
    specs = {len(args) + i: ANYWHERE for i in range(len(after))}
    shape = ((half + extra, HALF), BF16)
    scratch = [pltpu.VMEM((rows, HALF), BF16)]
    chain.own, send = call(body, [shape, shape], *args, *after, scratch=scratch, specs=specs)
    chain.recv = swap_dp(send, chain.steps[0])
    chain.rows = half


class Exchange:
    def __init__(self, order, rows):
        halving, whole = [list(zip(*[core[i] for core in order])) for i in range(2)]
        self.cut, self.whole = len(halving), len(halving) + len(whole)
        self.steps = halving + whole + halving[::-1]
        self.bits = [[core[0] + core[1] for core in order][c] for c in range(2)]
        self.at = 0
        pieces = 1 << self.cut
        self.piece = -(-rows // (16 * pieces)) * 16
        self.rows = self.piece * pieces

    def step(self, after, small=()):
        bits, following = self.steps[self.at : self.at + 2]
        self.at += 1
        head, rest = self.rows, self.own.shape[0] - self.rows
        halve, ends, last = self.at < self.cut, self.at == self.cut, self.at == self.whole
        gather = self.at > self.whole
        with_small = SUMS if small and ends else 0

        def body(own, recv, after_ref, *refs):
            small_refs, outs = refs[: len(small) if ends else 0], refs[len(small) if ends else 0 :]
            me = digit(bits)
            out = outs[0]
            if gather:
                out[part(me, head)] = own[...]
                out[part(1 - me, head)] = recv[...]
                return
            tails = []
            if halve:
                values, send = outs[-1], outs[1]
                values[...] = added(own[0:head], recv[0:head])
                index = digit(following)
                out[0 : head // 2] = values[part(index, head // 2)]
                send[0 : head // 2] = values[part(1 - index, head // 2)]
                tails = [(out, head // 2), (send, head // 2)]
            else:
                out[0:head] = added(own[0:head], recv[0:head])
                if with_small:
                    out[head : head + SUMS] = (small_refs[0][...] + small_refs[1][...]).astype(BF16)
                tails = [(outs[-1], 0 if last else head + with_small)]
            if rest:
                low = me == 0
                mine, theirs = own[head:], recv[head:]
                for ref, at in tails:
                    ref[at : at + rest] = jnp.where(low, mine, theirs)
                    ref[at + rest : at + 2 * rest] = jnp.where(low, theirs, mine)

        def shape(rows):
            return ((rows, HALF), BF16)

        if gather:
            outs, self.rows = [shape(2 * head)], 2 * head
        elif halve:
            outs, self.rows = [shape(head // 2 + 2 * rest)] * 2, head // 2
        else:
            self.rows = head + with_small
            outs = [shape(self.rows), shape(2 * rest)] if last and rest else [shape(self.rows + 2 * rest)]
        args = (self.own, self.recv, after) + (tuple(small) if ends else ())
        scratch = [pltpu.VMEM((head, HALF), BF16)] if halve else []
        results = call(body, outs, *args, scratch=scratch, specs={2: ANYWHERE})
        self.own = results[0]
        if last and rest:
            self.gathered = results[1]
        self.recv = swap_dp(results[1] if halve else self.own, following)


def time_results(n, gathered, other, order, table, tw_own, tw_recv, after):
    steps, width = table.shape
    padded = -(-steps // HALF) * HALF
    blocks = gathered.shape[0] // EXTRA
    maps = 8 * 2 * blocks

    def owner(core, block):
        return sum((block >> i & 1) << bit for i, bit in enumerate(order[core]))

    def body(rows_ref, other_ref, table_ref, tw_own_ref, tw_recv_ref, after_ref, *refs):
        table_grad, tw_grad, time_b, turn, extra, act_high, act_low = refs
        me = lax.axis_index("mp")
        first = me == 0
        for block in range(blocks):
            rows = slice(block * EXTRA, (block + 1) * EXTRA)
            own_at = jnp.where(first, owner(0, block), owner(1, block))
            other_at = jnp.where(first, owner(1, block), owner(0, block))
            extra[2 * own_at + me] = rows_ref[rows].astype(F32)
            extra[2 * other_at + 1 - me] = other_ref[rows].astype(F32)
        lane = lax.broadcasted_iota(jnp.int32, (maps, HALF), 1)
        row = lax.broadcasted_iota(jnp.int32, (maps, HALF), 0) & 7
        held = row < n
        left = jnp.where(held, extra[:, 0:8].reshape(maps, HALF), 0.0)
        right = jnp.where(held, extra[:, 8:16].reshape(maps, HALF), 0.0)
        step_rows = jnp.broadcast_to(extra[:, n : n + 1], (2 * blocks, 8, HALF)).reshape(maps, HALF)
        weight = jnp.where(held & (lane == row), 32.0, jnp.where(held & (lane == row + n), 1.0, 0.0))
        step = jnp.sum(step_rows * weight, axis=1, keepdims=True).astype(jnp.int32)
        mine = jnp.where(first, left, right)
        time_b[...] = col_sum(mine)
        lane = lax.broadcasted_iota(jnp.int32, (maps, padded), 1)
        pick = jnp.where(lane == step, 1.0, 0.0).astype(BF16)
        tw = join(first, tw_own_ref[...], tw_recv_ref[...], 1)
        back = dot_bt(jnp.concatenate([left, right], axis=1).astype(BF16), tw)
        back_high = back.astype(BF16)
        back_low = (back - back_high.astype(F32)).astype(BF16)
        e = table_ref[...]
        sig = sigmoid(e)
        spread = (dot_at(pick, back_high) + dot_at(pick, back_low))[0:steps]
        table_grad[...] = spread * (sig * (1.0 + e * (1.0 - sig)))
        act = e * sig
        high = act.astype(BF16).astype(F32)
        act_high[steps:padded] = jnp.zeros((padded - steps, width), F32)
        act_low[steps:padded] = jnp.zeros((padded - steps, width), F32)
        act_high[0:steps] = high
        act_low[0:steps] = act - high
        by_step = dot_at(mine.astype(BF16), pick)
        step_high = by_step.astype(BF16)
        step_low = (by_step - step_high.astype(F32)).astype(BF16)
        high, low = act_high[...].astype(BF16), act_low[...].astype(BF16)
        tw_grad[...] = (dot(step_high, high) + dot(step_high, low) + dot(step_low, high)).T
        turn[...] = jnp.zeros_like(turn)

    outs = [(table.shape, F32), (tw_own.shape, F32), ((1, HALF), F32), ((8, HALF), F32)]
    scratch = [
        pltpu.VMEM((2 * blocks, EXTRA, HALF), F32),
        pltpu.VMEM((padded, width), F32),
        pltpu.VMEM((padded, width), F32),
    ]
    args = (gathered, other, table, tw_own, tw_recv, after)
    return call(body, outs, *args, scratch=scratch, specs={5: ANYWHERE}, limit=24)


def laid(chain, own, recv, values):
    me, rows = digit(chain.steps[-1]), own.shape[0]
    values[part(me, rows)] = own[...]
    values[part(1 - me, rows)] = recv[...]
    return row_reader(values, chain.piece, values.shape[0] >> chain.cut)


def put_taps(conv2, at, taps, read):
    for i in range(taps):
        for h in range(2):
            conv2[at + i, :, h * HALF : (h + 1) * HALF] = read((2 * i + h) * HALF, HALF)


def early_results(chain, after):
    taps = len(CONV2_TAPS[1])

    def body(after_ref, own, recv, conv1, last, gains, biases, conv_b, qkv_b, out_b, values):
        read = laid(chain, own, recv, values)
        put_taps(last, 0, taps, read)
        conv1[...] = read(taps * C, 9 * C)
        full = values.shape[0] >> chain.cut
        small = None
        for p in range(1 << chain.cut):
            base = p * full + chain.piece
            block = values[base : base + SUMS].astype(F32)
            small = block if small is None else small + block
        gains[...] = small[0:3]
        biases[...] = small[3:6]
        conv_b[...] = small[6:8]
        qkv_b[...] = small[8:10]
        out_b[...] = small[10:11]

    outs = [
        ((9 * C, HALF), F32), ((taps, HALF, C), F32),
        ((3, HALF), F32), ((3, HALF), F32), ((2, HALF), F32), ((2, HALF), F32), ((1, HALF), F32),
    ]
    scratch = [pltpu.VMEM((2 * chain.own.shape[0], HALF), BF16)]
    return call(body, outs, after, chain.own, chain.recv, scratch=scratch)


def late_results(chain, last):
    taps = len(CONV2_TAPS[0])

    def body(last_ref, own, recv, conv2, qkv, out_w, values):
        read = laid(chain, own, recv, values)
        put_taps(conv2, 0, taps, read)
        conv2[taps:9] = last_ref[...]
        at = taps * C
        for j in range(3):
            qkv[j] = read(at + j * C, C)
        for h in range(2):
            out_w[:, h * HALF : (h + 1) * HALF] = read(at + 3 * C + h * HALF, HALF)

    outs = [((9, HALF, C), F32), ((3, C, HALF), F32), ((HALF, C), F32)]
    scratch = [pltpu.VMEM((2 * chain.own.shape[0], HALF), BF16)]
    return call(body, outs, last, chain.own, chain.recv, scratch=scratch)


def row_reader(values, piece, full):
    def read(start, size):
        found = []
        while size:
            at, left = start % piece, piece - start % piece
            now = min(size, left)
            base = start // piece * full + at
            found.append(values[base : base + now].astype(F32))
            start, size = start + now, size - now
        return jnp.concatenate(found, axis=0)

    return read


def on_device(
    maps_in, timesteps, temb_table, norm_gain, norm_bias, conv1_weight, conv_bias, temb_weight,
    temb_bias, conv2_weight, qkv_weight, qkv_bias, out_weight, out_bias, out_grad,
):
    count = lax.axis_size("dp")
    orders = bits_of(count)
    total = maps_in.shape[0]
    n = total // 2
    maps_shape, half_shape = (n, PIX, C), (n, PIX, HALF)
    weight_shape = ((9, C, C), BF16)

    x_recv = swap_mp(maps_in)
    w1_own = conv1_weight.reshape(9, C, HALF)
    w1_recv = swap_mp(w1_own)
    blank = call(blank_kernel, [((4, HALF), F32)], flops=10**11)[0]
    pk_own = jnp.concatenate(
        [norm_gain, norm_bias, conv_bias, qkv_bias, out_bias[None], temb_bias[None], blank]
    )
    pk_own, step_row = call(
        time_kernel, [((PACK + total, HALF), F32), ((8, HALF), F32)],
        timesteps, pk_own, temb_table, temb_weight, w1_own,
        specs={0: SCALAR},
    )
    pk_recv = swap_mp(pk_own)
    tw_recv = swap_mp(temb_weight)
    w2_own = conv2_weight.reshape(9, HALF, C)
    w2_recv = swap_mp(w2_own)
    qw_own = jnp.transpose(qkv_weight, (1, 0, 2))
    qw_recv = swap_mp(qw_own)
    ow_recv = swap_mp(out_weight)
    g_recv = swap_mp(out_grad)

    hid, act1_t, act2_t, stat0, stat1, prm, w1_full, *win2 = call(
        first_kernel,
        [
            (maps_shape, F32), ((C, n * PIX), BF16), ((C, n * PIX), BF16),
            ((2 * n, C), F32), ((2 * n, C), F32), ((PACK, C), F32), weight_shape,
        ] + [WIN] * n,
        maps_in, x_recv, w1_own, w1_recv, pk_own, pk_recv,
        scratch=[pltpu.VMEM(*WIN)] * n + [pltpu.VMEM(w1_own.shape, BF16), pltpu.SemaphoreType.DMA],
        specs={3: ANYWHERE},
        flops=10**11,
    )
    tile_f32, tile_low = pltpu.VMEM((PIX, C), F32), pltpu.VMEM((PIX, C), BF16)
    three_low = pltpu.VMEM((3, PIX, C), BF16)
    out_keep, out_send, dmid, wg_keep, wg_send, sums3, w2_full, *win3 = call(
        middle_kernel,
        [
            (half_shape, BF16), (half_shape, BF16), (maps_shape, F32),
            ((4 * C, HALF), BF16), ((4 * C, HALF), BF16), ((8, C), F32), weight_shape,
        ] + [WIN] * n,
        maps_in, x_recv, w2_own, w2_recv, prm, out_grad, g_recv, qw_own, qw_recv, out_weight, ow_recv, *win2,
        scratch=[pltpu.VMEM((3, C, C), BF16), tile_low]
        + [tile_f32] * (3 * n) + [tile_low] * n + [three_low] * n + [tile_low] * (3 * n) + [three_low] * n,
    )
    def swapped(keep, send):
        return keep, swap_mp(send)

    shape = ((len(CONV2_TAPS[0]) * C + wg_keep.shape[0], HALF), BF16)
    late_pair = swapped(*call(conv2_grad_kernel, [shape, shape], act2_t, wg_keep, wg_send, *win3))
    sums2, time_rows, *win4 = call(
        hidden_back_kernel,
        [((8, C), F32), ((EXTRA, HALF), BF16)] + [WIN] * n,
        step_row, late_pair[0], hid, stat1, w2_full, prm, *win3,
        specs={1: ANYWHERE},
    )

    early, late = chains = [
        Exchange(order, rows) for order, rows in zip(orders, (11 * C, late_pair[0].shape[0]))
    ]

    shape = ((11 * C, HALF), BF16)
    half = (late.rows // 2, HALF)
    keep, send, late.own, late_send = call(
        functools.partial(last_grad_kernel, late.steps[0]), [shape, shape, (half, BF16), (half, BF16)],
        act2_t, act1_t, *late_pair, *win3, *win4,
        scratch=[pltpu.VMEM((late.rows, HALF), BF16)],
    )
    early_pair = swapped(keep, send)
    late.recv = swap_dp(late_send, late.steps[0])
    late.rows //= 2
    start_exchange(early, (early_pair,), (time_rows,), (late.own,))
    mg_keep, mg_send, out_send, rows_keep, rows_send = call(
        input_back_kernel,
        [(half_shape, F32), (half_shape, BF16), (half_shape, BF16), ((SUMS, HALF), F32), ((SUMS, HALF), F32)],
        early.own, maps_in, x_recv, stat0, w1_full, prm, dmid, sums2, sums3, out_send, *win4,
        specs={0: ANYWHERE},
        flops=10**10,
    )
    rows_recv = swap_mp(rows_send)
    mg_recv, out_recv = swap_mp(mg_send), swap_mp(out_send)
    turn = rows_keep
    for i in range(len(early.steps) - 1):
        early.step(turn, (rows_keep, rows_recv))
        late.step(early.own)
        if i == 0:
            maps_out, maps_grad, turn = call(
                maps_kernel, [(maps_in.shape, BF16), (maps_in.shape, F32), ((8, HALF), F32)],
                late.own, tw_recv, out_keep, out_recv, mg_keep, mg_recv,
                specs={0: ANYWHERE, 1: ANYWHERE},
            )
        if i == early.whole - 1:
            table_grad, tw_grad, time_b, turn = time_results(
                n, early.gathered, swap_mp(early.gathered), early.bits, temb_table, temb_weight, tw_recv, late.own,
            )
    conv1, last_taps, gains, biases, conv_b, qkv_b, out_b = early_results(early, turn)
    conv2, qkv, out_w = late_results(late, last_taps)
    return (
        maps_out, maps_grad, table_grad, gains, biases, conv1.reshape(3, 3, C, HALF), conv_b, tw_grad,
        time_b.reshape(HALF), conv2.reshape(3, 3, HALF, C), jnp.transpose(qkv, (1, 0, 2)), qkv_b, out_w,
        out_b.reshape(HALF),
    )


def solution(mesh):
    args = (
        P("dp", None, "mp"), P("dp"), P(), P(None, "mp"), P(None, "mp"), P(None, None, None, "mp"),
        P(None, "mp"), P(None, "mp"), P("mp"), P(None, None, "mp", None), P(None, None, "mp"),
        P(None, "mp"), P("mp", None), P("mp"), P("dp", None, "mp"),
    )
    outs = (
        P("dp", None, "mp"), P("dp", None, "mp"), P(), P(None, "mp"), P(None, "mp"),
        P(None, None, None, "mp"), P(None, "mp"), P(None, "mp"), P("mp"), P(None, None, "mp", None),
        P(None, None, "mp"), P(None, "mp"), P("mp", None), P("mp"),
    )
    return jax.shard_map(on_device, mesh=mesh, in_specs=args, out_specs=outs, check_vma=False)
```
